128 devices in a mesh: role: 4 (over z_hi, core), shard: 32 (over y, x, z_lo).
Axes of the slice: x: 4, y: 4, z: 4 (z_hi: 2, z_lo: 2; z = z_hi * 2 + z_lo), core: 2. Of those that a mesh axis runs over, the one named last changes fastest.
Arguments:
- action_ids: int32 [128, 8], P(('role', 'shard')), may hold values from 0 to 255
- traj_lengths: int32 [128], P(('role', 'shard')), may hold values from 1 to 8
- action_table: bfloat16 [256, 4096], P(None, 'shard'), may hold values from -6 to 6
- prefix_keys: bfloat16 [128, 128, 2048], P(('role', 'shard')), may hold values from -6 to 6
- prefix_values: bfloat16 [128, 128, 2048], P(('role', 'shard')), may hold values from -6 to 6
- qkv_weight: bfloat16 [4096, 6144], P('shard'), may hold values from -0.09375 to 0.09375
- out_weight: bfloat16 [2048, 4096], P(None, 'shard'), may hold values from -0.125 to 0.125
- first_qkv: float32 [4096, 6144], P('shard', 'role'), may hold values from -6 to 6
- second_qkv: float32 [4096, 6144], P('shard', 'role'), may hold values from 1 to 100
- first_out: float32 [2048, 4096], P('role', 'shard'), may hold values from -6 to 6
- second_out: float32 [2048, 4096], P('role', 'shard'), may hold values from 1 to 100
- out_cotangent: bfloat16 [1024, 4096], P('role', 'shard'), may hold values from -6 to 6
Outputs:
- decoded: bfloat16 [1024, 4096], P('role', 'shard')
- new_qkv: bfloat16 [4096, 6144], P('shard')
- new_out: bfloat16 [2048, 4096], P(None, 'shard')
- moment_qkv: float32 [4096, 6144], P('shard', 'role')
- square_qkv: float32 [4096, 6144], P('shard', 'role')
- moment_out: float32 [2048, 4096], P('role', 'shard')
- square_out: float32 [2048, 4096], P('role', 'shard')
The draws below stay inside these ranges and needn't reach their ends.
All inputs are finite; a program needn't handle non-finite values.
Results may differ from the reference program's by a relative error of at most 0.0071.
Values may be sent and summed in bfloat16 or wider, within the bound.
A program may use at most 64 MiB of HBM per device.

```python
import math
import jax
import jax.numpy as jnp
from jax import lax

D = 4096
HD = 128
BINS = 256
PREFIX = 128
TRAJ = 8
HW = 2048
EPIS = 128
ROWS = 1024
N_ROLE = 4


def plant(array, own_key, least, largest):
    dims = array.shape
    place = [jax.random.randint(jax.random.fold_in(own_key, axis), (), 0, dims[axis]) for axis in range(len(dims))]
    array = array.at[tuple(place)].set(least)
    longest = dims.index(max(dims))
    place[longest] = (place[longest] + 1) % dims[longest]
    return array.at[tuple(place)].set(largest)


def shard_levels(key, extent, split, smallest, high):
    def one(dim, parts):
        steps = jax.random.uniform(jax.random.fold_in(jax.random.fold_in(key, 6), dim), (parts,), jnp.float32, smallest / len(split), high / len(split))
        return jnp.repeat(jnp.exp(steps), extent[dim] // parts).reshape((-1,) + (1,) * (len(extent) - dim - 1))

    gain = one(*split[0])
    for cut in split[1:]:
        gain = gain * one(*cut)
    return gain


def normal_values(rng, extent, width, most, pieces=(), kind=jnp.bfloat16):
    entries = width * jax.random.normal(rng, extent, jnp.float32)
    if pieces:
        entries = entries * shard_levels(rng, extent, pieces, -0.22, 0.18)
    return jnp.clip(entries, -most, most).astype(kind)


def setup_inputs(seed: int = 0) -> dict:
    splits = jax.random.split(jax.random.key(seed), 13)
    return {
        "action_ids": plant(jax.random.randint(splits[0], (EPIS, TRAJ), 0, BINS), jax.random.fold_in(splits[0], 1), 0, BINS - 1).astype(jnp.int32),
        "traj_lengths": plant(jax.random.randint(splits[1], (EPIS,), 1, TRAJ + 1), jax.random.fold_in(splits[1], 1), 1, TRAJ).astype(jnp.int32),
        "action_table": normal_values(splits[2], (BINS, D), 1.0, 6.0, ((1, 32),)),
        "prefix_keys": normal_values(splits[3], (EPIS, PREFIX, HW), 1.0, 6.0, ((0, 128),)),
        "prefix_values": normal_values(splits[4], (EPIS, PREFIX, HW), 1.0, 6.0, ((0, 128),)),
        "qkv_weight": normal_values(splits[5], (D, 3 * HW), D ** -0.5, 0.09375, ((0, 32),)),
        "out_weight": normal_values(splits[6], (HW, D), HW ** -0.5, 0.125, ((1, 32),)),
        "first_qkv": normal_values(splits[7], (D, 3 * HW), 1.0, 6.0, ((0, 32), (1, 4)), jnp.float32),
        "second_qkv": jnp.clip(jnp.exp(math.log(100.0) - 4.6051702 * jax.random.uniform(splits[8], (D, 3 * HW), jnp.float32) ** shard_levels(splits[8], (D, 3 * HW), ((0, 32), (1, 4)), -0.2, 0.2)), 1.0, 100.0),
        "first_out": normal_values(splits[9], (HW, D), 1.0, 6.0, ((0, 4), (1, 32)), jnp.float32),
        "second_out": jnp.clip(jnp.exp(math.log(100.0) - 4.6051702 * jax.random.uniform(splits[10], (HW, D), jnp.float32) ** shard_levels(splits[10], (HW, D), ((0, 4), (1, 32)), -0.2, 0.2)), 1.0, 100.0),
        "out_cotangent": normal_values(splits[11], (ROWS, D), 1.0, 6.0, ((0, 4), (1, 32))),
    }


learn_rate = 0.001
first_decay = 0.9
second_decay = 0.95
adam_eps = 1e-08
weight_decay = 0.1
first_fix = 1.0 - 0.9 ** 10
second_fix = 1.0 - 0.95 ** 10

def unpack(qkv_rows, keys_pre, vals_pre):
    span_width = keys_pre.shape[-1]
    head_count = span_width // HD
    positions = qkv_rows.shape[0]
    total_keys = keys_pre.shape[0] + positions
    queries = qkv_rows[:, :span_width].astype(jnp.float32).reshape(positions, head_count, HD)
    all_keys = jnp.concatenate([keys_pre, qkv_rows[:, span_width:2 * span_width]], 0).astype(jnp.float32).reshape(total_keys, head_count, HD)
    all_values = jnp.concatenate([vals_pre, qkv_rows[:, 2 * span_width:]], 0).astype(jnp.float32).reshape(total_keys, head_count, HD)
    return (queries, all_keys, all_values)

def attend(qkv_rows, keys_pre, vals_pre, length):
    queries, all_keys, all_values = unpack(qkv_rows, keys_pre, vals_pre)
    prefix_len = keys_pre.shape[0]
    positions = qkv_rows.shape[0]
    attn_scale = HD ** (-0.5)
    scores = jnp.einsum('thd,lhd->htl', queries, all_keys) * attn_scale
    position = jnp.arange(positions, dtype=jnp.int32)[:, None]
    offset = jnp.arange(prefix_len + positions, dtype=jnp.int32)[None, :] - prefix_len
    allowed = (offset < 0) | (offset <= position) & (offset < length)
    scores = jnp.where(allowed[None], scores, -1e+30)
    weights = jax.nn.softmax(scores, axis=-1)
    rounded = lax.optimization_barrier(weights.astype(jnp.bfloat16))
    head_mix = jnp.einsum('htl,lhd->thd', rounded.astype(jnp.float32), all_values)
    return (head_mix.reshape(positions, -1).astype(jnp.bfloat16), weights, rounded)

def attend_back(qkv_rows, keys_pre, vals_pre, weights, rounded, upstream):
    queries, all_keys, all_values = unpack(qkv_rows, keys_pre, vals_pre)
    prefix_len = keys_pre.shape[0]
    positions = qkv_rows.shape[0]
    attn_scale = HD ** (-0.5)
    grads_head = upstream.astype(jnp.float32).reshape(positions, -1, HD)
    grad_weights = jnp.einsum('thd,lhd->htl', grads_head, all_values)
    grad_scores = weights * (grad_weights - lax.optimization_barrier(jnp.sum(weights * grad_weights, axis=-1, keepdims=True))) * attn_scale
    grad_rounded = lax.optimization_barrier(grad_scores.astype(jnp.bfloat16)).astype(jnp.float32)
    grad_query = jnp.einsum('htl,lhd->thd', grad_rounded, all_keys).reshape(positions, -1)
    grad_key = jnp.einsum('htl,thd->lhd', grad_rounded[:, :, prefix_len:], queries).reshape(positions, -1)
    grad_value = jnp.einsum('htl,thd->lhd', rounded.astype(jnp.float32)[:, :, prefix_len:], grads_head).reshape(positions, -1)
    return jnp.concatenate([grad_query, grad_key, grad_value], 1).astype(jnp.bfloat16)

def adamw(params, gradient, first_moment, second_moment):
    moment_one = first_decay * first_moment + (1.0 - first_decay) * gradient
    moment_two = second_decay * second_moment + (1.0 - second_decay) * gradient * gradient
    stepped = moment_one / first_fix / (jnp.sqrt(moment_two / second_fix) + adam_eps)
    wide_params = params.astype(jnp.float32)
    updated = wide_params - learn_rate * (stepped + weight_decay * wide_params)
    return (updated, moment_one, moment_two)

def reference(action_ids, traj_lengths, action_table, prefix_keys, prefix_values, qkv_weight, out_weight, first_qkv, second_qkv, first_out, second_out, out_cotangent):
    episodes = action_ids.shape[0]
    horizon = action_ids.shape[1]
    contract_rows = (((0,), (0,)), ((), ()))
    onehot = (action_ids.reshape(-1)[:, None] == jnp.arange(BINS, dtype=jnp.int32)[None, :]).astype(jnp.bfloat16)
    inputs = jnp.dot(onehot, action_table, preferred_element_type=jnp.float32).astype(jnp.bfloat16)
    projected = jnp.dot(inputs, qkv_weight, preferred_element_type=jnp.float32).astype(jnp.bfloat16).reshape(episodes, horizon, -1)
    head_mix, weights, rounded = jax.vmap(attend)(projected, prefix_keys, prefix_values, traj_lengths)
    head_rows = head_mix.reshape(episodes * horizon, -1)
    decoded = jnp.dot(head_rows, out_weight, preferred_element_type=jnp.float32).astype(jnp.bfloat16)
    first_ep = (N_ROLE - 1) * episodes // N_ROLE
    first_row = first_ep * horizon
    valid = (jnp.arange(horizon, dtype=jnp.int32)[None, :] < traj_lengths[:, None]).reshape(-1)
    masked = jnp.where(valid[:, None], out_cotangent, jnp.zeros_like(out_cotangent))[first_row:]
    grad_out = lax.dot_general(head_rows[first_row:], masked, contract_rows, preferred_element_type=jnp.float32)
    grad_heads = lax.dot_general(masked, out_weight, (((1,), (1,)), ((), ())), preferred_element_type=jnp.float32).astype(jnp.bfloat16)
    grad_heads = grad_heads.reshape(episodes - first_ep, horizon, -1)
    grad_proj = jax.vmap(attend_back)(projected[first_ep:], prefix_keys[first_ep:], prefix_values[first_ep:], weights[first_ep:], rounded[first_ep:], grad_heads)
    grad_proj = grad_proj.reshape((episodes - first_ep) * horizon, -1)
    grad_qkv = lax.dot_general(inputs[first_row:], grad_proj, contract_rows, preferred_element_type=jnp.float32)
    new_qkv, moment_qkv, square_qkv = adamw(qkv_weight, grad_qkv, first_qkv, second_qkv)
    new_out, moment_out, square_out = adamw(out_weight, grad_out, first_out, second_out)
    return (decoded, new_qkv.astype(jnp.bfloat16), new_out.astype(jnp.bfloat16), moment_qkv, square_qkv, moment_out, square_out)
```

```python
import jax
import jax.numpy as jnp
from jax import lax
from jax.experimental import pallas as pl
from jax.experimental.pallas import tpu as pltpu
from jax.sharding import PartitionSpec as P

HD = 128
MESH = pl.DeviceIdType.MESH
F32 = jnp.float32
BF16 = jnp.bfloat16
LEARNER = 3

learn_rate = 0.001
first_decay = 0.9
second_decay = 0.95
adam_eps = 1e-08
weight_decay = 0.1
first_fix = 1.0 - 0.9**10
second_fix = 1.0 - 0.95**10
scale = HD ** (-0.5)

N_CHUNK = 4
CHUNK = 1536 // N_CHUNK


def adamw(params, gradient, first_moment, second_moment):
    moment_one = first_decay * first_moment + (1.0 - first_decay) * gradient
    moment_two = second_decay * second_moment + (1.0 - second_decay) * gradient * gradient
    stepped = moment_one / first_fix / (jnp.sqrt(moment_two / second_fix) + adam_eps)
    wide_params = params.astype(F32)
    updated = wide_params - learn_rate * (stepped + weight_decay * wide_params)
    return (updated, moment_one, moment_two)


def settle(ref, sem):
    pltpu.make_async_copy(ref, ref, sem).wait()


def nt(a, b):
    return lax.dot_general(a, b, (((1,), (1,)), ((), ())), preferred_element_type=F32)


def tn(a, b):
    return lax.dot_general(a, b, (((0,), (0,)), ((), ())), preferred_element_type=F32)


def nn(a, b):
    return jnp.dot(a, b, preferred_element_type=F32)


def kernel(
    ids_ref, len_ref, table_hbm, keys_hbm, vals_hbm, wqkv_hbm, wout_hbm,
    m_q_hbm, v_q_hbm, m_o_hbm, v_o_hbm, cot_hbm,
    dec_out, nq_out, no_out, mq_out, sq_out, mo_out, so_out,
    table, keys, vals, wq, wout, m_q, v_q, m_o, v_o, cot,
    tsend, trecv, gsend, grecv, idx4, idsend, idrecv, selsend, selrecv,
    xsend, xrecv, hrs, hrrecv, rsend, rmsg, agrecv, nq, no, dec,
    loc, out_sem, id_s, id_r, idg_s, idg_r, ts_s, ts_r, gs_s, gs_r,
    cot_s, cot_r, sel_s, sel_r, x_s, x_r, rel_s, rel_r, ag_s, ag_r, hr_s, hr_r,
    e_s, e_r,
):
    role = lax.axis_index("role")
    shard = lax.axis_index("shard")
    y, x, zl = shard // 8, (shard // 2) % 4, shard % 2
    z_hi, core = role // 2, role % 2
    sibling = z_hi * 2 + (1 - core)
    across = (1 - z_hi) * 2 + core

    def peer(k):
        py, px, pz = (y + k // 8) % 4, (x + (k // 2) % 4) % 4, (zl + k % 2) % 2
        spot = (px + py) % 4
        return py * 8 + px * 2 + pz, spot < 3, py * 6 + spot * 2 + pz

    my_spot = (x + y) % 4
    holder = my_spot < 3
    my_unit = jnp.where(holder, y * 6 + my_spot * 2 + zl, 0)

    def put(src, dst, send, recv, to_role, to_shard):
        pltpu.make_async_remote_copy(
            src_ref=src, dst_ref=dst, send_sem=send, recv_sem=recv,
            device_id=(to_role, to_shard), device_id_type=MESH,
        ).start()

    def each_peer(body):
        def step(k, carry):
            body(k, *peer(k))
            return carry
        lax.fori_loop(1, 32, step, 0)

    barrier = pltpu.get_barrier_semaphore()
    each_peer(lambda k, p, h, u: pl.semaphore_signal(
        barrier, inc=1, device_id=(role, p), device_id_type=MESH))
    for q in range(1, 4):
        pl.semaphore_signal(
            barrier, inc=1, device_id=((role + q) % 4, shard), device_id_type=MESH)

    col0 = pl.multiple_of(role * 1536, 128)
    row0 = pl.multiple_of(role * 512, 128)
    fetches = [
        pltpu.make_async_copy(a, b, loc.at[i])
        for i, (a, b) in enumerate((
            (table_hbm, table),
            (wqkv_hbm.at[:, pl.ds(col0, 1536)], wq),
            (wout_hbm, wout),
            (cot_hbm, cot),
            (keys_hbm.at[0], keys),
            (vals_hbm.at[0], vals),
            (m_q_hbm, m_q),
            (v_q_hbm, v_q),
            (m_o_hbm, m_o),
            (v_o_hbm, v_o),
        ))
    ]
    for i, f in enumerate(fetches):
        if i != 3:
            f.start()

    @pl.when(role == LEARNER)
    def _():
        fetches[3].start()

    row8 = lax.broadcasted_iota(jnp.int32, (8, 128), 0)
    lane8 = lax.broadcasted_iota(jnp.int32, (8, 128), 1)
    ids = jnp.zeros((8, 128), jnp.int32)
    for i in range(8):
        ids = jnp.where(row8 == i, ids_ref[0, i], ids)
    ids = ids.astype(F32)
    length = len_ref[0]
    live8 = row8 < length
    idx4[role] = ids

    fetches[0].wait()
    fetches[1].wait()
    for c in range(12):
        part = nn(table[...], wq[:, c * 128:(c + 1) * 128]).astype(BF16)
        tsend[2 * c] = part[0:128]
        tsend[2 * c + 1] = part[128:256]

    pl.semaphore_wait(barrier, 34)

    for q in range(1, 4):
        put(idx4.at[role], idx4.at[role], id_s.at[q - 1], id_r.at[q - 1], (role + q) % 4, shard)

    def send_part(k, p, h, u):
        @pl.when(h)
        def _():
            put(tsend.at[u], trecv.at[k - 1], ts_s, ts_r, role, p)
    each_peer(send_part)

    for q in range(1, 4):
        settle(idx4.at[0], id_r.at[q - 1])
    all_ids = jnp.concatenate([idx4[q] for q in range(4)], axis=0).astype(BF16)
    idsend[...] = all_ids
    idrecv[shard] = all_ids

    def send_ids(k, p, h, u):
        @pl.when(h)
        def _():
            put(idsend, idrecv.at[shard], idg_s, idg_r, role, p)
    each_peer(send_ids)

    fetches[2].wait()

    @pl.when(role == LEARNER)
    def _():
        fetches[3].wait()
        for q in range(3):
            put(cot_hbm, cot, cot_s.at[q], cot_r, q, shard)
        for i in range(8):
            upper = nt(cot[...], wout[i * 128:(i + 1) * 128, :]).reshape(32, 8, 128)
            lower = nt(cot[...], wout[1024 + i * 128:1024 + (i + 1) * 128, :]).reshape(32, 8, 128)
            gsend[:, :, i * 128:(i + 1) * 128] = jnp.concatenate([upper, lower], axis=1).astype(BF16)

        def send_grad(k, p, h, u):
            put(gsend.at[p], grecv.at[k - 1], gs_s, gs_r, role, p)
        each_peer(send_grad)

    @pl.when(holder)
    def _():
        settle(trecv, ts_r)

        def add(k, total):
            return total + trecv[k].astype(F32)
        total = lax.fori_loop(0, 31, add, tsend[my_unit].astype(F32))
        whole = total.astype(BF16)
        settle(idrecv.at[0:31], idg_r)
        lane = lax.broadcasted_iota(jnp.int32, (1024, 128), 1) + 128 * (my_unit % 2)
        chosen = jnp.where(
            idrecv[...].reshape(1024, 128).astype(F32) == lane.astype(F32), 1.0, 0.0).astype(BF16)
        selsend[...] = nn(chosen, whole).astype(BF16).reshape(32, 32, 128)

        def send_rows(k, p, h, u):
            put(selsend.at[p], selrecv.at[my_unit], sel_s, sel_r, role, p)
        each_peer(send_rows)
        selrecv[my_unit] = selsend[shard]
        settle(selrecv.at[0:23], sel_r)

    @pl.when(jnp.logical_not(holder))
    def _():
        settle(selrecv, sel_r)

    blocks = [selrecv[2 * c].astype(F32) + selrecv[2 * c + 1].astype(F32) for c in range(12)]
    for q in range(4):
        for i in range(6):
            pair = jnp.concatenate(
                [blocks[i][8 * q:8 * q + 8], blocks[6 + i][8 * q:8 * q + 8]], axis=0)
            xsend[q, :, i * 128:(i + 1) * 128] = pair.astype(BF16)
    for q in range(1, 4):
        to = (role + q) % 4
        put(xsend.at[to], xrecv.at[role], x_s.at[q - 1], x_r.at[q - 1], to, shard)
    xrecv[role] = xsend[role]
    fetches[4].wait()
    fetches[5].wait()
    for q in range(1, 4):
        settle(xrecv.at[0], x_r.at[q - 1])

    pieces = [xrecv[q].astype(F32) for q in range(4)]

    def tile(c):
        block, i = divmod(c, 12)
        return pieces[block][8 * (i // 6):8 * (i // 6) + 8, (i % 6) * 128:(i % 6 + 1) * 128]

    def stack(tiles):
        return jnp.concatenate(tiles, axis=0)

    q_tiles = [tile(h) for h in range(16)]
    q_all = stack(q_tiles).astype(BF16)
    k_new = stack([tile(16 + h) for h in range(16)]).astype(BF16)
    v_new = stack([tile(32 + h) for h in range(16)]).astype(BF16)

    def head(ref, h):
        return ref[:, h * 128:(h + 1) * 128]

    s1 = stack([nt(q_tiles[h].astype(BF16), head(keys, h)) for h in range(16)]) * scale
    s2 = nt(q_all, k_new) * scale
    ri = lax.broadcasted_iota(jnp.int32, (128, 128), 0)
    ci = lax.broadcasted_iota(jnp.int32, (128, 128), 1)
    allowed = (ri // 8 == ci // 8) & (ci % 8 <= ri % 8) & (ci % 8 < length)
    s2 = jnp.where(allowed, s2, -1e30)
    top = jnp.maximum(jnp.max(s1, axis=1, keepdims=True), jnp.max(s2, axis=1, keepdims=True))
    e1, e2 = jnp.exp(s1 - top), jnp.exp(s2 - top)
    den = jnp.sum(e1, axis=1, keepdims=True) + jnp.sum(e2, axis=1, keepdims=True)
    w1, w2 = e1 / den, e2 / den
    r2 = w2.astype(BF16)
    o2 = nn(r2, v_new)
    out_tiles = [
        nn(w1[8 * h:8 * h + 8].astype(BF16), head(vals, h)) + o2[8 * h:8 * h + 8]
        for h in range(16)
    ]
    for i in range(8):
        hrs[:, i * 128:(i + 1) * 128] = stack([out_tiles[i], out_tiles[8 + i]]).astype(BF16)

    @pl.when(role == LEARNER)
    def _():
        settle(grecv, gs_r)
        live16 = jnp.concatenate([live8, live8], axis=0)
        g_pieces = []
        for i in range(8):
            cols = slice(i * 128, (i + 1) * 128)

            def add(k, total):
                return total + grecv[k, :, cols].astype(F32)
            total = lax.fori_loop(0, 31, add, gsend[shard, :, cols].astype(F32), unroll=True)
            g_pieces.append(jnp.where(live16, total, 0.0))
        g_tiles = [g_pieces[h % 8][8 * (h // 8):8 * (h // 8) + 8] for h in range(16)]
        g_all = stack(g_tiles).astype(BF16)
        gw1 = stack([nt(g_tiles[h].astype(BF16), head(vals, h)) for h in range(16)])
        gw2 = nt(g_all, v_new)
        dots = jnp.sum(w1 * gw1, axis=1, keepdims=True) + jnp.sum(w2 * gw2, axis=1, keepdims=True)
        gs1 = w1 * (gw1 - dots) * scale
        gs2 = (w2 * (gw2 - dots) * scale).astype(BF16)
        gq2 = nn(gs2, k_new)
        gk = tn(gs2, q_all)
        gv = tn(r2, g_all)
        gp = [
            nn(gs1[8 * h:8 * h + 8].astype(BF16), head(keys, h)) + gq2[8 * h:8 * h + 8]
            for h in range(16)
        ]
        gp += [gk[8 * h:8 * h + 8] for h in range(16)]
        gp += [gv[8 * h:8 * h + 8] for h in range(16)]
        live_out = [jnp.where(live8, t, 0.0) for t in out_tiles]
        for q in range(4):
            tiles = [(gp[12 * q + i], gp[12 * q + 6 + i]) for i in range(6)]
            tiles += [(live_out[4 * q + i], live_out[4 * q + 2 + i]) for i in range(2)]
            tiles += [(ids, ids)]
            for i, pair in enumerate(tiles):
                rsend[q, :, i * 128:(i + 1) * 128] = stack(pair).astype(BF16)
        for q in range(3):
            put(rsend.at[q], rmsg, rel_s.at[q], rel_r, q, shard)
        rmsg[...] = rsend[3]

    @pl.when(role != LEARNER)
    def _():
        settle(rmsg, rel_r)
        settle(cot, cot_r)

    agrecv[shard] = rmsg[...]
    hrrecv[shard] = hrs[...]
    each_peer(lambda k, p, h, u: put(rmsg, agrecv.at[shard], ag_s, ag_r, role, p))
    each_peer(lambda k, p, h, u: put(hrs, hrrecv.at[shard], hr_s, hr_r, role, p))

    settle(agrecv.at[0:31], ag_r)
    got_ids = agrecv[:, :, 1024:1152].reshape(512, 128).astype(F32)
    lane = lax.broadcasted_iota(jnp.int32, (512, 128), 1).astype(F32)
    half = (lax.broadcasted_iota(jnp.int32, (512, 128), 0) // 8) % 2
    low = jnp.where(got_ids == lane, 1.0, 0.0).astype(BF16)
    high = jnp.where(got_ids == lane + 128.0, 1.0, 0.0).astype(BF16)
    rows = nn(low, table[0:128, :]) + nn(high, table[128:256, :])
    halves = [jnp.where(half == j, rows, 0.0).astype(BF16) for j in range(2)]
    for f in fetches[6:]:
        f.wait()

    copies = []

    def copy_out(a, b):
        c = pltpu.make_async_copy(a, b, out_sem.at[len(copies)])
        c.start()
        copies.append(c)

    def spread(src, dst, n):
        put(src, dst, e_s.at[0, n], e_r.at[0, n], sibling, shard)
        put(src, dst, e_s.at[1, n], e_r.at[1, n], across, shard)
        copy_out(src, dst)

    def q_cols(of, c):
        return nq_out.at[:, pl.ds(pl.multiple_of(of * 1536 + c * CHUNK, 128), CHUNK)]

    def o_rows(of):
        return no_out.at[pl.ds(pl.multiple_of(of * 512, 128), 512), :]

    for c in range(N_CHUNK):
        j, at = divmod(c * CHUNK, 768)
        cols = slice(c * CHUNK, (c + 1) * CHUNK)
        grad = tn(halves[j], agrecv[:, :, at:at + CHUNK].reshape(512, CHUNK))
        new, one, two = adamw(wq[:, cols], grad, m_q[:, cols], v_q[:, cols])
        nq[:, cols] = new.astype(BF16)
        m_q[:, cols] = one
        v_q[:, cols] = two
        spread(nq.at[:, cols], q_cols(role, c), c)

    cot_wide = jnp.broadcast_to(
        cot[...].astype(F32).reshape(32, 1, 8, 128), (32, 2, 8, 128)).reshape(512, 128)
    cot_both = jnp.concatenate(
        [jnp.where(half == j, cot_wide, 0.0).astype(BF16) for j in range(2)], axis=1)
    grad_out = tn(agrecv[:, :, 768:1024].reshape(512, 256), cot_both)
    for j in range(2):
        here = slice(j * 256, (j + 1) * 256)
        params = wout[pl.ds(pl.multiple_of(row0 + j * 256, 128), 256), :]
        new, one, two = adamw(
            params, grad_out[:, j * 128:(j + 1) * 128], m_o[here, :], v_o[here, :])
        no[here, :] = new.astype(BF16)
        m_o[here, :] = one
        v_o[here, :] = two
    spread(no, o_rows(role), N_CHUNK)
    copy_out(m_q, mq_out)
    copy_out(v_q, sq_out)
    copy_out(m_o, mo_out)
    copy_out(v_o, so_out)

    def part(of, n):
        return q_cols(of, n) if n < N_CHUNK else o_rows(of)

    for n in range(N_CHUNK + 1):
        settle(part(across, n), e_r.at[1, n])
        put(part(across, n), part(across, n), e_s.at[2, n], e_r.at[2, n], sibling, shard)

    settle(hrrecv.at[0:31], hr_r)
    mix = hrrecv[...].reshape(512, 1024)
    upper = nn(mix, wout[0:1024, :]).reshape(32, 2, 8, 128)
    lower = nn(mix, wout[1024:2048, :]).reshape(32, 2, 8, 128)
    dec[...] = (upper[:, 0] + lower[:, 1]).reshape(256, 128).astype(BF16)
    copy_out(dec, dec_out)

    for n in range(N_CHUNK + 1):
        settle(part(sibling, n), e_r.at[0, n])
        settle(part((1 - z_hi) * 2 + (1 - core), n), e_r.at[2, n])
        for way in range(3):
            settle(part(role, n), e_s.at[way, n])
    for c in copies:
        c.wait()
    for q in range(3):
        settle(idx4.at[0], id_s.at[q])
        settle(xsend.at[0], x_s.at[q])

    @pl.when(holder)
    def _():
        settle(tsend.at[0:23], ts_s)
        settle(idrecv.at[0:23], idg_s)
        settle(selsend.at[0:31], sel_s)

    @pl.when(jnp.logical_not(holder))
    def _():
        settle(tsend, ts_s)
        settle(idrecv.at[0:24], idg_s)

    @pl.when(role == LEARNER)
    def _():
        settle(gsend.at[0:31], gs_s)
        for q in range(3):
            settle(cot, cot_s.at[q])
            settle(rmsg, rel_s.at[q])
    settle(agrecv.at[0:31], ag_s)
    settle(hrrecv.at[0:31], hr_s)


def shards(*args):
    any_ = pl.BlockSpec(memory_space=pl.ANY)
    smem = pl.BlockSpec(memory_space=pltpu.SMEM)
    dma, vm = pltpu.SemaphoreType.DMA, pltpu.VMEM
    return tuple(pl.pallas_call(
        kernel,
        out_shape=(
            jax.ShapeDtypeStruct((256, 128), BF16),
            jax.ShapeDtypeStruct((128, 6144), BF16),
            jax.ShapeDtypeStruct((2048, 128), BF16),
            jax.ShapeDtypeStruct((128, 1536), F32),
            jax.ShapeDtypeStruct((128, 1536), F32),
            jax.ShapeDtypeStruct((512, 128), F32),
            jax.ShapeDtypeStruct((512, 128), F32),
        ),
        in_specs=[smem, smem] + [any_] * 10,
        out_specs=(any_,) * 7,
        scratch_shapes=[
            vm((256, 128), BF16),
            vm((128, 2048), BF16),
            vm((128, 2048), BF16),
            vm((128, 1536), BF16),
            vm((2048, 128), BF16),
            vm((128, 1536), F32),
            vm((128, 1536), F32),
            vm((512, 128), F32),
            vm((512, 128), F32),
            vm((256, 128), BF16),
            vm((24, 128, 128), BF16),
            vm((31, 128, 128), BF16),
            vm((32, 16, 1024), BF16),
            vm((31, 16, 1024), BF16),
            vm((4, 8, 128), F32),
            vm((32, 128), BF16),
            vm((32, 32, 128), BF16),
            vm((32, 32, 128), BF16),
            vm((24, 32, 128), BF16),
            vm((4, 16, 768), BF16),
            vm((4, 16, 768), BF16),
            vm((16, 1024), BF16),
            vm((32, 16, 1024), BF16),
            vm((4, 16, 1152), BF16),
            vm((16, 1152), BF16),
            vm((32, 16, 1152), BF16),
            vm((128, 1536), BF16),
            vm((512, 128), BF16),
            vm((256, 128), BF16),
            dma((10,)),
            dma((N_CHUNK + 6,)),
            dma((3,)), dma((3,)),
            dma, dma,
            dma, dma,
            dma, dma,
            dma((3,)), dma,
            dma, dma,
            dma((3,)), dma((3,)),
            dma((3,)), dma,
            dma, dma,
            dma, dma,
            dma((3, N_CHUNK + 1)), dma((3, N_CHUNK + 1)),
        ],
        compiler_params=pltpu.CompilerParams(
            collective_id=0, has_side_effects=True, vmem_limit_bytes=48 * 1024 * 1024),
        name="policy_update",
    )(*args))


def solution(mesh):
    both = ("role", "shard")
    return jax.shard_map(
        shards,
        mesh=mesh,
        in_specs=(
            P(both, None), P(both), P(None, "shard"), P(both, None, None), P(both, None, None),
            P("shard", None), P(None, "shard"), P("shard", "role"), P("shard", "role"),
            P("role", "shard"), P("role", "shard"), P("role", "shard"),
        ),
        out_specs=(
            P("role", "shard"), P("shard", None), P(None, "shard"), P("shard", "role"),
            P("shard", "role"), P("role", "shard"), P("role", "shard"),
        ),
        check_vma=False,
    )
```

```python
import jax
import jax.numpy as jnp
from jax import lax
from jax.experimental import pallas as pl
from jax.experimental.pallas import tpu as pltpu
from jax.sharding import PartitionSpec as P

HD = 128
MESH = pl.DeviceIdType.MESH
F32 = jnp.float32
BF16 = jnp.bfloat16
LEARNER = 3

learn_rate = 0.001
first_decay = 0.9
second_decay = 0.95
adam_eps = 1e-08
weight_decay = 0.1
first_fix = 1.0 - 0.9**10
second_fix = 1.0 - 0.95**10
scale = HD ** (-0.5)

N_CHUNK = 4
ORDER = 13
CHUNK = 1536 // N_CHUNK


def adamw(params, gradient, first_moment, second_moment):
    moment_one = first_decay * first_moment + (1.0 - first_decay) * gradient
    moment_two = second_decay * second_moment + (1.0 - second_decay) * gradient * gradient
    stepped = moment_one / first_fix / (jnp.sqrt(moment_two / second_fix) + adam_eps)
    wide_params = params.astype(F32)
    updated = wide_params - learn_rate * (stepped + weight_decay * wide_params)
    return (updated, moment_one, moment_two)


def settle(ref, sem):
    pltpu.make_async_copy(ref, ref, sem).wait()


def nt(a, b):
    return lax.dot_general(a, b, (((1,), (1,)), ((), ())), preferred_element_type=F32)


def tn(a, b):
    return lax.dot_general(a, b, (((0,), (0,)), ((), ())), preferred_element_type=F32)


def nn(a, b):
    return jnp.dot(a, b, preferred_element_type=F32)


def kernel(
    ids_ref, len_ref, table_hbm, keys_hbm, vals_hbm, wqkv_hbm, wout_hbm,
    m_q_hbm, v_q_hbm, m_o_hbm, v_o_hbm, cot_hbm,
    dec_out, nq_out, no_out, mq_out, sq_out, mo_out, so_out,
    table, keys, vals, wq, wout, m_q, v_q, m_o, v_o, cot,
    tsend, trecv, gsend, grecv, idx4, idsend, idrecv, selsend, selrecv,
    xsend, xrecv, hrs, hrrecv, rsend, rmsg, agrecv, nq, no, dec,
    loc, out_sem, id_s, id_r, idg_s, idg_r, ts_s, ts_r, gs_s, gs_r,
    cot_s, cot_r, sel_s, sel_r, x_s, x_r, rel_s, rel_r, ag_s, ag_r, hr_s, hr_r,
    e_s, e_r,
):
    role = lax.axis_index("role")
    shard = lax.axis_index("shard")
    y, x, zl = shard // 8, (shard // 2) % 4, shard % 2
    z_hi, core = role // 2, role % 2
    sibling = z_hi * 2 + (1 - core)
    across = (1 - z_hi) * 2 + core

    def peer(k):
        py, px, pz = (y + k // 8) % 4, (x + (k // 2) % 4) % 4, (zl + k % 2) % 2
        spot = (px + py) % 4
        return py * 8 + px * 2 + pz, spot < 3, py * 6 + spot * 2 + pz

    my_spot = (x + y) % 4
    holder = my_spot < 3
    my_unit = jnp.where(holder, y * 6 + my_spot * 2 + zl, 0)

    def put(src, dst, send, recv, to_role, to_shard):
        pltpu.make_async_remote_copy(
            src_ref=src, dst_ref=dst, send_sem=send, recv_sem=recv,
            device_id=(to_role, to_shard), device_id_type=MESH,
        ).start()

    def each_peer(body, first=1, last=32):
        def step(j, carry):
            k = (j * ORDER) % 32
            body(k, *peer(k))
            return carry
        lax.fori_loop(first, last, step, 0)

    barrier = pltpu.get_barrier_semaphore()
    each_peer(lambda k, p, h, u: pl.semaphore_signal(
        barrier, inc=1, device_id=(role, p), device_id_type=MESH))
    for q in range(1, 4):
        pl.semaphore_signal(
            barrier, inc=1, device_id=((role + q) % 4, shard), device_id_type=MESH)

    col0 = pl.multiple_of(role * 1536, 128)
    row0 = pl.multiple_of(role * 512, 128)
    fetches = [
        pltpu.make_async_copy(a, b, loc.at[i])
        for i, (a, b) in enumerate((
            (table_hbm, table),
            (wqkv_hbm.at[:, pl.ds(col0, 1536)], wq),
            (wout_hbm, wout),
            (cot_hbm, cot),
            (keys_hbm.at[0], keys),
            (vals_hbm.at[0], vals),
            (m_q_hbm, m_q),
            (v_q_hbm, v_q),
            (m_o_hbm, m_o),
            (v_o_hbm, v_o),
        ))
    ]
    for i, f in enumerate(fetches):
        if i != 3:
            f.start()

    @pl.when(role == LEARNER)
    def _():
        fetches[3].start()

    row8 = lax.broadcasted_iota(jnp.int32, (8, 128), 0)
    lane8 = lax.broadcasted_iota(jnp.int32, (8, 128), 1)
    ids = jnp.zeros((8, 128), jnp.int32)
    for i in range(8):
        ids = jnp.where(row8 == i, ids_ref[0, i], ids)
    ids = ids.astype(F32)
    length = len_ref[0]
    live8 = row8 < length
    idx4[role] = ids

    fetches[0].wait()
    fetches[1].wait()
    for c in range(12):
        part = nn(table[...], wq[:, c * 128:(c + 1) * 128]).astype(BF16)
        tsend[2 * c] = part[0:128]
        tsend[2 * c + 1] = part[128:256]

    pl.semaphore_wait(barrier, 34)

    for q in range(1, 4):
        put(idx4.at[role], idx4.at[role], id_s.at[q - 1], id_r.at[q - 1], (role + q) % 4, shard)

    def send_part(k, p, h, u):
        @pl.when(h)
        def _():
            put(tsend.at[u], trecv.at[k - 1], ts_s, ts_r, role, p)
    each_peer(send_part, 1, 12)

    for q in range(1, 4):
        settle(idx4.at[0], id_r.at[q - 1])
    lane16 = lax.broadcasted_iota(jnp.int32, (16, 128), 1)
    all_ids = jnp.where(
        lane16 < 64,
        jnp.concatenate([idx4[0], idx4[1]], axis=0),
        jnp.concatenate([idx4[2], idx4[3]], axis=0)).astype(BF16)
    idsend[...] = all_ids
    idrecv[shard] = all_ids

    def send_ids(now):
        def body(k, p, h, u):
            @pl.when(h if now else jnp.logical_not(h))
            def _():
                put(idsend, idrecv.at[shard], idg_s, idg_r, role, p)
        each_peer(body)
    send_ids(True)
    each_peer(send_part, 12, 32)

    @pl.when(role == LEARNER)
    def _():
        fetches[2].wait()
        fetches[3].wait()
        for i in range(8):
            upper, lower = (
                nt(cot[...], wout[j * 1024 + i * 128:j * 1024 + (i + 1) * 128, :])
                .reshape(32, 8, 128)
                for j in range(2)
            )
            gsend[:, :, i * 128:(i + 1) * 128] = jnp.concatenate(
                [upper, lower], axis=1).astype(BF16)

    @pl.when(role != LEARNER)
    def _():
        fetches[2].wait()

    @pl.when(holder)
    def _():
        settle(trecv, ts_r)

        def add(k, total):
            return total + trecv[k].astype(F32)
        total = lax.fori_loop(0, 31, add, tsend[my_unit].astype(F32))
        whole = total.astype(BF16)
        settle(idrecv.at[0:31], idg_r)
        got = idrecv[...].astype(F32)
        got = jnp.concatenate([
            jnp.broadcast_to(got[:, :, 0:1], (32, 16, 128)),
            jnp.broadcast_to(got[:, :, 64:65], (32, 16, 128))], axis=1).reshape(1024, 128)
        lane = lax.broadcasted_iota(jnp.int32, (1024, 128), 1) + 128 * (my_unit % 2)
        chosen = jnp.where(got == lane.astype(F32), 1.0, 0.0).astype(BF16)
        selsend[...] = nn(chosen, whole).astype(BF16).reshape(32, 32, 128)

        def send_rows(k, p, h, u):
            put(selsend.at[p], selrecv.at[my_unit], sel_s, sel_r, role, p)
        each_peer(send_rows)
        selrecv[my_unit] = selsend[shard]

    @pl.when(role == LEARNER)
    def _():
        each_peer(lambda k, p, h, u: put(gsend.at[p], grecv.at[k - 1], gs_s, gs_r, role, p))
    send_ids(False)

    @pl.when(holder)
    def _():
        settle(selrecv.at[0:23], sel_r)

    @pl.when(jnp.logical_not(holder))
    def _():
        settle(idrecv.at[0:31], idg_r)
        settle(selrecv, sel_r)

    blocks = [selrecv[2 * c].astype(F32) + selrecv[2 * c + 1].astype(F32) for c in range(12)]
    for q in range(4):
        for i in range(6):
            pair = jnp.concatenate(
                [blocks[i][8 * q:8 * q + 8], blocks[6 + i][8 * q:8 * q + 8]], axis=0)
            xsend[q, :, i * 128:(i + 1) * 128] = pair.astype(BF16)
    for q in range(1, 4):
        to = (role + q) % 4
        put(xsend.at[to], xrecv.at[role], x_s.at[q - 1], x_r.at[q - 1], to, shard)
    xrecv[role] = xsend[role]
    fetches[4].wait()
    fetches[5].wait()
    for q in range(1, 4):
        settle(xrecv.at[0], x_r.at[q - 1])

    pieces = [xrecv[q].astype(F32) for q in range(4)]

    def tile(c):
        block, i = divmod(c, 12)
        return pieces[block][8 * (i // 6):8 * (i // 6) + 8, (i % 6) * 128:(i % 6 + 1) * 128]

    def stack(tiles):
        return jnp.concatenate(tiles, axis=0)

    q_tiles = [tile(h) for h in range(16)]
    q_all = stack(q_tiles).astype(BF16)
    k_new = stack([tile(16 + h) for h in range(16)]).astype(BF16)
    v_new = stack([tile(32 + h) for h in range(16)]).astype(BF16)

    def head(ref, h):
        return ref[:, h * 128:(h + 1) * 128]

    s1 = stack([nt(q_tiles[h].astype(BF16), head(keys, h)) for h in range(16)]) * scale
    s2 = nt(q_all, k_new) * scale
    ri = lax.broadcasted_iota(jnp.int32, (128, 128), 0)
    ci = lax.broadcasted_iota(jnp.int32, (128, 128), 1)
    allowed = (ri // 8 == ci // 8) & (ci % 8 <= ri % 8) & (ci % 8 < length)
    s2 = jnp.where(allowed, s2, -1e30)
    top = jnp.maximum(jnp.max(s1, axis=1, keepdims=True), jnp.max(s2, axis=1, keepdims=True))
    e1, e2 = jnp.exp(s1 - top), jnp.exp(s2 - top)
    den = jnp.sum(e1, axis=1, keepdims=True) + jnp.sum(e2, axis=1, keepdims=True)
    w1, w2 = e1 / den, e2 / den
    r2 = w2.astype(BF16)
    o2 = nn(r2, v_new)
    out_tiles = [
        nn(w1[8 * h:8 * h + 8].astype(BF16), head(vals, h)) + o2[8 * h:8 * h + 8]
        for h in range(16)
    ]
    for i in range(8):
        hrs[:, i * 128:(i + 1) * 128] = stack([out_tiles[i], out_tiles[8 + i]]).astype(BF16)

    @pl.when(role == LEARNER)
    def _():
        settle(grecv, gs_r)
        g_tiles = [None] * 16
        for i in range(8):
            cols = slice(i * 128, (i + 1) * 128)
            total = gsend[shard, :, cols].astype(F32)
            for k in range(31):
                total += grecv[k, :, cols].astype(F32)
            g_tiles[i] = jnp.where(live8, total[0:8], 0.0)
            g_tiles[8 + i] = jnp.where(live8, total[8:16], 0.0)
        g_all = stack(g_tiles).astype(BF16)
        gw1 = stack([nt(g_tiles[h].astype(BF16), head(vals, h)) for h in range(16)])
        gw2 = nt(g_all, v_new)
        dots = jnp.sum(w1 * gw1, axis=1, keepdims=True) + jnp.sum(w2 * gw2, axis=1, keepdims=True)
        gs1 = w1 * (gw1 - dots) * scale
        gs2 = (w2 * (gw2 - dots) * scale).astype(BF16)
        gq2 = nn(gs2, k_new)
        gk = tn(gs2, q_all)
        gv = tn(r2, g_all)
        gp = [
            nn(gs1[8 * h:8 * h + 8].astype(BF16), head(keys, h)) + gq2[8 * h:8 * h + 8]
            for h in range(16)
        ]
        gp += [gk[8 * h:8 * h + 8] for h in range(16)]
        gp += [gv[8 * h:8 * h + 8] for h in range(16)]
        live_out = [jnp.where(live8, t, 0.0) for t in out_tiles]
        for q in range(4):
            tiles = [(gp[12 * q + i], gp[12 * q + 6 + i]) for i in range(6)]
            tiles += [(live_out[4 * q + i], live_out[4 * q + 2 + i]) for i in range(2)]
            for i, pair in enumerate(tiles):
                rsend[q, :, i * 128:(i + 1) * 128] = stack(pair).astype(BF16)
        for q in range(3):
            put(rsend.at[q], rmsg, rel_s.at[q], rel_r, q, shard)
        for q in range(3):
            put(cot_hbm, cot, cot_s.at[q], cot_r, q, shard)
        rmsg[...] = rsend[3]

    def shard_at(py, px, pz):
        return (py % 4) * 8 + (px % 4) * 2 + pz % 2

    class Gather:
        def __init__(self, msg, buf, send, recv):
            self.msg, self.buf, self.send, self.recv = msg, buf, send, recv

        def hop(self, step, half, src, dst, dy, dx, dz):
            put(src, dst, self.send, self.recv.at[half, step], role,
                shard_at(y + dy, x + dx, zl + dz))

        def first(self):
            self.buf[y, x, zl] = self.msg[...]
            for half in range(2):
                lanes = pl.ds(half * 512, 512)
                for d, dz in ((1, 0), (3, 0), (0, 1), (1, 1), (3, 1)):
                    self.hop(0, half, self.msg.at[:, lanes], self.buf.at[y, x, zl, :, lanes],
                             d * half, d * (1 - half), dz)

        def second(self):
            for half in range(2):
                settle(selrecv.at[0:10], self.recv.at[half, 0])
                lanes = pl.ds(half * 512, 512)
                dy, dx = half, 1 - half
                before = self.buf.at[(y + 3 * dy) % 4, (x + 3 * dx) % 4, zl, :, lanes]
                after = self.buf.at[(y + dy) % 4, (x + dx) % 4, 1 - zl, :, lanes]
                self.hop(1, half, before, before, dy, dx, 0)
                self.hop(1, half, after, after, 3 * dy, 3 * dx, 0)

        def third(self):
            for half in range(2):
                settle(trecv.at[0:1], self.recv.at[half, 1])
                lanes = pl.ds(half * 512, 512)
                line = self.buf.at[:, x, :, :, lanes] if half else self.buf.at[y, :, :, :, lanes]
                for d in (1, 3):
                    self.hop(2, half, line, line, d * (1 - half), d * half, 0)

        def fourth(self):
            for half in range(2):
                settle(trecv.at[0:8], self.recv.at[half, 2])
                lanes = pl.ds(half * 512, 512)
                if half:
                    before = self.buf.at[0:2, (x + 3) % 4, :, :, lanes]
                    after = self.buf.at[2:4, (x + 1) % 4, :, :, lanes]
                else:
                    before = self.buf.at[(y + 3) % 4, 0:2, :, :, lanes]
                    after = self.buf.at[(y + 1) % 4, 2:4, :, :, lanes]
                self.hop(3, half, before, before, 1 - half, half, 0)
                self.hop(3, half, after, after, 3 * (1 - half), 3 * half, 0)

        def last(self):
            for half in range(2):
                settle(trecv.at[0:4], self.recv.at[half, 3])

        def sent(self):
            settle(trecv, self.send)

    mixes = Gather(hrs, hrrecv, hr_s, hr_r)
    grads = Gather(rmsg, agrecv, ag_s, ag_r)

    @pl.when(role != LEARNER)
    def _():
        mixes.first()
        settle(rmsg, rel_r)
    grads.first()

    @pl.when(role == LEARNER)
    def _():
        mixes.first()
    grads.second()
    grads.third()
    mixes.second()
    grads.fourth()
    mixes.third()
    grads.last()

    got_ids = idrecv[...].astype(F32)[:, 8:16, 64:65]
    got_ids = jnp.broadcast_to(
        jnp.concatenate([got_ids, got_ids], axis=1), (32, 16, 128)).reshape(512, 128)
    lane = lax.broadcasted_iota(jnp.int32, (512, 128), 1).astype(F32)
    half = (lax.broadcasted_iota(jnp.int32, (512, 128), 0) // 8) % 2
    low = jnp.where(got_ids == lane, 1.0, 0.0).astype(BF16)
    high = jnp.where(got_ids == lane + 128.0, 1.0, 0.0).astype(BF16)
    rows = nn(low, table[0:128, :]) + nn(high, table[128:256, :])
    halves = [jnp.where(half == j, rows, 0.0).astype(BF16) for j in range(2)]
    for f in fetches[6:]:
        f.wait()

    copies = []

    def copy_out(a, b):
        c = pltpu.make_async_copy(a, b, out_sem.at[len(copies)])
        c.start()
        copies.append(c)

    def spread(src, dst, n):
        put(src, dst, e_s.at[0, n], e_r.at[0, n], sibling, shard)
        put(src, dst, e_s.at[1, n], e_r.at[1, n], across, shard)
        copy_out(src, dst)

    def q_cols(of, c):
        return nq_out.at[:, pl.ds(pl.multiple_of(of * 1536 + c * CHUNK, 128), CHUNK)]

    def o_rows(of):
        return no_out.at[pl.ds(pl.multiple_of(of * 512, 128), 512), :]

    for c in range(N_CHUNK):
        j, at = divmod(c * CHUNK, 768)
        cols = slice(c * CHUNK, (c + 1) * CHUNK)
        grad = tn(halves[j], agrecv[:, :, :, :, at:at + CHUNK].reshape(512, CHUNK))
        new, one, two = adamw(wq[:, cols], grad, m_q[:, cols], v_q[:, cols])
        nq[:, cols] = new.astype(BF16)
        m_q[:, cols] = one
        v_q[:, cols] = two
        spread(nq.at[:, cols], q_cols(role, c), c)

    @pl.when(role != LEARNER)
    def _():
        settle(cot, cot_r)
    cot_wide = jnp.broadcast_to(
        cot[...].astype(F32).reshape(32, 1, 8, 128), (32, 2, 8, 128)).reshape(512, 128)
    cot_both = jnp.concatenate(
        [jnp.where(half == j, cot_wide, 0.0).astype(BF16) for j in range(2)], axis=1)
    grad_out = tn(agrecv[:, :, :, :, 768:1024].reshape(512, 256), cot_both)
    for j in range(2):
        here = slice(j * 256, (j + 1) * 256)
        params = wout[pl.ds(pl.multiple_of(row0 + j * 256, 128), 256), :]
        new, one, two = adamw(
            params, grad_out[:, j * 128:(j + 1) * 128], m_o[here, :], v_o[here, :])
        no[here, :] = new.astype(BF16)
        m_o[here, :] = one
        v_o[here, :] = two
    spread(no, o_rows(role), N_CHUNK)
    copy_out(m_q, mq_out)
    copy_out(v_q, sq_out)
    copy_out(m_o, mo_out)
    copy_out(v_o, so_out)

    mixes.fourth()

    def part(of, n):
        return q_cols(of, n) if n < N_CHUNK else o_rows(of)

    for n in range(N_CHUNK + 1):
        settle(part(across, n), e_r.at[1, n])
        put(part(across, n), part(across, n), e_s.at[2, n], e_r.at[2, n], sibling, shard)

    mixes.last()
    mix = hrrecv[...].reshape(512, 1024)
    upper = nn(mix, wout[0:1024, :]).reshape(32, 2, 8, 128)
    lower = nn(mix, wout[1024:2048, :]).reshape(32, 2, 8, 128)
    dec[...] = (upper[:, 0] + lower[:, 1]).reshape(256, 128).astype(BF16)
    copy_out(dec, dec_out)

    for n in range(N_CHUNK + 1):
        settle(part(sibling, n), e_r.at[0, n])
        settle(part((1 - z_hi) * 2 + (1 - core), n), e_r.at[2, n])
        for way in range(3):
            settle(part(role, n), e_s.at[way, n])
    for c in copies:
        c.wait()
    for q in range(3):
        settle(idx4.at[0], id_s.at[q])
        settle(xsend.at[0], x_s.at[q])

    @pl.when(holder)
    def _():
        settle(tsend.at[0:23], ts_s)
        settle(selsend.at[0:31], sel_s)

    @pl.when(jnp.logical_not(holder))
    def _():
        settle(tsend, ts_s)

    @pl.when(role == LEARNER)
    def _():
        for q in range(3):
            settle(cot, cot_s.at[q])
            settle(rmsg, rel_s.at[q])
        settle(gsend.at[0:31], gs_s)
    settle(idrecv.at[0:31], idg_s)
    grads.sent()
    mixes.sent()


SHAPES = (
    ((256, 128), BF16), ((128, 6144), BF16), ((2048, 128), BF16),
    ((128, 1536), F32), ((128, 1536), F32), ((512, 128), F32), ((512, 128), F32),
)


def hand_over(*refs):
    ins, outs, stage, sems = refs[:7], refs[7:14], refs[14:21], refs[21]
    moves = []
    for a, v, b in zip(ins, stage, outs):
        pieces = 4 if a.shape == (128, 6144) else 2 if a.shape[0] * a.shape[1] > 131072 else 1
        rows = a.shape[0] // pieces
        for i in range(pieces):
            part, n = pl.ds(i * rows, rows), len(moves)
            moves.append((
                pltpu.make_async_copy(a.at[part, :], v.at[part, :], sems.at[0, n]),
                pltpu.make_async_copy(v.at[part, :], b.at[part, :], sems.at[1, n])))
    for m, _ in moves:
        m.start()
    for m, n in moves:
        m.wait()
        n.start()
    for _, n in moves:
        n.wait()


def shards(*args):
    any_ = pl.BlockSpec(memory_space=pl.ANY)
    smem = pl.BlockSpec(memory_space=pltpu.SMEM)
    dma, vm = pltpu.SemaphoreType.DMA, pltpu.VMEM
    done = pl.pallas_call(
        kernel,
        out_shape=tuple(jax.ShapeDtypeStruct(*a) for a in SHAPES),
        in_specs=[smem, smem] + [any_] * 10,
        out_specs=(any_,) * 7,
        scratch_shapes=[
            vm((256, 128), BF16),
            vm((128, 2048), BF16),
            vm((128, 2048), BF16),
            vm((128, 1536), BF16),
            vm((2048, 128), BF16),
            vm((128, 1536), F32),
            vm((128, 1536), F32),
            vm((512, 128), F32),
            vm((512, 128), F32),
            vm((256, 128), BF16),
            vm((24, 128, 128), BF16),
            vm((31, 128, 128), BF16),
            vm((32, 16, 1024), BF16),
            vm((31, 16, 1024), BF16),
            vm((4, 8, 128), F32),
            vm((16, 128), BF16),
            vm((32, 16, 128), BF16),
            vm((32, 32, 128), BF16),
            vm((24, 32, 128), BF16),
            vm((4, 16, 768), BF16),
            vm((4, 16, 768), BF16),
            vm((16, 1024), BF16),
            vm((4, 4, 2, 16, 1024), BF16),
            vm((4, 16, 1024), BF16),
            vm((16, 1024), BF16),
            vm((4, 4, 2, 16, 1024), BF16),
            vm((128, 1536), BF16),
            vm((512, 128), BF16),
            vm((256, 128), BF16),
            dma((10,)),
            dma((N_CHUNK + 6,)),
            dma((3,)), dma((3,)),
            dma, dma,
            dma, dma,
            dma, dma,
            dma((3,)), dma,
            dma, dma,
            dma((3,)), dma((3,)),
            dma((3,)), dma,
            dma, dma((2, 4)),
            dma, dma((2, 4)),
            dma((3, N_CHUNK + 1)), dma((3, N_CHUNK + 1)),
        ],
        compiler_params=pltpu.CompilerParams(
            collective_id=0, has_side_effects=True, vmem_limit_bytes=60 * 1024 * 1024),
        name="policy_update",
    )(*args)
    return tuple(pl.pallas_call(
        hand_over,
        out_shape=tuple(jax.ShapeDtypeStruct(*a) for a in SHAPES),
        in_specs=[any_] * 7,
        out_specs=(any_,) * 7,
        scratch_shapes=[vm(*a) for a in SHAPES] + [dma((2, 16))],
        compiler_params=pltpu.CompilerParams(vmem_limit_bytes=60 * 1024 * 1024),
        name="hand_over",
    )(*done))


def solution(mesh):
    both = ("role", "shard")
    return jax.shard_map(
        shards,
        mesh=mesh,
        in_specs=(
            P(both, None), P(both), P(None, "shard"), P(both, None, None), P(both, None, None),
            P("shard", None), P(None, "shard"), P("shard", "role"), P("shard", "role"),
            P("role", "shard"), P("role", "shard"), P("role", "shard"),
        ),
        out_specs=(
            P("role", "shard"), P("shard", None), P(None, "shard"), P("shard", "role"),
            P("shard", "role"), P("role", "shard"), P("role", "shard"),
        ),
        check_vma=False,
    )
```

```python
import jax
import jax.numpy as jnp
from jax import lax
from jax.experimental import pallas as pl
from jax.experimental.pallas import tpu as pltpu
from jax.sharding import PartitionSpec as P

HD = 128
MESH = pl.DeviceIdType.MESH
F32 = jnp.float32
BF16 = jnp.bfloat16
LEARNER = 3

learn_rate = 0.001
first_decay = 0.9
second_decay = 0.95
adam_eps = 1e-08
weight_decay = 0.1
first_fix = 1.0 - 0.9**10
second_fix = 1.0 - 0.95**10
scale = HD ** (-0.5)

N_CHUNK = 4
ORDER = 13
CHUNK = 1536 // N_CHUNK


def adamw(params, gradient, first_moment, second_moment):
    moment_one = first_decay * first_moment + (1.0 - first_decay) * gradient
    moment_two = second_decay * second_moment + (1.0 - second_decay) * gradient * gradient
    stepped = moment_one / first_fix / (jnp.sqrt(moment_two / second_fix) + adam_eps)
    wide_params = params.astype(F32)
    updated = wide_params - learn_rate * (stepped + weight_decay * wide_params)
    return (updated, moment_one, moment_two)


def settle(ref, sem):
    pltpu.make_async_copy(ref, ref, sem).wait()


def nt(a, b):
    return lax.dot_general(a, b, (((1,), (1,)), ((), ())), preferred_element_type=F32)


def tn(a, b):
    return lax.dot_general(a, b, (((0,), (0,)), ((), ())), preferred_element_type=F32)


def nn(a, b):
    return jnp.dot(a, b, preferred_element_type=F32)


def kernel(
    ids_ref, len_ref, table_hbm, keys_hbm, vals_hbm, wqkv_hbm, wout_hbm,
    m_q_hbm, v_q_hbm, m_o_hbm, v_o_hbm, cot_hbm,
    dec_out, nq_out, no_out, mq_out, sq_out, mo_out, so_out,
    table, keys, vals, wq, wout, m_q, v_q, m_o, v_o, cot,
    tsend, trecv, gsend, grecv, idx4, idsend, idrecv, selsend, selrecv,
    xsend, xrecv, hrs, hrrecv, hsend, hmsg, hgrecv, rsend, rmsg, agrecv,
    count_mix, count_grad, nq, no, dec,
    loc, out_sem, id_s, id_r, idg_s, idg_r, ts_s, ts_r, gs_s, gs_r,
    cot_s, cot_r, sel_s, sel_r, x_s, x_r, hrel_s, hrel_r, rel_s, rel_r,
    hg_s, hg_r, ag_s, ag_r, hr_s, hr_r,
    e_s, e_r,
):
    role = lax.axis_index("role")
    shard = lax.axis_index("shard")
    y, x, zl = shard // 8, (shard // 2) % 4, shard % 2
    z_hi, core = role // 2, role % 2
    sibling = z_hi * 2 + (1 - core)
    across = (1 - z_hi) * 2 + core

    def peer(k):
        py, px, pz = (y + k // 8) % 4, (x + (k // 2) % 4) % 4, (zl + k % 2) % 2
        spot = (px + py) % 4
        return py * 8 + px * 2 + pz, spot < 3, py * 6 + spot * 2 + pz

    my_spot = (x + y) % 4
    holder = my_spot < 3
    my_unit = jnp.where(holder, y * 6 + my_spot * 2 + zl, 0)

    def put(src, dst, send, recv, to_role, to_shard):
        pltpu.make_async_remote_copy(
            src_ref=src, dst_ref=dst, send_sem=send, recv_sem=recv,
            device_id=(to_role, to_shard), device_id_type=MESH,
        ).start()

    def each_peer(body, first=1, last=32):
        def step(j, carry):
            k = (j * ORDER) % 32
            body(k, *peer(k))
            return carry
        lax.fori_loop(first, last, step, 0)

    barrier = pltpu.get_barrier_semaphore()
    each_peer(lambda k, p, h, u: pl.semaphore_signal(
        barrier, inc=1, device_id=(role, p), device_id_type=MESH))
    for q in range(1, 4):
        pl.semaphore_signal(
            barrier, inc=1, device_id=((role + q) % 4, shard), device_id_type=MESH)

    col0 = pl.multiple_of(role * 1536, 128)
    row0 = pl.multiple_of(role * 512, 128)
    fetches = [
        pltpu.make_async_copy(a, b, loc.at[i])
        for i, (a, b) in enumerate((
            (table_hbm, table),
            (wqkv_hbm.at[:, pl.ds(col0, 1536)], wq),
            (wout_hbm, wout),
            (cot_hbm, cot),
            (keys_hbm.at[0], keys),
            (vals_hbm.at[0], vals),
            (m_q_hbm, m_q),
            (v_q_hbm, v_q),
            (m_o_hbm, m_o),
            (v_o_hbm, v_o),
        ))
    ]
    for i, f in enumerate(fetches):
        if i != 3:
            f.start()

    @pl.when(role == LEARNER)
    def _():
        fetches[3].start()

    row8 = lax.broadcasted_iota(jnp.int32, (8, 128), 0)
    lane8 = lax.broadcasted_iota(jnp.int32, (8, 128), 1)
    ids = jnp.zeros((8, 128), jnp.int32)
    for i in range(8):
        ids = jnp.where(row8 == i, ids_ref[0, i], ids)
    ids = ids.astype(F32)
    length = len_ref[0]
    live8 = row8 < length
    idx4[role] = ids

    fetches[0].wait()
    fetches[1].wait()
    for c in range(12):
        part = nn(table[...], wq[:, c * 128:(c + 1) * 128]).astype(BF16)
        tsend[2 * c] = part[0:128]
        tsend[2 * c + 1] = part[128:256]

    pl.semaphore_wait(barrier, 34)

    for q in range(1, 4):
        put(idx4.at[role], idx4.at[role], id_s.at[q - 1], id_r.at[q - 1], (role + q) % 4, shard)

    def send_part(k, p, h, u):
        @pl.when(h)
        def _():
            put(tsend.at[u], trecv.at[k - 1], ts_s, ts_r, role, p)
    each_peer(send_part, 1, 12)

    for q in range(1, 4):
        settle(idx4.at[0], id_r.at[q - 1])
    lane16 = lax.broadcasted_iota(jnp.int32, (16, 128), 1)
    all_ids = jnp.where(
        lane16 < 64,
        jnp.concatenate([idx4[0], idx4[1]], axis=0),
        jnp.concatenate([idx4[2], idx4[3]], axis=0)).astype(BF16)
    idsend[...] = all_ids
    idrecv[shard] = all_ids

    def send_ids(now):
        def body(k, p, h, u):
            @pl.when(h if now else jnp.logical_not(h))
            def _():
                put(idsend, idrecv.at[shard], idg_s, idg_r, role, p)
        each_peer(body)
    send_ids(True)
    each_peer(send_part, 12, 32)

    @pl.when(role == LEARNER)
    def _():
        fetches[2].wait()
        fetches[3].wait()
        for i in range(8):
            upper, lower = (
                nt(cot[...], wout[j * 1024 + i * 128:j * 1024 + (i + 1) * 128, :])
                .reshape(32, 8, 128)
                for j in range(2)
            )
            gsend[:, :, i * 128:(i + 1) * 128] = jnp.concatenate(
                [upper, lower], axis=1).astype(BF16)

    @pl.when(role != LEARNER)
    def _():
        fetches[2].wait()

    @pl.when(holder)
    def _():
        settle(idrecv.at[0:31], idg_r)
        got = idrecv[...].astype(F32)
        got = jnp.concatenate([
            jnp.broadcast_to(got[:, :, 0:1], (32, 16, 128)),
            jnp.broadcast_to(got[:, :, 64:65], (32, 16, 128))], axis=1).reshape(1024, 128)
        lane = lax.broadcasted_iota(jnp.int32, (1024, 128), 1) + 128 * (my_unit % 2)
        chosen = jnp.where(got == lane.astype(F32), 1.0, 0.0).astype(BF16)
        settle(trecv, ts_r)

        def add(k, total):
            return total + trecv[k].astype(F32)
        total = lax.fori_loop(0, 31, add, tsend[my_unit].astype(F32))
        whole = total.astype(BF16)
        selsend[...] = nn(chosen, whole).astype(BF16).reshape(32, 32, 128)

        def send_rows(k, p, h, u):
            put(selsend.at[p], selrecv.at[my_unit], sel_s, sel_r, role, p)
        each_peer(send_rows)
        selrecv[my_unit] = selsend[shard]

    @pl.when(role == LEARNER)
    def _():
        each_peer(lambda k, p, h, u: put(gsend.at[p], grecv.at[k - 1], gs_s, gs_r, role, p))
        for q in range(3):
            put(cot_hbm, cot, cot_s.at[q], cot_r, q, shard)
    send_ids(False)

    @pl.when(holder)
    def _():
        settle(selrecv.at[0:23], sel_r)

    @pl.when(jnp.logical_not(holder))
    def _():
        settle(idrecv.at[0:31], idg_r)
        settle(selrecv, sel_r)

    blocks = [selrecv[2 * c].astype(F32) + selrecv[2 * c + 1].astype(F32) for c in range(12)]
    for q in range(4):
        for i in range(6):
            pair = jnp.concatenate(
                [blocks[i][8 * q:8 * q + 8], blocks[6 + i][8 * q:8 * q + 8]], axis=0)
            xsend[q, :, i * 128:(i + 1) * 128] = pair.astype(BF16)
    for q in range(1, 4):
        to = (role + q) % 4
        put(xsend.at[to], xrecv.at[role], x_s.at[q - 1], x_r.at[q - 1], to, shard)
    xrecv[role] = xsend[role]
    fetches[4].wait()
    fetches[5].wait()
    for q in range(1, 4):
        settle(xrecv.at[0], x_r.at[q - 1])

    pieces = [xrecv[q].astype(F32) for q in range(4)]

    def tile(c):
        block, i = divmod(c, 12)
        return pieces[block][8 * (i // 6):8 * (i // 6) + 8, (i % 6) * 128:(i % 6 + 1) * 128]

    def stack(tiles):
        return jnp.concatenate(tiles, axis=0)

    q_tiles = [tile(h) for h in range(16)]
    q_all = stack(q_tiles).astype(BF16)
    k_new = stack([tile(16 + h) for h in range(16)]).astype(BF16)
    v_new = stack([tile(32 + h) for h in range(16)]).astype(BF16)

    def head(ref, h):
        return ref[:, h * 128:(h + 1) * 128]

    s1 = stack([nt(q_tiles[h].astype(BF16), head(keys, h)) for h in range(16)]) * scale
    s2 = nt(q_all, k_new) * scale
    ri = lax.broadcasted_iota(jnp.int32, (128, 128), 0)
    ci = lax.broadcasted_iota(jnp.int32, (128, 128), 1)
    allowed = (ri // 8 == ci // 8) & (ci % 8 <= ri % 8) & (ci % 8 < length)
    s2 = jnp.where(allowed, s2, -1e30)
    top = jnp.maximum(jnp.max(s1, axis=1, keepdims=True), jnp.max(s2, axis=1, keepdims=True))
    e1, e2 = jnp.exp(s1 - top), jnp.exp(s2 - top)
    den = jnp.sum(e1, axis=1, keepdims=True) + jnp.sum(e2, axis=1, keepdims=True)
    w1, w2 = e1 / den, e2 / den
    r2 = w2.astype(BF16)
    o2 = nn(r2, v_new)
    out_tiles = [
        nn(w1[8 * h:8 * h + 8].astype(BF16), head(vals, h)) + o2[8 * h:8 * h + 8]
        for h in range(16)
    ]
    for i in range(8):
        hrs[:, i * 128:(i + 1) * 128] = stack([out_tiles[i], out_tiles[8 + i]]).astype(BF16)

    @pl.when(role == LEARNER)
    def _():
        live_out = [jnp.where(live8, t, 0.0) for t in out_tiles]
        for q in range(4):
            for i in range(2):
                hsend[q, :, i * 128:(i + 1) * 128] = stack(
                    [live_out[4 * q + i], live_out[4 * q + 2 + i]]).astype(BF16)
        for q in range(3):
            put(hsend.at[q], hmsg, hrel_s.at[q], hrel_r, q, shard)
        hmsg[...] = hsend[3]
        settle(grecv, gs_r)
        g_tiles = [None] * 16
        for i in range(8):
            cols = slice(i * 128, (i + 1) * 128)
            total = gsend[shard, :, cols].astype(F32)
            for k in range(31):
                total += grecv[k, :, cols].astype(F32)
            g_tiles[i] = jnp.where(live8, total[0:8], 0.0)
            g_tiles[8 + i] = jnp.where(live8, total[8:16], 0.0)
        g_all = stack(g_tiles).astype(BF16)
        gw1 = stack([nt(g_tiles[h].astype(BF16), head(vals, h)) for h in range(16)])
        gw2 = nt(g_all, v_new)
        dots = jnp.sum(w1 * gw1, axis=1, keepdims=True) + jnp.sum(w2 * gw2, axis=1, keepdims=True)
        gs1 = w1 * (gw1 - dots) * scale
        gs2 = (w2 * (gw2 - dots) * scale).astype(BF16)
        gq2 = nn(gs2, k_new)
        gk = tn(gs2, q_all)
        gv = tn(r2, g_all)
        gp = [
            nn(gs1[8 * h:8 * h + 8].astype(BF16), head(keys, h)) + gq2[8 * h:8 * h + 8]
            for h in range(16)
        ]
        gp += [gk[8 * h:8 * h + 8] for h in range(16)]
        gp += [gv[8 * h:8 * h + 8] for h in range(16)]
        for q in range(4):
            tiles = [(gp[12 * q + i], gp[12 * q + 6 + i]) for i in range(6)]
            for i, pair in enumerate(tiles):
                rsend[q, :, i * 128:(i + 1) * 128] = stack(pair).astype(BF16)
        for q in range(3):
            put(rsend.at[q], rmsg, rel_s.at[q], rel_r, q, shard)

        rmsg[...] = rsend[3]

    def shard_at(py, px, pz):
        return (py % 4) * 8 + (px % 4) * 2 + pz % 2

    class Gather:
        def __init__(self, msg, buf, send, recv, count):
            self.msg, self.buf, self.send, self.recv, self.count = msg, buf, send, recv, count

        def lanes(self, half):
            width = self.msg.shape[1] // 2
            return pl.ds(half * width, width)

        def hop(self, step, half, src, dst, dy, dx, dz):
            put(src, dst, self.send.at[half], self.recv.at[half, step], role,
                shard_at(y + dy, x + dx, zl + dz))

        def arrived(self, half, step, blocks):
            settle(self.count.at[0:blocks], self.recv.at[half, step])

        def start(self, far):
            self.buf[y, x, zl] = self.msg[...]
            for half in range(2):
                n = self.lanes(half)
                spots = [(0, 1), (1, 0), (3, 0), (1, 1), (3, 1)] + far
                for d, dz in spots:
                    self.hop(0, half, self.msg.at[:, n], self.buf.at[y, x, zl, :, n],
                             d * half, d * (1 - half), dz)

        def line(self, half):
            n = self.lanes(half)
            return self.buf.at[:, x, :, :, n] if half else self.buf.at[y, :, :, :, n]

        def sent(self):
            for half in range(2):
                settle(self.count.at[0:31], self.send.at[half])

    class Short(Gather):
        def first(self):
            self.start([(2, 0), (2, 1)])

        def second(self):
            for half in range(2):
                self.arrived(half, 0, 7)
                for d in (2, 1, 3):
                    self.hop(1, half, self.line(half), self.line(half),
                             d * (1 - half), d * half, 0)

        def last(self):
            for half in range(2):
                self.arrived(half, 1, 24)

    class Long(Gather):
        def first(self):
            self.start([])

        def second(self):
            for half in range(2):
                self.arrived(half, 0, 5)
                n = self.lanes(half)
                dy, dx = half, 1 - half
                before = self.buf.at[(y + 3 * dy) % 4, (x + 3 * dx) % 4, zl, :, n]
                after = self.buf.at[(y + dy) % 4, (x + dx) % 4, 1 - zl, :, n]
                self.hop(1, half, before, before, dy, dx, 0)
                self.hop(1, half, after, after, 3 * dy, 3 * dx, 0)

        def third(self):
            for half in range(2):
                self.arrived(half, 1, 2)
                for d in (1, 3):
                    self.hop(2, half, self.line(half), self.line(half),
                             d * (1 - half), d * half, 0)

        def fourth(self):
            for half in range(2):
                self.arrived(half, 2, 16)
                n = self.lanes(half)
                if half:
                    before = self.buf.at[0:2, (x + 3) % 4, :, :, n]
                    after = self.buf.at[2:4, (x + 1) % 4, :, :, n]
                else:
                    before = self.buf.at[(y + 3) % 4, 0:2, :, :, n]
                    after = self.buf.at[(y + 1) % 4, 2:4, :, :, n]
                self.hop(3, half, before, before, 1 - half, half, 0)
                self.hop(3, half, after, after, 3 * (1 - half), 3 * half, 0)

        def last(self):
            for half in range(2):
                self.arrived(half, 3, 8)

    mixes = Long(hrs, hrrecv, hr_s, hr_r, count_mix)
    heads = Short(hmsg, hgrecv, hg_s, hg_r, idrecv)
    grads = Short(rmsg, agrecv, ag_s, ag_r, count_grad)

    @pl.when(role != LEARNER)
    def _():
        settle(hmsg, hrel_r)
        heads.first()
        mixes.first()
        settle(rmsg, rel_r)
    grads.first()

    @pl.when(role == LEARNER)
    def _():
        heads.first()
        mixes.first()
    heads.second()
    grads.second()
    mixes.second()

    got_ids = idrecv[...].astype(F32)[:, 8:16, 64:65]
    got_ids = jnp.broadcast_to(
        jnp.concatenate([got_ids, got_ids], axis=1), (32, 16, 128)).reshape(512, 128)
    lane = lax.broadcasted_iota(jnp.int32, (512, 128), 1).astype(F32)
    half = (lax.broadcasted_iota(jnp.int32, (512, 128), 0) // 8) % 2
    low = jnp.where(got_ids == lane, 1.0, 0.0).astype(BF16)
    high = jnp.where(got_ids == lane + 128.0, 1.0, 0.0).astype(BF16)
    rows = nn(low, table[0:128, :]) + nn(high, table[128:256, :])
    halves = [jnp.where(half == j, rows, 0.0).T.astype(BF16) for j in range(2)]
    for f in fetches[6:]:
        f.wait()

    copies = []

    def copy_out(a, b):
        c = pltpu.make_async_copy(a, b, out_sem.at[len(copies)])
        c.start()
        copies.append(c)

    def spread(src, dst, n):
        put(src, dst, e_s.at[1, n], e_r.at[1, n], across, shard)
        put(src, dst, e_s.at[0, n], e_r.at[0, n], sibling, shard)
        copy_out(src, dst)

    def q_cols(of, c):
        return nq_out.at[:, pl.ds(pl.multiple_of(of * 1536 + c * CHUNK, 128), CHUNK)]

    def o_rows(of):
        return no_out.at[pl.ds(pl.multiple_of(of * 512, 128), 512), :]

    @pl.when(role != LEARNER)
    def _():
        settle(cot, cot_r)
    cot_wide = jnp.broadcast_to(
        cot[...].astype(F32).reshape(32, 1, 8, 128), (32, 2, 8, 128)).reshape(512, 128)
    cot_both = jnp.concatenate(
        [jnp.where(half == j, cot_wide, 0.0).astype(BF16) for j in range(2)], axis=1)
    heads.last()
    grad_out = tn(hgrecv[...].reshape(512, 256), cot_both)
    for j in range(2):
        here = slice(j * 256, (j + 1) * 256)
        params = wout[pl.ds(pl.multiple_of(row0 + j * 256, 128), 256), :]
        new, one, two = adamw(
            params, grad_out[:, j * 128:(j + 1) * 128], m_o[here, :], v_o[here, :])
        no[here, :] = new.astype(BF16)
        m_o[here, :] = one
        v_o[here, :] = two
    spread(no, o_rows(role), N_CHUNK)
    copy_out(m_o, mo_out)
    copy_out(v_o, so_out)
    mixes.third()

    grads.last()
    for c in range(N_CHUNK):
        j, at = divmod(c * CHUNK, 768)
        cols = slice(c * CHUNK, (c + 1) * CHUNK)
        grad = nn(halves[j], agrecv[:, :, :, :, at:at + CHUNK].reshape(512, CHUNK))
        new, one, two = adamw(wq[:, cols], grad, m_q[:, cols], v_q[:, cols])
        nq[:, cols] = new.astype(BF16)
        m_q[:, cols] = one
        v_q[:, cols] = two
        spread(nq.at[:, cols], q_cols(role, c), c)
    copy_out(m_q, mq_out)
    copy_out(v_q, sq_out)
    mixes.fourth()

    def part(of, n):
        return q_cols(of, n) if n < N_CHUNK else o_rows(of)

    for n in (N_CHUNK, *range(N_CHUNK)):
        settle(part(across, n), e_r.at[1, n])
        put(part(across, n), part(across, n), e_s.at[2, n], e_r.at[2, n], sibling, shard)

    mixes.last()
    mix = hrrecv[...].reshape(512, 1024)
    upper = nn(mix, wout[0:1024, :]).reshape(32, 2, 8, 128)
    lower = nn(mix, wout[1024:2048, :]).reshape(32, 2, 8, 128)
    dec[...] = (upper[:, 0] + lower[:, 1]).reshape(256, 128).astype(BF16)
    copy_out(dec, dec_out)

    for n in range(N_CHUNK + 1):
        settle(part(sibling, n), e_r.at[0, n])
        settle(part((1 - z_hi) * 2 + (1 - core), n), e_r.at[2, n])
        for way in range(3):
            settle(part(role, n), e_s.at[way, n])
    for c in copies:
        c.wait()
    for q in range(3):
        settle(idx4.at[0], id_s.at[q])
        settle(xsend.at[0], x_s.at[q])

    @pl.when(holder)
    def _():
        settle(tsend.at[0:23], ts_s)
        settle(selsend.at[0:31], sel_s)

    @pl.when(jnp.logical_not(holder))
    def _():
        settle(tsend, ts_s)

    @pl.when(role == LEARNER)
    def _():
        for q in range(3):
            settle(cot, cot_s.at[q])
            settle(rmsg, rel_s.at[q])
            settle(hmsg, hrel_s.at[q])
        settle(gsend.at[0:31], gs_s)
    settle(idrecv.at[0:31], idg_s)
    heads.sent()
    grads.sent()
    mixes.sent()


SHAPES = (
    ((256, 128), BF16), ((128, 6144), BF16), ((2048, 128), BF16),
    ((128, 1536), F32), ((128, 1536), F32), ((512, 128), F32), ((512, 128), F32),
)


def hand_over(*refs):
    ins, outs, stage, sems = refs[:7], refs[7:14], refs[14:21], refs[21]
    moves = []
    for a, v, b in zip(ins, stage, outs):
        pieces = 4 if a.shape == (128, 6144) else 2 if a.shape[0] * a.shape[1] > 131072 else 1
        rows = a.shape[0] // pieces
        for i in range(pieces):
            part, n = pl.ds(i * rows, rows), len(moves)
            moves.append((
                pltpu.make_async_copy(a.at[part, :], v.at[part, :], sems.at[0, n]),
                pltpu.make_async_copy(v.at[part, :], b.at[part, :], sems.at[1, n])))
    for m, _ in moves:
        m.start()
    for m, n in moves:
        m.wait()
        n.start()
    for _, n in moves:
        n.wait()


def shards(*args):
    any_ = pl.BlockSpec(memory_space=pl.ANY)
    smem = pl.BlockSpec(memory_space=pltpu.SMEM)
    dma, vm = pltpu.SemaphoreType.DMA, pltpu.VMEM
    done = pl.pallas_call(
        kernel,
        out_shape=tuple(jax.ShapeDtypeStruct(*a) for a in SHAPES),
        in_specs=[smem, smem] + [any_] * 10,
        out_specs=(any_,) * 7,
        scratch_shapes=[
            vm((256, 128), BF16),
            vm((128, 2048), BF16),
            vm((128, 2048), BF16),
            vm((128, 1536), BF16),
            vm((2048, 128), BF16),
            vm((128, 1536), F32),
            vm((128, 1536), F32),
            vm((512, 128), F32),
            vm((512, 128), F32),
            vm((256, 128), BF16),
            vm((24, 128, 128), BF16),
            vm((31, 128, 128), BF16),
            vm((32, 16, 1024), BF16),
            vm((31, 16, 1024), BF16),
            vm((4, 8, 128), F32),
            vm((16, 128), BF16),
            vm((32, 16, 128), BF16),
            vm((32, 32, 128), BF16),
            vm((24, 32, 128), BF16),
            vm((4, 16, 768), BF16),
            vm((4, 16, 768), BF16),
            vm((16, 1024), BF16),
            vm((4, 4, 2, 16, 1024), BF16),
            vm((4, 16, 256), BF16),
            vm((16, 256), BF16),
            vm((4, 4, 2, 16, 256), BF16),
            vm((4, 16, 768), BF16),
            vm((16, 768), BF16),
            vm((4, 4, 2, 16, 768), BF16),
            vm((31, 16, 512), BF16),
            vm((31, 16, 384), BF16),
            vm((128, 1536), BF16),
            vm((512, 128), BF16),
            vm((256, 128), BF16),
            dma((10,)),
            dma((N_CHUNK + 6,)),
            dma((3,)), dma((3,)),
            dma, dma,
            dma, dma,
            dma, dma,
            dma((3,)), dma,
            dma, dma,
            dma((3,)), dma((3,)),
            dma((3,)), dma,
            dma((3,)), dma,
            dma((2,)), dma((2, 2)),
            dma((2,)), dma((2, 2)),
            dma((2,)), dma((2, 4)),
            dma((3, N_CHUNK + 1)), dma((3, N_CHUNK + 1)),
        ],
        compiler_params=pltpu.CompilerParams(
            collective_id=0, has_side_effects=True, vmem_limit_bytes=60 * 1024 * 1024),
        name="policy_update",
    )(*args)
    return tuple(pl.pallas_call(
        hand_over,
        out_shape=tuple(jax.ShapeDtypeStruct(*a) for a in SHAPES),
        in_specs=[any_] * 7,
        out_specs=(any_,) * 7,
        scratch_shapes=[vm(*a) for a in SHAPES] + [dma((2, 16))],
        compiler_params=pltpu.CompilerParams(vmem_limit_bytes=60 * 1024 * 1024),
        name="hand_over",
    )(*done))


def solution(mesh):
    both = ("role", "shard")
    return jax.shard_map(
        shards,
        mesh=mesh,
        in_specs=(
            P(both, None), P(both), P(None, "shard"), P(both, None, None), P(both, None, None),
            P("shard", None), P(None, "shard"), P("shard", "role"), P("shard", "role"),
            P("role", "shard"), P("role", "shard"), P("role", "shard"),
        ),
        out_specs=(
            P("role", "shard"), P("shard", None), P(None, "shard"), P("shard", "role"),
            P("shard", "role"), P("role", "shard"), P("role", "shard"),
        ),
        check_vma=False,
    )
```

```python
import jax
import jax.numpy as jnp
from jax import lax
from jax.experimental import pallas as pl
from jax.experimental.pallas import tpu as pltpu
from jax.sharding import PartitionSpec as P

HD = 128
MESH = pl.DeviceIdType.MESH
F32 = jnp.float32
BF16 = jnp.bfloat16
LEARNER = 3

learn_rate = 0.001
first_decay = 0.9
second_decay = 0.95
adam_eps = 1e-08
weight_decay = 0.1
first_fix = 1.0 - 0.9**10
second_fix = 1.0 - 0.95**10
scale = HD ** (-0.5)

N_CHUNK = 4
CHUNKS = ((0, 256), (768, 256), (256, 512), (1024, 512))
ORDER = 13


def adamw(params, gradient, first_moment, second_moment):
    moment_one = first_decay * first_moment + (1.0 - first_decay) * gradient
    moment_two = second_decay * second_moment + (1.0 - second_decay) * gradient * gradient
    stepped = moment_one / first_fix / (jnp.sqrt(moment_two / second_fix) + adam_eps)
    wide_params = params.astype(F32)
    updated = wide_params - learn_rate * (stepped + weight_decay * wide_params)
    return (updated, moment_one, moment_two)


def settle(ref, sem):
    pltpu.make_async_copy(ref, ref, sem).wait()


def nt(a, b):
    return lax.dot_general(a, b, (((1,), (1,)), ((), ())), preferred_element_type=F32)


def tn(a, b):
    return lax.dot_general(a, b, (((0,), (0,)), ((), ())), preferred_element_type=F32)


def nn(a, b):
    return jnp.dot(a, b, preferred_element_type=F32)


def kernel(
    ids_ref, len_ref, table_hbm, keys_hbm, vals_hbm, wqkv_hbm, wout_hbm,
    m_q_hbm, v_q_hbm, m_o_hbm, v_o_hbm, cot_hbm,
    dec_out, nq_out, no_out, mq_out, sq_out, mo_out, so_out,
    table, keys, vals, wq, wout, m_q, v_q, m_o, v_o, cot,
    tsend, trecv, gsend, grecv, idx4, idsend, idrecv, selsend, selrecv,
    xsend, xrecv, hrs, hrrecv, hsend, hmsg, hgrecv, rsend_a, rsend_b, rmsg_a, rmsg_b,
    agrecv_a, agrecv_b,
    count_mix, count_grad, nq, no, dec,
    loc, out_sem, id_s, id_r, idg_s, idg_r, ts_s, ts_r, gs_s, gs_r,
    cot_s, cot_r, sel_s, sel_r, x_s, x_r, hrel_s, hrel_r, rela_s, rela_r, relb_s, relb_r,
    hg_s, hg_r, aga_s, aga_r, agb_s, agb_r, hr_s, hr_r,
    e_s, e_r,
):
    role = lax.axis_index("role")
    shard = lax.axis_index("shard")
    y, x, zl = shard >> 3, (shard >> 1) & 3, shard & 1
    z_hi, core = role >> 1, role & 1
    sibling = z_hi * 2 + (1 - core)
    across = (1 - z_hi) * 2 + core
    others = [(role + q) & 3 for q in range(4)]

    ys = [(y + d) & 3 for d in range(4)]
    xs = [(x + d) & 3 for d in range(4)]
    zs = [zl, 1 - zl]
    spots = [(x + y + d) & 3 for d in range(4)]
    holds = [spot < 3 for spot in spots]
    rows_at = [v * 8 for v in ys]
    cols_at = [v * 2 for v in xs]
    unit_row = [v * 6 for v in ys]
    unit_col = [v * 2 for v in spots]

    def peer(k):
        dy, dx, dz = k >> 3, (k >> 1) & 3, k & 1
        turn = (dy + dx) & 3
        return (rows_at[dy] + cols_at[dx] + zs[dz], holds[turn],
                unit_row[dy] + unit_col[turn] + zs[dz])

    holder = holds[0]
    my_unit = jnp.where(holder, peer(0)[2], 0)

    def put(src, dst, send, recv, to_role, to_shard):
        pltpu.make_async_remote_copy(
            src_ref=src, dst_ref=dst, send_sem=send, recv_sem=recv,
            device_id=(to_role, to_shard), device_id_type=MESH,
        ).start()

    def each_peer(body, first=1, last=32):
        for j in range(first, last):
            k = j * ORDER % 32
            body(k, *peer(k))

    barrier = pltpu.get_barrier_semaphore()
    each_peer(lambda k, p, h, u: pl.semaphore_signal(
        barrier, inc=1, device_id=(role, p), device_id_type=MESH))
    for q in range(1, 4):
        pl.semaphore_signal(
            barrier, inc=1, device_id=(others[q], shard), device_id_type=MESH)

    col0 = pl.multiple_of(role * 1536, 128)
    row0 = pl.multiple_of(role * 512, 128)
    fetches = [
        pltpu.make_async_copy(a, b, loc.at[i])
        for i, (a, b) in enumerate((
            (table_hbm, table),
            (wqkv_hbm.at[:, pl.ds(col0, 1536)], wq),
            (wout_hbm, wout),
            (cot_hbm, cot),
            (keys_hbm.at[0], keys),
            (vals_hbm.at[0], vals),
            (m_q_hbm, m_q),
            (v_q_hbm, v_q),
            (m_o_hbm, m_o),
            (v_o_hbm, v_o),
        ))
    ]
    for i, f in enumerate(fetches):
        if i != 3:
            f.start()

    @pl.when(role == LEARNER)
    def _():
        fetches[3].start()

    row8 = lax.broadcasted_iota(jnp.int32, (8, 128), 0)
    lane8 = lax.broadcasted_iota(jnp.int32, (8, 128), 1)
    ids = jnp.zeros((8, 128), jnp.int32)
    for i in range(8):
        ids = jnp.where(row8 == i, ids_ref[0, i], ids)
    ids = ids.astype(F32)
    length = len_ref[0]
    live8 = row8 < length
    idx4[role] = ids

    fetches[0].wait()
    fetches[1].wait()
    for c in range(12):
        part = nn(table[...], wq[:, c * 128:(c + 1) * 128]).astype(BF16)
        tsend[2 * c] = part[0:128]
        tsend[2 * c + 1] = part[128:256]

    pl.semaphore_wait(barrier, 34)

    for q in range(1, 4):
        put(idx4.at[role], idx4.at[role], id_s.at[q - 1], id_r.at[q - 1], others[q], shard)

    def send_part(k, p, h, u):
        @pl.when(h)
        def _():
            put(tsend.at[u], trecv.at[k - 1], ts_s, ts_r, role, p)
    each_peer(send_part, 1, 12)

    for q in range(1, 4):
        settle(idx4.at[0], id_r.at[q - 1])
    lane16 = lax.broadcasted_iota(jnp.int32, (16, 128), 1)
    all_ids = jnp.where(
        lane16 < 64,
        jnp.concatenate([idx4[0], idx4[1]], axis=0),
        jnp.concatenate([idx4[2], idx4[3]], axis=0)).astype(BF16)
    idsend[...] = all_ids
    idrecv[shard] = all_ids

    def send_ids(now):
        def body(k, p, h, u):
            @pl.when(h if now else jnp.logical_not(h))
            def _():
                put(idsend, idrecv.at[shard], idg_s, idg_r, role, p)
        each_peer(body)
    send_ids(True)
    each_peer(send_part, 12, 32)

    @pl.when(role == LEARNER)
    def _():
        fetches[2].wait()
        fetches[3].wait()
        for i in range(8):
            upper, lower = (
                nt(cot[...], wout[j * 1024 + i * 128:j * 1024 + (i + 1) * 128, :])
                .reshape(32, 8, 128)
                for j in range(2)
            )
            gsend[:, :, i * 128:(i + 1) * 128] = jnp.concatenate(
                [upper, lower], axis=1).astype(BF16)

    @pl.when(role != LEARNER)
    def _():
        fetches[2].wait()

    @pl.when(holder)
    def _():
        settle(idrecv.at[0:31], idg_r)
        got = idrecv[...].astype(F32)
        got = jnp.concatenate([
            jnp.broadcast_to(got[:, :, 0:1], (32, 16, 128)),
            jnp.broadcast_to(got[:, :, 64:65], (32, 16, 128))], axis=1).reshape(1024, 128)
        lane = lax.broadcasted_iota(jnp.int32, (1024, 128), 1) + 128 * (my_unit & 1)
        chosen = jnp.where(got == lane.astype(F32), 1.0, 0.0).astype(BF16)
        settle(trecv, ts_r)

        def add(k, total):
            return total + trecv[k].astype(F32)
        total = lax.fori_loop(0, 31, add, tsend[my_unit].astype(F32))
        whole = total.astype(BF16)
        selsend[...] = nn(chosen, whole).astype(BF16).reshape(32, 32, 128)

        def send_rows(k, p, h, u):
            put(selsend.at[p], selrecv.at[my_unit], sel_s, sel_r, role, p)
        each_peer(send_rows)
        selrecv[my_unit] = selsend[shard]

    @pl.when(role == LEARNER)
    def _():
        each_peer(lambda k, p, h, u: put(gsend.at[p], grecv.at[k - 1], gs_s, gs_r, role, p))
        for q in range(3):
            put(cot_hbm, cot, cot_s.at[q], cot_r, q, shard)
    send_ids(False)

    @pl.when(holder)
    def _():
        settle(selrecv.at[0:23], sel_r)

    @pl.when(jnp.logical_not(holder))
    def _():
        settle(idrecv.at[0:31], idg_r)
        settle(selrecv, sel_r)

    blocks = [selrecv[2 * c].astype(F32) + selrecv[2 * c + 1].astype(F32) for c in range(12)]
    for q in range(4):
        for i in range(6):
            pair = jnp.concatenate(
                [blocks[i][8 * q:8 * q + 8], blocks[6 + i][8 * q:8 * q + 8]], axis=0)
            xsend[q, :, i * 128:(i + 1) * 128] = pair.astype(BF16)
    for q in range(1, 4):
        to = others[q]
        put(xsend.at[to], xrecv.at[role], x_s.at[q - 1], x_r.at[q - 1], to, shard)
    xrecv[role] = xsend[role]

    fetches[4].wait()
    fetches[5].wait()
    for q in range(1, 4):
        settle(xrecv.at[0], x_r.at[q - 1])

    pieces = [xrecv[q].astype(F32) for q in range(4)]

    def tile(c):
        block, i = divmod(c, 12)
        return pieces[block][8 * (i // 6):8 * (i // 6) + 8, (i % 6) * 128:(i % 6 + 1) * 128]

    def stack(tiles):
        return jnp.concatenate(tiles, axis=0)

    q_tiles = [tile(h) for h in range(16)]
    q_all = stack(q_tiles).astype(BF16)
    k_new = stack([tile(16 + h) for h in range(16)]).astype(BF16)
    v_new = stack([tile(32 + h) for h in range(16)]).astype(BF16)

    def head(ref, h):
        return ref[:, h * 128:(h + 1) * 128]

    s1 = stack([nt(q_tiles[h].astype(BF16), head(keys, h)) for h in range(16)]) * scale
    s2 = nt(q_all, k_new) * scale
    ri = lax.broadcasted_iota(jnp.int32, (128, 128), 0)
    ci = lax.broadcasted_iota(jnp.int32, (128, 128), 1)
    allowed = (ri // 8 == ci // 8) & (ci % 8 <= ri % 8) & (ci % 8 < length)
    s2 = jnp.where(allowed, s2, -1e30)
    top = jnp.maximum(jnp.max(s1, axis=1, keepdims=True), jnp.max(s2, axis=1, keepdims=True))
    e1, e2 = jnp.exp(s1 - top), jnp.exp(s2 - top)
    den = jnp.sum(e1, axis=1, keepdims=True) + jnp.sum(e2, axis=1, keepdims=True)
    w1, w2 = e1 / den, e2 / den
    r2 = w2.astype(BF16)
    o2 = nn(r2, v_new)
    out_tiles = [
        nn(w1[8 * h:8 * h + 8].astype(BF16), head(vals, h)) + o2[8 * h:8 * h + 8]
        for h in range(16)
    ]
    for i in range(8):
        hrs[:, i * 128:(i + 1) * 128] = stack([out_tiles[i], out_tiles[8 + i]]).astype(BF16)

    @pl.when(role == LEARNER)
    def _():
        live_out = [jnp.where(live8, t, 0.0) for t in out_tiles]
        for q in range(4):
            for i in range(2):
                hsend[q, :, i * 128:(i + 1) * 128] = stack(
                    [live_out[4 * q + i], live_out[4 * q + 2 + i]]).astype(BF16)
        for q in range(3):
            put(hsend.at[q], hmsg, hrel_s.at[q], hrel_r, q, shard)
        hmsg[...] = hsend[3]

    @pl.when(role != LEARNER)
    def _():
        settle(hmsg, hrel_r)
    def shard_at(py, px, pz):
        return rows_at[py] + cols_at[px] + zs[pz]

    class Gather:
        def __init__(self, msg, buf, send, recv, count):
            self.msg, self.buf, self.send, self.recv, self.count = msg, buf, send, recv, count

        def lanes(self, half):
            width = self.msg.shape[1] // 2
            return pl.ds(half * width, width)

        def hop(self, step, half, src, dst, dy, dx, dz):
            put(src, dst, self.send.at[half], self.recv.at[half, step], role,
                shard_at(dy, dx, dz))

        def arrived(self, half, step, blocks):
            settle(self.count.at[0:blocks], self.recv.at[half, step])

        def start(self, far):
            self.buf[y, x, zl] = self.msg[...]
            for half in range(2):
                n = self.lanes(half)
                spots = [(0, 1), (1, 0), (3, 0), (1, 1), (3, 1)] + far
                for d, dz in spots:
                    self.hop(0, half, self.msg.at[:, n], self.buf.at[y, x, zl, :, n],
                             d * half, d * (1 - half), dz)

        def line(self, half):
            n = self.lanes(half)
            return self.buf.at[:, x, :, :, n] if half else self.buf.at[y, :, :, :, n]

        def sent(self):
            for half in range(2):
                settle(self.count.at[0:31], self.send.at[half])

    class Short(Gather):
        def first(self):
            self.start([(2, 0), (2, 1)])

        def second(self):
            for half in range(2):
                self.arrived(half, 0, 7)
                for d in (2, 1, 3):
                    self.hop(1, half, self.line(half), self.line(half),
                             d * (1 - half), d * half, 0)

        def last(self):
            for half in range(2):
                self.arrived(half, 1, 24)

    class Long(Gather):
        def first(self):
            self.start([])

        def second(self):
            for half in range(2):
                self.arrived(half, 0, 5)
                n = self.lanes(half)
                dy, dx = half, 1 - half
                before = self.buf.at[ys[3 * dy], xs[3 * dx], zl, :, n]
                after = self.buf.at[ys[dy], xs[dx], 1 - zl, :, n]
                self.hop(1, half, before, before, dy, dx, 0)
                self.hop(1, half, after, after, 3 * dy, 3 * dx, 0)

        def third(self):
            for half in range(2):
                self.arrived(half, 1, 2)
                for d in (1, 3):
                    self.hop(2, half, self.line(half), self.line(half),
                             d * (1 - half), d * half, 0)

        def fourth(self):
            for half in range(2):
                self.arrived(half, 2, 16)
                n = self.lanes(half)
                if half:
                    before = self.buf.at[0:2, xs[3], :, :, n]
                    after = self.buf.at[2:4, xs[1], :, :, n]
                else:
                    before = self.buf.at[ys[3], 0:2, :, :, n]
                    after = self.buf.at[ys[1], 2:4, :, :, n]
                self.hop(3, half, before, before, 1 - half, half, 0)
                self.hop(3, half, after, after, 3 * (1 - half), 3 * half, 0)

        def last(self):
            for half in range(2):
                self.arrived(half, 3, 8)

    mixes = Long(hrs, hrrecv, hr_s, hr_r, count_mix)
    heads = Short(hmsg, hgrecv, hg_s, hg_r, idrecv)
    grads_a = Short(rmsg_a, agrecv_a, aga_s, aga_r, idrecv)
    grads_b = Short(rmsg_b, agrecv_b, agb_s, agb_r, count_grad)

    heads.first()

    @pl.when(role != LEARNER)
    def _():
        mixes.first()

    @pl.when(role == LEARNER)
    def _():
        settle(grecv, gs_r)
        g_tiles = [None] * 16
        for i in range(8):
            cols = slice(i * 128, (i + 1) * 128)
            total = gsend[shard, :, cols].astype(F32)
            for k in range(31):
                total += grecv[k, :, cols].astype(F32)
            g_tiles[i] = jnp.where(live8, total[0:8], 0.0)
            g_tiles[8 + i] = jnp.where(live8, total[8:16], 0.0)
        g_all = stack(g_tiles).astype(BF16)
        gw1 = stack([nt(g_tiles[h].astype(BF16), head(vals, h)) for h in range(16)])
        gw2 = nt(g_all, v_new)
        dots = jnp.sum(w1 * gw1, axis=1, keepdims=True) + jnp.sum(w2 * gw2, axis=1, keepdims=True)
        gs1 = w1 * (gw1 - dots) * scale
        gs2 = (w2 * (gw2 - dots) * scale).astype(BF16)
        gq2 = nn(gs2, k_new)
        gk = tn(gs2, q_all)
        gv = tn(r2, g_all)
        gp = [
            nn(gs1[8 * h:8 * h + 8].astype(BF16), head(keys, h)) + gq2[8 * h:8 * h + 8]
            for h in range(16)
        ]
        gp += [gk[8 * h:8 * h + 8] for h in range(16)]
        gp += [gv[8 * h:8 * h + 8] for h in range(16)]
        for q in range(4):
            for i in range(6):
                pair = stack([gp[12 * q + i], gp[12 * q + 6 + i]]).astype(BF16)
                if i < 2:
                    rsend_a[q, :, i * 128:(i + 1) * 128] = pair
                else:
                    rsend_b[q, :, (i - 2) * 128:(i - 1) * 128] = pair
        for q in range(3):
            put(rsend_a.at[q], rmsg_a, rela_s.at[q], rela_r, q, shard)
        for q in range(3):
            put(rsend_b.at[q], rmsg_b, relb_s.at[q], relb_r, q, shard)
        rmsg_a[...] = rsend_a[3]
        rmsg_b[...] = rsend_b[3]

    copies = []

    def copy_out(a, b):
        pltpu.make_async_copy(a, b, out_sem.at[len(copies)]).start()
        copies.append(a)

    def spread(src, dst, n):
        put(src, dst, e_s.at[1, n], e_r.at[1, n], across, shard)
        put(src, dst, e_s.at[0, n], e_r.at[0, n], sibling, shard)
        copy_out(src, dst)

    def q_cols(of, n):
        at, width = CHUNKS[n]
        return nq_out.at[:, pl.ds(pl.multiple_of(of * 1536 + at, 128), width)]

    def o_rows(of):
        return no_out.at[pl.ds(pl.multiple_of(of * 512, 128), 512), :]

    half = (lax.broadcasted_iota(jnp.int32, (512, 128), 0) // 8) % 2

    def update_out():
        copies.clear()
        fetches[8].wait()
        fetches[9].wait()
        cot_wide = jnp.broadcast_to(
            cot[...].astype(F32).reshape(32, 1, 8, 128), (32, 2, 8, 128)).reshape(512, 128)
        cot_both = jnp.concatenate(
            [jnp.where(half == j, cot_wide, 0.0).astype(BF16) for j in range(2)], axis=1)
        heads.last()
        grad_out = tn(hgrecv[...].reshape(512, 256), cot_both)
        for j in range(2):
            here = slice(j * 256, (j + 1) * 256)
            params = wout[pl.ds(pl.multiple_of(row0 + j * 256, 128), 256), :]
            new, one, two = adamw(
                params, grad_out[:, j * 128:(j + 1) * 128], m_o[here, :], v_o[here, :])
            no[here, :] = new.astype(BF16)
            m_o[here, :] = one
            v_o[here, :] = two
        spread(no, o_rows(role), N_CHUNK)
        copy_out(m_o, mo_out)
        copy_out(v_o, so_out)

    @pl.when(role != LEARNER)
    def _():
        settle(rmsg_a, rela_r)
    grads_a.first()

    @pl.when(role != LEARNER)
    def _():
        settle(rmsg_b, relb_r)
    grads_b.first()
    heads.second()
    grads_a.second()
    grads_b.second()

    @pl.when(role == LEARNER)
    def _():
        mixes.first()

    @pl.when(role != LEARNER)
    def _():
        settle(cot, cot_r)
    mixes.second()
    update_out()

    got_ids = idrecv[...].astype(F32)[:, 8:16, 64:65]
    got_ids = jnp.broadcast_to(
        jnp.concatenate([got_ids, got_ids], axis=1), (32, 16, 128)).reshape(512, 128)
    lane = lax.broadcasted_iota(jnp.int32, (512, 128), 1).astype(F32)
    low = jnp.where(got_ids == lane, 1.0, 0.0).astype(BF16)
    high = jnp.where(got_ids == lane + 128.0, 1.0, 0.0).astype(BF16)
    rows = nn(low, table[0:128, :]) + nn(high, table[128:256, :])
    halves = [jnp.where(half == j, rows, 0.0).T.astype(BF16) for j in range(2)]
    fetches[6].wait()
    fetches[7].wait()
    for n, (at, width) in enumerate(CHUNKS):
        cols = slice(at, at + width)
        if n == 0:
            grads_a.last()
        if n == 2:
            mixes.third()
            grads_b.last()
        buf = agrecv_b if n >= 2 else agrecv_a
        grad = nn(halves[n % 2], buf[...].reshape(512, width))
        new, one, two = adamw(wq[:, cols], grad, m_q[:, cols], v_q[:, cols])
        nq[:, cols] = new.astype(BF16)
        m_q[:, cols] = one
        v_q[:, cols] = two
        spread(nq.at[:, cols], q_cols(role, n), n)
    copy_out(m_q, mq_out)
    copy_out(v_q, sq_out)
    mixes.fourth()

    def part(of, n):
        return q_cols(of, n) if n < N_CHUNK else o_rows(of)

    for n in (N_CHUNK, *range(N_CHUNK)):
        settle(part(across, n), e_r.at[1, n])
        put(part(across, n), part(across, n), e_s.at[2, n], e_r.at[2, n], sibling, shard)

    mixes.last()
    mix = hrrecv[...].reshape(512, 1024)
    upper = nn(mix, wout[0:1024, :]).reshape(32, 2, 8, 128)
    lower = nn(mix, wout[1024:2048, :]).reshape(32, 2, 8, 128)
    dec[...] = (upper[:, 0] + lower[:, 1]).reshape(256, 128).astype(BF16)
    copy_out(dec, dec_out)

    for n in range(N_CHUNK + 1):
        settle(part(sibling, n), e_r.at[0, n])
        settle(part((1 - z_hi) * 2 + (1 - core), n), e_r.at[2, n])
        for way in range(3):
            settle(part(role, n), e_s.at[way, n])
    for i, a in enumerate(copies):
        settle(a, out_sem.at[i])
    for q in range(3):
        settle(idx4.at[0], id_s.at[q])
        settle(xsend.at[0], x_s.at[q])

    @pl.when(holder)
    def _():
        settle(tsend.at[0:23], ts_s)
        settle(selsend.at[0:31], sel_s)

    @pl.when(jnp.logical_not(holder))
    def _():
        settle(tsend, ts_s)

    @pl.when(role == LEARNER)
    def _():
        for q in range(3):
            settle(cot, cot_s.at[q])
            settle(rmsg_a, rela_s.at[q])
            settle(rmsg_b, relb_s.at[q])
            settle(hmsg, hrel_s.at[q])
        settle(gsend.at[0:31], gs_s)
    settle(idrecv.at[0:31], idg_s)
    heads.sent()
    grads_a.sent()
    grads_b.sent()
    mixes.sent()


SHAPES = (
    ((256, 128), BF16), ((128, 6144), BF16), ((2048, 128), BF16),
    ((128, 1536), F32), ((128, 1536), F32), ((512, 128), F32), ((512, 128), F32),
)


def hand_over(*refs):
    ins, outs, stage, sems = refs[:7], refs[7:14], refs[14:21], refs[21]
    moves = []
    for a, v, b in zip(ins, stage, outs):
        pieces = 4 if a.shape == (128, 6144) else 2 if a.shape[0] * a.shape[1] > 131072 else 1
        rows = a.shape[0] // pieces
        for i in range(pieces):
            part, n = pl.ds(i * rows, rows), len(moves)
            moves.append((
                pltpu.make_async_copy(a.at[part, :], v.at[part, :], sems.at[0, n]),
                pltpu.make_async_copy(v.at[part, :], b.at[part, :], sems.at[1, n])))
    for m, _ in moves:
        m.start()
    for m, n in moves:
        m.wait()
        n.start()
    for _, n in moves:
        n.wait()


def shards(*args):
    any_ = pl.BlockSpec(memory_space=pl.ANY)
    smem = pl.BlockSpec(memory_space=pltpu.SMEM)
    dma, vm = pltpu.SemaphoreType.DMA, pltpu.VMEM
    done = pl.pallas_call(
        kernel,
        out_shape=tuple(jax.ShapeDtypeStruct(*a) for a in SHAPES),
        in_specs=[smem, smem] + [any_] * 10,
        out_specs=(any_,) * 7,
        scratch_shapes=[
            vm((256, 128), BF16),
            vm((128, 2048), BF16),
            vm((128, 2048), BF16),
            vm((128, 1536), BF16),
            vm((2048, 128), BF16),
            vm((128, 1536), F32),
            vm((128, 1536), F32),
            vm((512, 128), F32),
            vm((512, 128), F32),
            vm((256, 128), BF16),
            vm((24, 128, 128), BF16),
            vm((31, 128, 128), BF16),
            vm((32, 16, 1024), BF16),
            vm((31, 16, 1024), BF16),
            vm((4, 8, 128), F32),
            vm((16, 128), BF16),
            vm((32, 16, 128), BF16),
            vm((32, 32, 128), BF16),
            vm((24, 32, 128), BF16),
            vm((4, 16, 768), BF16),
            vm((4, 16, 768), BF16),
            vm((16, 1024), BF16),
            vm((4, 4, 2, 16, 1024), BF16),
            vm((4, 16, 256), BF16),
            vm((16, 256), BF16),
            vm((4, 4, 2, 16, 256), BF16),
            vm((4, 16, 256), BF16),
            vm((4, 16, 512), BF16),
            vm((16, 256), BF16),
            vm((16, 512), BF16),
            vm((4, 4, 2, 16, 256), BF16),
            vm((4, 4, 2, 16, 512), BF16),
            vm((31, 16, 512), BF16),
            vm((31, 16, 256), BF16),
            vm((128, 1536), BF16),
            vm((512, 128), BF16),
            vm((256, 128), BF16),
            dma((10,)),
            dma((N_CHUNK + 6,)),
            dma((3,)), dma((3,)),
            dma, dma,
            dma, dma,
            dma, dma,
            dma((3,)), dma,
            dma, dma,
            dma((3,)), dma((3,)),
            dma((3,)), dma,
            dma((3,)), dma,
            dma((3,)), dma,
            dma((2,)), dma((2, 2)),
            dma((2,)), dma((2, 2)),
            dma((2,)), dma((2, 2)),
            dma((2,)), dma((2, 4)),
            dma((3, N_CHUNK + 1)), dma((3, N_CHUNK + 1)),
        ],
        compiler_params=pltpu.CompilerParams(
            collective_id=0, has_side_effects=True, vmem_limit_bytes=60 * 1024 * 1024),
        name="policy_update",
    )(*args)
    return tuple(pl.pallas_call(
        hand_over,
        out_shape=tuple(jax.ShapeDtypeStruct(*a) for a in SHAPES),
        in_specs=[any_] * 7,
        out_specs=(any_,) * 7,
        scratch_shapes=[vm(*a) for a in SHAPES] + [dma((2, 16))],
        compiler_params=pltpu.CompilerParams(vmem_limit_bytes=60 * 1024 * 1024),
        name="hand_over",
    )(*done))


def solution(mesh):
    both = ("role", "shard")
    return jax.shard_map(
        shards,
        mesh=mesh,
        in_specs=(
            P(both, None), P(both), P(None, "shard"), P(both, None, None), P(both, None, None),
            P("shard", None), P(None, "shard"), P("shard", "role"), P("shard", "role"),
            P("role", "shard"), P("role", "shard"), P("role", "shard"),
        ),
        out_specs=(
            P("role", "shard"), P("shard", None), P(None, "shard"), P("shard", "role"),
            P("shard", "role"), P("role", "shard"), P("role", "shard"),
        ),
        check_vma=False,
    )
```

```python
import jax
import jax.numpy as jnp
from jax import lax
from jax.experimental import pallas as pl
from jax.experimental.pallas import tpu as pltpu
from jax.sharding import PartitionSpec as P

HD = 128
MESH = pl.DeviceIdType.MESH
F32 = jnp.float32
BF16 = jnp.bfloat16
LEARNER = 3

learn_rate = 0.001
first_decay = 0.9
second_decay = 0.95
adam_eps = 1e-08
weight_decay = 0.1
first_fix = 1.0 - 0.9**10
second_fix = 1.0 - 0.95**10
scale = HD ** (-0.5)

N_CHUNK = 4
CHUNKS = ((0, 256), (768, 256), (256, 512), (1024, 512))
MIDDLE = BF16
ORDER = 13


def adamw(params, gradient, first_moment, second_moment):
    moment_one = first_decay * first_moment + (1.0 - first_decay) * gradient
    moment_two = second_decay * second_moment + (1.0 - second_decay) * gradient * gradient
    stepped = moment_one / first_fix / (jnp.sqrt(moment_two / second_fix) + adam_eps)
    wide_params = params.astype(F32)
    updated = wide_params - learn_rate * (stepped + weight_decay * wide_params)
    return (updated, moment_one, moment_two)


def settle(ref, sem):
    pltpu.make_async_copy(ref, ref, sem).wait()


def nt(a, b):
    return lax.dot_general(a, b, (((1,), (1,)), ((), ())), preferred_element_type=F32)


def tn(a, b):
    return lax.dot_general(a, b, (((0,), (0,)), ((), ())), preferred_element_type=F32)


def nn(a, b):
    return jnp.dot(a, b, preferred_element_type=F32)


def kernel(
    ids_ref, len_ref, table_hbm, keys_hbm, vals_hbm, wqkv_hbm, wout_hbm,
    m_q_hbm, v_q_hbm, m_o_hbm, v_o_hbm, cot_hbm,
    dec_out, nq_out, no_out, mq_out, sq_out, mo_out, so_out,
    table, keys, vals, wq, wout, m_q, v_q, m_o, v_o, cot,
    tsend, line_in, line_sum, line_out, plane_in, gsend, grecv, idx4, idsend, idrecv, selsend, selrecv,
    xsend, xrecv, hrs, hrrecv, hsend, hmsg, hgrecv, rsend_a, rsend_b, rmsg_a, rmsg_b,
    agrecv_a, agrecv_b,
    count_mix, count_grad, nq, no, dec,
    loc, out_sem, id_s, id_r, idg_s, idg_r, ts_s, ts_r, tp_s, tp_r, gs_s, gs_r,
    cot_s, cot_r, sel_s, sel_r, x_s, x_r, hrel_s, hrel_r, rela_s, rela_r, relb_s, relb_r,
    hg_s, hg_r, aga_s, aga_r, agb_s, agb_r, hr_s, hr_r,
    e_s, e_r,
):
    role = lax.axis_index("role")
    shard = lax.axis_index("shard")
    y, x, zl = shard >> 3, (shard >> 1) & 3, shard & 1
    z_hi, core = role >> 1, role & 1
    sibling = z_hi * 2 + (1 - core)
    across = (1 - z_hi) * 2 + core
    others = [(role + q) & 3 for q in range(4)]

    ys = [(y + d) & 3 for d in range(4)]
    xs = [(x + d) & 3 for d in range(4)]
    zs = [zl, 1 - zl]
    spots = [(x + y + d) & 3 for d in range(4)]
    holds = [spot < 3 for spot in spots]
    rows_at = [v * 8 for v in ys]
    cols_at = [v * 2 for v in xs]
    unit_row = [v * 6 for v in ys]
    unit_col = [v * 2 for v in spots]

    def peer(k):
        dy, dx, dz = k >> 3, (k >> 1) & 3, k & 1
        turn = (dy + dx) & 3
        return (rows_at[dy] + cols_at[dx] + zs[dz], holds[turn],
                unit_row[dy] + unit_col[turn] + zs[dz])

    holder = holds[0]
    my_unit = jnp.where(holder, peer(0)[2], 0)

    def put(src, dst, send, recv, to_role, to_shard):
        pltpu.make_async_remote_copy(
            src_ref=src, dst_ref=dst, send_sem=send, recv_sem=recv,
            device_id=(to_role, to_shard), device_id_type=MESH,
        ).start()

    def each_peer(body, first=1, last=32):
        for j in range(first, last):
            k = j * ORDER % 32
            body(k, *peer(k))

    barrier = pltpu.get_barrier_semaphore()
    each_peer(lambda k, p, h, u: pl.semaphore_signal(
        barrier, inc=1, device_id=(role, p), device_id_type=MESH))
    for q in range(1, 4):
        pl.semaphore_signal(
            barrier, inc=1, device_id=(others[q], shard), device_id_type=MESH)

    col0 = pl.multiple_of(role * 1536, 128)
    row0 = pl.multiple_of(role * 512, 128)
    fetches = [
        pltpu.make_async_copy(a, b, loc.at[i])
        for i, (a, b) in enumerate((
            (table_hbm, table),
            (wqkv_hbm.at[:, pl.ds(col0, 1536)], wq),
            (wout_hbm, wout),
            (cot_hbm, cot),
            (keys_hbm.at[0], keys),
            (vals_hbm.at[0], vals),
            (m_q_hbm, m_q),
            (v_q_hbm, v_q),
            (m_o_hbm, m_o),
            (v_o_hbm, v_o),
        ))
    ]
    for i, f in enumerate(fetches):
        if i != 3:
            f.start()

    @pl.when(role == LEARNER)
    def _():
        fetches[3].start()

    row8 = lax.broadcasted_iota(jnp.int32, (8, 128), 0)
    lane8 = lax.broadcasted_iota(jnp.int32, (8, 128), 1)
    ids = jnp.zeros((8, 128), jnp.int32)
    for i in range(8):
        ids = jnp.where(row8 == i, ids_ref[0, i], ids)
    ids = ids.astype(F32)
    length = len_ref[0]
    live8 = row8 < length
    idx4[role] = ids

    fetches[0].wait()
    fetches[1].wait()
    for c in range(12):
        part = nn(table[...], wq[:, c * 128:(c + 1) * 128]).astype(BF16)
        for h in range(2):
            u = 2 * c + h
            row, spot, pz = u // 6, u % 6 // 2, u % 2
            tsend[0, u] = part[h * 128:h * 128 + 64]
            tsend[1, (spot - row) % 4 * 6 + spot * 2 + pz] = part[h * 128 + 64:h * 128 + 128]

    pl.semaphore_wait(barrier, 34)

    for q in range(1, 4):
        put(idx4.at[role], idx4.at[role], id_s.at[q - 1], id_r.at[q - 1], others[q], shard)

    for d in (2, 1, 3):
        put(tsend.at[0, pl.ds(ys[d] * 6, 6)], line_in.at[0, d - 1], ts_s.at[0], ts_r.at[0],
            role, rows_at[d] + cols_at[0] + zs[0])
        put(tsend.at[1, pl.ds(xs[d] * 6, 6)], line_in.at[1, d - 1], ts_s.at[1], ts_r.at[1],
            role, rows_at[0] + cols_at[d] + zs[0])

    for q in range(1, 4):
        settle(idx4.at[0], id_r.at[q - 1])
    lane16 = lax.broadcasted_iota(jnp.int32, (16, 128), 1)
    all_ids = jnp.where(
        lane16 < 64,
        jnp.concatenate([idx4[0], idx4[1]], axis=0),
        jnp.concatenate([idx4[2], idx4[3]], axis=0)).astype(BF16)
    idsend[...] = all_ids
    idrecv[shard] = all_ids

    def send_ids(now):
        def body(k, p, h, u):
            @pl.when(h if now else jnp.logical_not(h))
            def _():
                put(idsend, idrecv.at[shard], idg_s, idg_r, role, p)
        each_peer(body)
    send_ids(True)

    for half in range(2):
        settle(line_in.at[half], ts_r.at[half])
        total = tsend[half, pl.ds((xs[0] if half else ys[0]) * 6, 6)].astype(F32)
        for d in range(3):
            total += line_in[half, d].astype(F32)
        line_sum[half] = total
        line_out[half] = total.astype(line_out.dtype)
        for d, dz in ((2, 0), (2, 1), (1, 1), (3, 1), (1, 0), (3, 0), (0, 1)):
            @pl.when(holds[d])
            def _():
                put(line_out.at[half, spots[d] * 2 + zs[dz]], plane_in.at[half, d * 2 + dz - 1],
                    tp_s.at[half], tp_r.at[half], role,
                    (rows_at[d] + cols_at[0] if half else rows_at[0] + cols_at[d]) + zs[dz])

    @pl.when(role == LEARNER)
    def _():
        fetches[2].wait()
        fetches[3].wait()
        for i in range(8):
            upper, lower = (
                nt(cot[...], wout[j * 1024 + i * 128:j * 1024 + (i + 1) * 128, :])
                .reshape(32, 8, 128)
                for j in range(2)
            )
            gsend[:, :, i * 128:(i + 1) * 128] = jnp.concatenate(
                [upper, lower], axis=1).astype(BF16)

    @pl.when(role != LEARNER)
    def _():
        fetches[2].wait()

    @pl.when(holder)
    def _():
        settle(idrecv.at[0:31], idg_r)
        got = idrecv[...].astype(F32)
        got = jnp.concatenate([
            jnp.broadcast_to(got[:, :, 0:1], (32, 16, 128)),
            jnp.broadcast_to(got[:, :, 64:65], (32, 16, 128))], axis=1).reshape(1024, 128)
        lane = lax.broadcasted_iota(jnp.int32, (1024, 128), 1) + 128 * (my_unit & 1)
        chosen = jnp.where(got == lane.astype(F32), 1.0, 0.0).astype(BF16)
        parts = []
        for half in range(2):
            settle(plane_in.at[half], tp_r.at[half])
            total = line_sum[half, spots[0] * 2 + zl]
            for k in range(7):
                total += plane_in[half, k].astype(F32)
            parts.append(total)
        whole = jnp.concatenate(parts, axis=0).astype(BF16)
        selsend[...] = nn(chosen, whole).astype(BF16).reshape(32, 32, 128)

        def send_rows(k, p, h, u):
            put(selsend.at[p], selrecv.at[my_unit], sel_s, sel_r, role, p)
        each_peer(send_rows)
        selrecv[my_unit] = selsend[shard]

    @pl.when(role == LEARNER)
    def _():
        each_peer(lambda k, p, h, u: put(gsend.at[p], grecv.at[k - 1], gs_s, gs_r, role, p))
        for q in range(3):
            put(cot_hbm, cot, cot_s.at[q], cot_r, q, shard)
    send_ids(False)

    @pl.when(holder)
    def _():
        settle(selrecv.at[0:23], sel_r)

    @pl.when(jnp.logical_not(holder))
    def _():
        settle(idrecv.at[0:31], idg_r)
        settle(selrecv, sel_r)

    blocks = [selrecv[2 * c].astype(F32) + selrecv[2 * c + 1].astype(F32) for c in range(12)]
    for q in range(4):
        for i in range(6):
            pair = jnp.concatenate(
                [blocks[i][8 * q:8 * q + 8], blocks[6 + i][8 * q:8 * q + 8]], axis=0)
            xsend[q, :, i * 128:(i + 1) * 128] = pair.astype(BF16)
    for q in range(1, 4):
        to = others[q]
        put(xsend.at[to], xrecv.at[role], x_s.at[q - 1], x_r.at[q - 1], to, shard)
    xrecv[role] = xsend[role]

    fetches[4].wait()
    fetches[5].wait()
    for q in range(1, 4):
        settle(xrecv.at[0], x_r.at[q - 1])

    pieces = [xrecv[q].astype(F32) for q in range(4)]

    def tile(c):
        block, i = divmod(c, 12)
        return pieces[block][8 * (i // 6):8 * (i // 6) + 8, (i % 6) * 128:(i % 6 + 1) * 128]

    def stack(tiles):
        return jnp.concatenate(tiles, axis=0)

    q_tiles = [tile(h) for h in range(16)]
    q_all = stack(q_tiles).astype(BF16)
    k_new = stack([tile(16 + h) for h in range(16)]).astype(BF16)
    v_new = stack([tile(32 + h) for h in range(16)]).astype(BF16)

    def head(ref, h):
        return ref[:, h * 128:(h + 1) * 128]

    s1 = stack([nt(q_tiles[h].astype(BF16), head(keys, h)) for h in range(16)]) * scale
    s2 = nt(q_all, k_new) * scale
    ri = lax.broadcasted_iota(jnp.int32, (128, 128), 0)
    ci = lax.broadcasted_iota(jnp.int32, (128, 128), 1)
    allowed = (ri // 8 == ci // 8) & (ci % 8 <= ri % 8) & (ci % 8 < length)
    s2 = jnp.where(allowed, s2, -1e30)
    top = jnp.maximum(jnp.max(s1, axis=1, keepdims=True), jnp.max(s2, axis=1, keepdims=True))
    e1, e2 = jnp.exp(s1 - top), jnp.exp(s2 - top)
    den = jnp.sum(e1, axis=1, keepdims=True) + jnp.sum(e2, axis=1, keepdims=True)
    w1, w2 = e1 / den, e2 / den
    r2 = w2.astype(BF16)
    o2 = nn(r2, v_new)
    out_tiles = [
        nn(w1[8 * h:8 * h + 8].astype(BF16), head(vals, h)) + o2[8 * h:8 * h + 8]
        for h in range(16)
    ]
    for i in range(8):
        hrs[:, i * 128:(i + 1) * 128] = stack([out_tiles[i], out_tiles[8 + i]]).astype(BF16)

    @pl.when(role == LEARNER)
    def _():
        live_out = [jnp.where(live8, t, 0.0) for t in out_tiles]
        for q in range(4):
            for i in range(2):
                hsend[q, :, i * 128:(i + 1) * 128] = stack(
                    [live_out[4 * q + i], live_out[4 * q + 2 + i]]).astype(BF16)
        for q in range(3):
            put(hsend.at[q], hmsg, hrel_s.at[q], hrel_r, q, shard)
        hmsg[...] = hsend[3]

    @pl.when(role != LEARNER)
    def _():
        settle(hmsg, hrel_r)
    def shard_at(py, px, pz):
        return rows_at[py] + cols_at[px] + zs[pz]

    class Gather:
        def __init__(self, msg, buf, send, recv, count):
            self.msg, self.buf, self.send, self.recv, self.count = msg, buf, send, recv, count

        def lanes(self, half):
            width = self.msg.shape[1] // 2
            return pl.ds(half * width, width)

        def hop(self, step, half, src, dst, dy, dx, dz):
            put(src, dst, self.send.at[half], self.recv.at[half, step], role,
                shard_at(dy, dx, dz))

        def arrived(self, half, step, blocks):
            settle(self.count.at[0:blocks], self.recv.at[half, step])

        def start(self, far):
            self.buf[y, x, zl] = self.msg[...]
            for half in range(2):
                n = self.lanes(half)
                spots = [(0, 1), (1, 0), (3, 0), (1, 1), (3, 1)] + far
                for d, dz in spots:
                    self.hop(0, half, self.msg.at[:, n], self.buf.at[y, x, zl, :, n],
                             d * half, d * (1 - half), dz)

        def line(self, half):
            n = self.lanes(half)
            return self.buf.at[:, x, :, :, n] if half else self.buf.at[y, :, :, :, n]

        def sent(self):
            for half in range(2):
                settle(self.count.at[0:31], self.send.at[half])

    class Short(Gather):
        def first(self):
            self.start([(2, 0), (2, 1)])

        def second(self):
            for half in range(2):
                self.arrived(half, 0, 7)
                for d in (2, 1, 3):
                    self.hop(1, half, self.line(half), self.line(half),
                             d * (1 - half), d * half, 0)

        def last(self):
            for half in range(2):
                self.arrived(half, 1, 24)

    class Long(Gather):
        def first(self):
            self.start([])

        def second(self):
            for half in range(2):
                self.arrived(half, 0, 5)
                n = self.lanes(half)
                dy, dx = half, 1 - half
                before = self.buf.at[ys[3 * dy], xs[3 * dx], zl, :, n]
                after = self.buf.at[ys[dy], xs[dx], 1 - zl, :, n]
                self.hop(1, half, before, before, dy, dx, 0)
                self.hop(1, half, after, after, 3 * dy, 3 * dx, 0)

        def third(self):
            for half in range(2):
                self.arrived(half, 1, 2)
                for d in (1, 3):
                    self.hop(2, half, self.line(half), self.line(half),
                             d * (1 - half), d * half, 0)

        def fourth(self):
            for half in range(2):
                self.arrived(half, 2, 16)
                n = self.lanes(half)
                if half:
                    before = self.buf.at[0:2, xs[3], :, :, n]
                    after = self.buf.at[2:4, xs[1], :, :, n]
                else:
                    before = self.buf.at[ys[3], 0:2, :, :, n]
                    after = self.buf.at[ys[1], 2:4, :, :, n]
                self.hop(3, half, before, before, 1 - half, half, 0)
                self.hop(3, half, after, after, 3 * (1 - half), 3 * half, 0)

        def last(self):
            for half in range(2):
                self.arrived(half, 3, 8)

    mixes = Long(hrs, hrrecv, hr_s, hr_r, count_mix)
    heads = Short(hmsg, hgrecv, hg_s, hg_r, idrecv)
    grads_a = Short(rmsg_a, agrecv_a, aga_s, aga_r, idrecv)
    grads_b = Short(rmsg_b, agrecv_b, agb_s, agb_r, count_grad)

    heads.first()

    @pl.when(role != LEARNER)
    def _():
        mixes.first()

    @pl.when(role == LEARNER)
    def _():
        settle(grecv, gs_r)
        g_tiles = [None] * 16
        for i in range(8):
            cols = slice(i * 128, (i + 1) * 128)
            total = gsend[shard, :, cols].astype(F32)
            for k in range(31):
                total += grecv[k, :, cols].astype(F32)
            g_tiles[i] = jnp.where(live8, total[0:8], 0.0)
            g_tiles[8 + i] = jnp.where(live8, total[8:16], 0.0)
        g_all = stack(g_tiles).astype(BF16)
        gw1 = stack([nt(g_tiles[h].astype(BF16), head(vals, h)) for h in range(16)])
        gw2 = nt(g_all, v_new)
        dots = jnp.sum(w1 * gw1, axis=1, keepdims=True) + jnp.sum(w2 * gw2, axis=1, keepdims=True)
        gs1 = w1 * (gw1 - dots) * scale
        gs2 = (w2 * (gw2 - dots) * scale).astype(BF16)
        gq2 = nn(gs2, k_new)
        gk = tn(gs2, q_all)
        gv = tn(r2, g_all)
        gp = [
            nn(gs1[8 * h:8 * h + 8].astype(BF16), head(keys, h)) + gq2[8 * h:8 * h + 8]
            for h in range(16)
        ]
        gp += [gk[8 * h:8 * h + 8] for h in range(16)]
        gp += [gv[8 * h:8 * h + 8] for h in range(16)]
        for q in range(4):
            for i in range(6):
                pair = stack([gp[12 * q + i], gp[12 * q + 6 + i]]).astype(BF16)
                if i < 2:
                    rsend_a[q, :, i * 128:(i + 1) * 128] = pair
                else:
                    rsend_b[q, :, (i - 2) * 128:(i - 1) * 128] = pair
        for q in range(3):
            put(rsend_a.at[q], rmsg_a, rela_s.at[q], rela_r, q, shard)
        for q in range(3):
            put(rsend_b.at[q], rmsg_b, relb_s.at[q], relb_r, q, shard)
        rmsg_a[...] = rsend_a[3]
        rmsg_b[...] = rsend_b[3]

    copies = []

    def copy_out(a, b):
        pltpu.make_async_copy(a, b, out_sem.at[len(copies)]).start()
        copies.append(a)

    def spread(src, dst, n):
        put(src, dst, e_s.at[1, n], e_r.at[1, n], across, shard)
        put(src, dst, e_s.at[0, n], e_r.at[0, n], sibling, shard)
        copy_out(src, dst)

    def q_cols(of, n):
        at, width = CHUNKS[n]
        return nq_out.at[:, pl.ds(pl.multiple_of(of * 1536 + at, 128), width)]

    def o_rows(of):
        return no_out.at[pl.ds(pl.multiple_of(of * 512, 128), 512), :]

    half = (lax.broadcasted_iota(jnp.int32, (512, 128), 0) // 8) % 2

    def update_out():
        copies.clear()
        fetches[8].wait()
        fetches[9].wait()
        cot_wide = jnp.broadcast_to(
            cot[...].astype(F32).reshape(32, 1, 8, 128), (32, 2, 8, 128)).reshape(512, 128)
        cot_both = jnp.concatenate(
            [jnp.where(half == j, cot_wide, 0.0).astype(BF16) for j in range(2)], axis=1)
        heads.last()
        grad_out = tn(hgrecv[...].reshape(512, 256), cot_both)
        for j in range(2):
            here = slice(j * 256, (j + 1) * 256)
            params = wout[pl.ds(pl.multiple_of(row0 + j * 256, 128), 256), :]
            new, one, two = adamw(
                params, grad_out[:, j * 128:(j + 1) * 128], m_o[here, :], v_o[here, :])
            no[here, :] = new.astype(BF16)
            m_o[here, :] = one
            v_o[here, :] = two
        spread(no, o_rows(role), N_CHUNK)
        copy_out(m_o, mo_out)
        copy_out(v_o, so_out)

    @pl.when(role != LEARNER)
    def _():
        settle(rmsg_a, rela_r)
    grads_a.first()

    @pl.when(role != LEARNER)
    def _():
        settle(rmsg_b, relb_r)
    grads_b.first()
    heads.second()
    grads_a.second()
    grads_b.second()

    @pl.when(role == LEARNER)
    def _():
        mixes.first()

    @pl.when(role != LEARNER)
    def _():
        settle(cot, cot_r)
    mixes.second()
    update_out()

    got_ids = idrecv[...].astype(F32)[:, 8:16, 64:65]
    got_ids = jnp.broadcast_to(
        jnp.concatenate([got_ids, got_ids], axis=1), (32, 16, 128)).reshape(512, 128)
    lane = lax.broadcasted_iota(jnp.int32, (512, 128), 1).astype(F32)
    low = jnp.where(got_ids == lane, 1.0, 0.0).astype(BF16)
    high = jnp.where(got_ids == lane + 128.0, 1.0, 0.0).astype(BF16)
    rows = nn(low, table[0:128, :]) + nn(high, table[128:256, :])
    halves = [jnp.where(half == j, rows, 0.0).T.astype(BF16) for j in range(2)]
    fetches[6].wait()
    fetches[7].wait()
    for n, (at, width) in enumerate(CHUNKS):
        cols = slice(at, at + width)
        if n == 0:
            grads_a.last()
        if n == 2:
            mixes.third()
            grads_b.last()
        buf = agrecv_b if n >= 2 else agrecv_a
        grad = nn(halves[n % 2], buf[...].reshape(512, width))
        new, one, two = adamw(wq[:, cols], grad, m_q[:, cols], v_q[:, cols])
        nq[:, cols] = new.astype(BF16)
        m_q[:, cols] = one
        v_q[:, cols] = two
        spread(nq.at[:, cols], q_cols(role, n), n)
    copy_out(m_q, mq_out)
    copy_out(v_q, sq_out)
    mixes.fourth()

    def part(of, n):
        return q_cols(of, n) if n < N_CHUNK else o_rows(of)

    for n in (N_CHUNK, *range(N_CHUNK)):
        settle(part(across, n), e_r.at[1, n])
        put(part(across, n), part(across, n), e_s.at[2, n], e_r.at[2, n], sibling, shard)

    mixes.last()
    mix = hrrecv[...].reshape(512, 1024)
    upper = nn(mix, wout[0:1024, :]).reshape(32, 2, 8, 128)
    lower = nn(mix, wout[1024:2048, :]).reshape(32, 2, 8, 128)
    dec[...] = (upper[:, 0] + lower[:, 1]).reshape(256, 128).astype(BF16)
    copy_out(dec, dec_out)

    for n in range(N_CHUNK + 1):
        settle(part(sibling, n), e_r.at[0, n])
        settle(part((1 - z_hi) * 2 + (1 - core), n), e_r.at[2, n])
        for way in range(3):
            settle(part(role, n), e_s.at[way, n])
    for i, a in enumerate(copies):
        settle(a, out_sem.at[i])
    for q in range(3):
        settle(idx4.at[0], id_s.at[q])
        settle(xsend.at[0], x_s.at[q])

    @pl.when(holder)
    def _():
        for half in range(2):
            settle(plane_in.at[half, 0:5], tp_s.at[half])
        settle(selsend.at[0:31], sel_s)

    @pl.when(jnp.logical_not(holder))
    def _():
        for half in range(2):
            settle(plane_in.at[half, 0:6], tp_s.at[half])

    @pl.when(role == LEARNER)
    def _():
        for q in range(3):
            settle(cot, cot_s.at[q])
            settle(rmsg_a, rela_s.at[q])
            settle(rmsg_b, relb_s.at[q])
            settle(hmsg, hrel_s.at[q])
        settle(gsend.at[0:31], gs_s)
    settle(idrecv.at[0:31], idg_s)
    for half in range(2):
        settle(line_in.at[half], ts_s.at[half])
    heads.sent()
    grads_a.sent()
    grads_b.sent()
    mixes.sent()


SHAPES = (
    ((256, 128), BF16), ((128, 6144), BF16), ((2048, 128), BF16),
    ((128, 1536), F32), ((128, 1536), F32), ((512, 128), F32), ((512, 128), F32),
)


def hand_over(*refs):
    ins, outs, stage, sems = refs[:7], refs[7:14], refs[14:21], refs[21]
    moves = []
    for a, v, b in zip(ins, stage, outs):
        pieces = 4 if a.shape == (128, 6144) else 2 if a.shape[0] * a.shape[1] > 131072 else 1
        rows = a.shape[0] // pieces
        for i in range(pieces):
            part, n = pl.ds(i * rows, rows), len(moves)
            moves.append((
                pltpu.make_async_copy(a.at[part, :], v.at[part, :], sems.at[0, n]),
                pltpu.make_async_copy(v.at[part, :], b.at[part, :], sems.at[1, n])))
    for m, _ in moves:
        m.start()
    for m, n in moves:
        m.wait()
        n.start()
    for _, n in moves:
        n.wait()


def shards(*args):
    any_ = pl.BlockSpec(memory_space=pl.ANY)
    smem = pl.BlockSpec(memory_space=pltpu.SMEM)
    dma, vm = pltpu.SemaphoreType.DMA, pltpu.VMEM
    done = pl.pallas_call(
        kernel,
        out_shape=tuple(jax.ShapeDtypeStruct(*a) for a in SHAPES),
        in_specs=[smem, smem] + [any_] * 10,
        out_specs=(any_,) * 7,
        scratch_shapes=[
            vm((256, 128), BF16),
            vm((128, 2048), BF16),
            vm((128, 2048), BF16),
            vm((128, 1536), BF16),
            vm((2048, 128), BF16),
            vm((128, 1536), F32),
            vm((128, 1536), F32),
            vm((512, 128), F32),
            vm((512, 128), F32),
            vm((256, 128), BF16),
            vm((2, 24, 64, 128), BF16),
            vm((2, 3, 6, 64, 128), BF16),
            vm((2, 6, 64, 128), F32),
            vm((2, 6, 64, 128), MIDDLE),
            vm((2, 7, 64, 128), MIDDLE),
            vm((32, 16, 1024), BF16),
            vm((31, 16, 1024), BF16),
            vm((4, 8, 128), F32),
            vm((16, 128), BF16),
            vm((32, 16, 128), BF16),
            vm((32, 32, 128), BF16),
            vm((24, 32, 128), BF16),
            vm((4, 16, 768), BF16),
            vm((4, 16, 768), BF16),
            vm((16, 1024), BF16),
            vm((4, 4, 2, 16, 1024), BF16),
            vm((4, 16, 256), BF16),
            vm((16, 256), BF16),
            vm((4, 4, 2, 16, 256), BF16),
            vm((4, 16, 256), BF16),
            vm((4, 16, 512), BF16),
            vm((16, 256), BF16),
            vm((16, 512), BF16),
            vm((4, 4, 2, 16, 256), BF16),
            vm((4, 4, 2, 16, 512), BF16),
            vm((31, 16, 512), BF16),
            vm((31, 16, 256), BF16),
            vm((128, 1536), BF16),
            vm((512, 128), BF16),
            vm((256, 128), BF16),
            dma((10,)),
            dma((N_CHUNK + 6,)),
            dma((3,)), dma((3,)),
            dma, dma,
            dma((2,)), dma((2,)),
            dma((2,)), dma((2,)),
            dma, dma,
            dma((3,)), dma,
            dma, dma,
            dma((3,)), dma((3,)),
            dma((3,)), dma,
            dma((3,)), dma,
            dma((3,)), dma,
            dma((2,)), dma((2, 2)),
            dma((2,)), dma((2, 2)),
            dma((2,)), dma((2, 2)),
            dma((2,)), dma((2, 4)),
            dma((3, N_CHUNK + 1)), dma((3, N_CHUNK + 1)),
        ],
        compiler_params=pltpu.CompilerParams(
            collective_id=0, has_side_effects=True, vmem_limit_bytes=60 * 1024 * 1024),
        name="policy_update",
    )(*args)
    return tuple(pl.pallas_call(
        hand_over,
        out_shape=tuple(jax.ShapeDtypeStruct(*a) for a in SHAPES),
        in_specs=[any_] * 7,
        out_specs=(any_,) * 7,
        scratch_shapes=[vm(*a) for a in SHAPES] + [dma((2, 16))],
        compiler_params=pltpu.CompilerParams(vmem_limit_bytes=60 * 1024 * 1024),
        name="hand_over",
    )(*done))


def solution(mesh):
    both = ("role", "shard")
    return jax.shard_map(
        shards,
        mesh=mesh,
        in_specs=(
            P(both, None), P(both), P(None, "shard"), P(both, None, None), P(both, None, None),
            P("shard", None), P(None, "shard"), P("shard", "role"), P("shard", "role"),
            P("role", "shard"), P("role", "shard"), P("role", "shard"),
        ),
        out_specs=(
            P("role", "shard"), P("shard", None), P(None, "shard"), P("shard", "role"),
            P("shard", "role"), P("role", "shard"), P("role", "shard"),
        ),
        check_vma=False,
    )
```

```python
import jax
import jax.numpy as jnp
from jax import lax
from jax.experimental import pallas as pl
from jax.experimental.pallas import tpu as pltpu
from jax.sharding import PartitionSpec as P

HD = 128
MESH = pl.DeviceIdType.MESH
F32 = jnp.float32
BF16 = jnp.bfloat16
LEARNER = 3

learn_rate = 0.001
first_decay = 0.9
second_decay = 0.95
adam_eps = 1e-08
weight_decay = 0.1
first_fix = 1.0 - 0.9**10
second_fix = 1.0 - 0.95**10
scale = HD ** (-0.5)

N_CHUNK = 4
CHUNKS = ((0, 256), (768, 256), (256, 512), (1024, 512))
MIDDLE = BF16
ORDER = 13


def adamw(params, gradient, first_moment, second_moment):
    moment_one = first_decay * first_moment + (1.0 - first_decay) * gradient
    moment_two = second_decay * second_moment + (1.0 - second_decay) * gradient * gradient
    stepped = moment_one / first_fix / (jnp.sqrt(moment_two / second_fix) + adam_eps)
    wide_params = params.astype(F32)
    updated = wide_params - learn_rate * (stepped + weight_decay * wide_params)
    return (updated, moment_one, moment_two)


def settle(ref, sem):
    pltpu.make_async_copy(ref, ref, sem).wait()


def nt(a, b):
    return lax.dot_general(a, b, (((1,), (1,)), ((), ())), preferred_element_type=F32)


def tn(a, b):
    return lax.dot_general(a, b, (((0,), (0,)), ((), ())), preferred_element_type=F32)


def nn(a, b):
    return jnp.dot(a, b, preferred_element_type=F32)


def kernel(
    ids_ref, len_ref, table_hbm, keys_hbm, vals_hbm, wqkv_hbm, wout_hbm,
    m_q_hbm, v_q_hbm, m_o_hbm, v_o_hbm, cot_hbm,
    dec_out, nq_out, no_out, mq_out, sq_out, mo_out, so_out,
    table, keys, vals, wq, wout, m_q, v_q, m_o, v_o, cot,
    tsend, line_in, line_sum, line_out, plane_in,
    gsend, g_line, g_sum, g_out, g_plane, idx4, idsend, idrecv, selsend, selrecv,
    xsend, xrecv, hrs, hrrecv, hsend, hmsg, hgrecv, rsend_a, rsend_b, rmsg_a, rmsg_b,
    agrecv_a, agrecv_b,
    count_mix, count_grad, nq, no, dec,
    loc, out_sem, id_s, id_r, idg_s, idg_r, ts_s, ts_r, tp_s, tp_r, gs_s, gs_r, gp_s, gp_r,
    cot_s, cot_r, sel_s, sel_r, x_s, x_r, hrel_s, hrel_r, rela_s, rela_r, relb_s, relb_r,
    hg_s, hg_r, aga_s, aga_r, agb_s, agb_r, hr_s, hr_r,
    e_s, e_r,
):
    role = lax.axis_index("role")
    shard = lax.axis_index("shard")
    y, x, zl = shard >> 3, (shard >> 1) & 3, shard & 1
    z_hi, core = role >> 1, role & 1
    sibling = z_hi * 2 + (1 - core)
    across = (1 - z_hi) * 2 + core
    others = [(role + q) & 3 for q in range(4)]

    ys = [(y + d) & 3 for d in range(4)]
    xs = [(x + d) & 3 for d in range(4)]
    zs = [zl, 1 - zl]
    spots = [(x + y + d) & 3 for d in range(4)]
    holds = [spot < 3 for spot in spots]
    rows_at = [v * 8 for v in ys]
    cols_at = [v * 2 for v in xs]
    unit_row = [v * 6 for v in ys]
    unit_col = [v * 2 for v in spots]

    def peer(k):
        dy, dx, dz = k >> 3, (k >> 1) & 3, k & 1
        turn = (dy + dx) & 3
        return (rows_at[dy] + cols_at[dx] + zs[dz], holds[turn],
                unit_row[dy] + unit_col[turn] + zs[dz])

    holder = holds[0]
    my_unit = jnp.where(holder, peer(0)[2], 0)

    def put(src, dst, send, recv, to_role, to_shard):
        pltpu.make_async_remote_copy(
            src_ref=src, dst_ref=dst, send_sem=send, recv_sem=recv,
            device_id=(to_role, to_shard), device_id_type=MESH,
        ).start()

    def each_peer(body, first=1, last=32):
        for j in range(first, last):
            k = j * ORDER % 32
            body(k, *peer(k))

    barrier = pltpu.get_barrier_semaphore()
    each_peer(lambda k, p, h, u: pl.semaphore_signal(
        barrier, inc=1, device_id=(role, p), device_id_type=MESH))
    for q in range(1, 4):
        pl.semaphore_signal(
            barrier, inc=1, device_id=(others[q], shard), device_id_type=MESH)

    col0 = pl.multiple_of(role * 1536, 128)
    row0 = pl.multiple_of(role * 512, 128)
    fetches = [
        pltpu.make_async_copy(a, b, loc.at[i])
        for i, (a, b) in enumerate((
            (table_hbm, table),
            (wqkv_hbm.at[:, pl.ds(col0, 1536)], wq),
            (wout_hbm, wout),
            (cot_hbm, cot),
            (keys_hbm.at[0], keys),
            (vals_hbm.at[0], vals),
            (m_q_hbm, m_q),
            (v_q_hbm, v_q),
            (m_o_hbm, m_o),
            (v_o_hbm, v_o),
        ))
    ]
    for i, f in enumerate(fetches):
        if i != 3:
            f.start()

    @pl.when(role == LEARNER)
    def _():
        fetches[3].start()

    row8 = lax.broadcasted_iota(jnp.int32, (8, 128), 0)
    lane8 = lax.broadcasted_iota(jnp.int32, (8, 128), 1)
    ids = jnp.zeros((8, 128), jnp.int32)
    for i in range(8):
        ids = jnp.where(row8 == i, ids_ref[0, i], ids)
    ids = ids.astype(F32)
    length = len_ref[0]
    live8 = row8 < length
    idx4[role] = ids

    fetches[0].wait()
    fetches[1].wait()
    for c in range(12):
        part = nn(table[...], wq[:, c * 128:(c + 1) * 128]).astype(BF16)
        for h in range(2):
            u = 2 * c + h
            row, spot, pz = u // 6, u % 6 // 2, u % 2
            tsend[0, u] = part[h * 128:h * 128 + 64]
            tsend[1, (spot - row) % 4 * 6 + spot * 2 + pz] = part[h * 128 + 64:h * 128 + 128]

    pl.semaphore_wait(barrier, 34)

    for q in range(1, 4):
        put(idx4.at[role], idx4.at[role], id_s.at[q - 1], id_r.at[q - 1], others[q], shard)

    for d in (2, 1, 3):
        put(tsend.at[0, pl.ds(ys[d] * 6, 6)], line_in.at[0, d - 1], ts_s.at[0], ts_r.at[0],
            role, rows_at[d] + cols_at[0] + zs[0])
        put(tsend.at[1, pl.ds(xs[d] * 6, 6)], line_in.at[1, d - 1], ts_s.at[1], ts_r.at[1],
            role, rows_at[0] + cols_at[d] + zs[0])

    for q in range(1, 4):
        settle(idx4.at[0], id_r.at[q - 1])
    lane16 = lax.broadcasted_iota(jnp.int32, (16, 128), 1)
    all_ids = jnp.where(
        lane16 < 64,
        jnp.concatenate([idx4[0], idx4[1]], axis=0),
        jnp.concatenate([idx4[2], idx4[3]], axis=0)).astype(BF16)
    idsend[...] = all_ids
    idrecv[shard] = all_ids

    def send_ids(now):
        def body(k, p, h, u):
            @pl.when(h if now else jnp.logical_not(h))
            def _():
                put(idsend, idrecv.at[shard], idg_s, idg_r, role, p)
        each_peer(body)
    send_ids(True)

    for half in range(2):
        settle(line_in.at[half], ts_r.at[half])
        total = tsend[half, pl.ds((xs[0] if half else ys[0]) * 6, 6)].astype(F32)
        for d in range(3):
            total += line_in[half, d].astype(F32)
        line_sum[half] = total
        line_out[half] = total.astype(line_out.dtype)
        for d, dz in ((2, 0), (2, 1), (1, 1), (3, 1), (1, 0), (3, 0), (0, 1)):
            @pl.when(holds[d])
            def _():
                put(line_out.at[half, spots[d] * 2 + zs[dz]], plane_in.at[half, d * 2 + dz - 1],
                    tp_s.at[half], tp_r.at[half], role,
                    (rows_at[d] + cols_at[0] if half else rows_at[0] + cols_at[d]) + zs[dz])

    @pl.when(role == LEARNER)
    def _():
        fetches[2].wait()
        fetches[3].wait()
        for i in range(8):
            upper, lower = (
                nt(cot[...], wout[j * 1024 + i * 128:j * 1024 + (i + 1) * 128, :])
                .reshape(32, 8, 128)
                for j in range(2)
            )
            gsend[i // 4, :, :, :, :, i % 4 * 128:(i % 4 + 1) * 128] = jnp.concatenate(
                [upper, lower], axis=1).astype(BF16).reshape(4, 4, 2, 16, 128)

    @pl.when(role != LEARNER)
    def _():
        fetches[2].wait()

    @pl.when(holder)
    def _():
        settle(idrecv.at[0:31], idg_r)
        got = idrecv[...].astype(F32)
        got = jnp.concatenate([
            jnp.broadcast_to(got[:, :, 0:1], (32, 16, 128)),
            jnp.broadcast_to(got[:, :, 64:65], (32, 16, 128))], axis=1).reshape(1024, 128)
        lane = lax.broadcasted_iota(jnp.int32, (1024, 128), 1) + 128 * (my_unit & 1)
        chosen = jnp.where(got == lane.astype(F32), 1.0, 0.0).astype(BF16)
        parts = []
        for half in range(2):
            settle(plane_in.at[half], tp_r.at[half])
            total = line_sum[half, spots[0] * 2 + zl]
            for k in range(7):
                total += plane_in[half, k].astype(F32)
            parts.append(total)
        whole = jnp.concatenate(parts, axis=0).astype(BF16)
        selsend[...] = nn(chosen, whole).astype(BF16).reshape(32, 32, 128)

        def send_rows(k, p, h, u):
            put(selsend.at[p], selrecv.at[my_unit], sel_s, sel_r, role, p)
        each_peer(send_rows)
        selrecv[my_unit] = selsend[shard]

    @pl.when(role == LEARNER)
    def _():
        for d in (2, 1, 3):
            put(gsend.at[0, ys[d]], g_line.at[0, d - 1], gs_s.at[0], gs_r.at[0],
                role, rows_at[d] + cols_at[0] + zs[0])
            put(gsend.at[1, :, xs[d]], g_line.at[1, d - 1], gs_s.at[1], gs_r.at[1],
                role, rows_at[0] + cols_at[d] + zs[0])
        for q in range(3):
            put(cot_hbm, cot, cot_s.at[q], cot_r, q, shard)
    send_ids(False)

    @pl.when(holder)
    def _():
        settle(selrecv.at[0:23], sel_r)

    @pl.when(jnp.logical_not(holder))
    def _():
        settle(idrecv.at[0:31], idg_r)
        settle(selrecv, sel_r)

    blocks = [selrecv[2 * c].astype(F32) + selrecv[2 * c + 1].astype(F32) for c in range(12)]
    for q in range(4):
        for i in range(6):
            pair = jnp.concatenate(
                [blocks[i][8 * q:8 * q + 8], blocks[6 + i][8 * q:8 * q + 8]], axis=0)
            xsend[q, :, i * 128:(i + 1) * 128] = pair.astype(BF16)
    for q in range(1, 4):
        to = others[q]
        put(xsend.at[to], xrecv.at[role], x_s.at[q - 1], x_r.at[q - 1], to, shard)
    xrecv[role] = xsend[role]

    @pl.when(role == LEARNER)
    def _():
        for half in range(2):
            settle(g_line.at[half], gs_r.at[half])
            total = (gsend[1, :, x] if half else gsend[0, y]).astype(F32)
            for d in range(3):
                total += g_line[half, d].astype(F32)
            g_sum[half] = total
            g_out[half] = total.astype(BF16)
            for d, dz in ((2, 0), (2, 1), (1, 1), (3, 1), (1, 0), (3, 0), (0, 1)):
                put(g_out.at[half, ys[d] if half else xs[d], zs[dz]],
                    g_plane.at[half, d * 2 + dz - 1], gp_s.at[half], gp_r.at[half], role,
                    (rows_at[d] + cols_at[0] if half else rows_at[0] + cols_at[d]) + zs[dz])

    fetches[4].wait()
    fetches[5].wait()
    for q in range(1, 4):
        settle(xrecv.at[0], x_r.at[q - 1])

    pieces = [xrecv[q].astype(F32) for q in range(4)]

    def tile(c):
        block, i = divmod(c, 12)
        return pieces[block][8 * (i // 6):8 * (i // 6) + 8, (i % 6) * 128:(i % 6 + 1) * 128]

    def stack(tiles):
        return jnp.concatenate(tiles, axis=0)

    q_tiles = [tile(h) for h in range(16)]
    q_all = stack(q_tiles).astype(BF16)
    k_new = stack([tile(16 + h) for h in range(16)]).astype(BF16)
    v_new = stack([tile(32 + h) for h in range(16)]).astype(BF16)

    def head(ref, h):
        return ref[:, h * 128:(h + 1) * 128]

    s1 = stack([nt(q_tiles[h].astype(BF16), head(keys, h)) for h in range(16)]) * scale
    s2 = nt(q_all, k_new) * scale
    ri = lax.broadcasted_iota(jnp.int32, (128, 128), 0)
    ci = lax.broadcasted_iota(jnp.int32, (128, 128), 1)
    allowed = (ri // 8 == ci // 8) & (ci % 8 <= ri % 8) & (ci % 8 < length)
    s2 = jnp.where(allowed, s2, -1e30)
    top = jnp.maximum(jnp.max(s1, axis=1, keepdims=True), jnp.max(s2, axis=1, keepdims=True))
    e1, e2 = jnp.exp(s1 - top), jnp.exp(s2 - top)
    den = jnp.sum(e1, axis=1, keepdims=True) + jnp.sum(e2, axis=1, keepdims=True)
    w1, w2 = e1 / den, e2 / den
    r2 = w2.astype(BF16)
    o2 = nn(r2, v_new)
    out_tiles = [
        nn(w1[8 * h:8 * h + 8].astype(BF16), head(vals, h)) + o2[8 * h:8 * h + 8]
        for h in range(16)
    ]
    for i in range(8):
        hrs[:, i * 128:(i + 1) * 128] = stack([out_tiles[i], out_tiles[8 + i]]).astype(BF16)

    @pl.when(role == LEARNER)
    def _():
        live_out = [jnp.where(live8, t, 0.0) for t in out_tiles]
        for q in range(4):
            for i in range(2):
                hsend[q, :, i * 128:(i + 1) * 128] = stack(
                    [live_out[4 * q + i], live_out[4 * q + 2 + i]]).astype(BF16)
        for q in range(3):
            put(hsend.at[q], hmsg, hrel_s.at[q], hrel_r, q, shard)
        hmsg[...] = hsend[3]

    @pl.when(role != LEARNER)
    def _():
        settle(hmsg, hrel_r)
    def shard_at(py, px, pz):
        return rows_at[py] + cols_at[px] + zs[pz]

    class Gather:
        def __init__(self, msg, buf, send, recv, count):
            self.msg, self.buf, self.send, self.recv, self.count = msg, buf, send, recv, count

        def lanes(self, half):
            width = self.msg.shape[1] // 2
            return pl.ds(half * width, width)

        def hop(self, step, half, src, dst, dy, dx, dz):
            put(src, dst, self.send.at[half], self.recv.at[half, step], role,
                shard_at(dy, dx, dz))

        def arrived(self, half, step, blocks):
            settle(self.count.at[0:blocks], self.recv.at[half, step])

        def start(self, far):
            self.buf[y, x, zl] = self.msg[...]
            for half in range(2):
                n = self.lanes(half)
                spots = [(0, 1), (1, 0), (3, 0), (1, 1), (3, 1)] + far
                for d, dz in spots:
                    self.hop(0, half, self.msg.at[:, n], self.buf.at[y, x, zl, :, n],
                             d * half, d * (1 - half), dz)

        def line(self, half):
            n = self.lanes(half)
            return self.buf.at[:, x, :, :, n] if half else self.buf.at[y, :, :, :, n]

        def sent(self):
            for half in range(2):
                settle(self.count.at[0:31], self.send.at[half])

    class Short(Gather):
        def first(self):
            self.start([(2, 0), (2, 1)])

        def second(self):
            for half in range(2):
                self.arrived(half, 0, 7)
                for d in (2, 1, 3):
                    self.hop(1, half, self.line(half), self.line(half),
                             d * (1 - half), d * half, 0)

        def last(self):
            for half in range(2):
                self.arrived(half, 1, 24)

    class Long(Gather):
        def first(self):
            self.start([])

        def second(self):
            for half in range(2):
                self.arrived(half, 0, 5)
                n = self.lanes(half)
                dy, dx = half, 1 - half
                before = self.buf.at[ys[3 * dy], xs[3 * dx], zl, :, n]
                after = self.buf.at[ys[dy], xs[dx], 1 - zl, :, n]
                self.hop(1, half, before, before, dy, dx, 0)
                self.hop(1, half, after, after, 3 * dy, 3 * dx, 0)

        def third(self):
            for half in range(2):
                self.arrived(half, 1, 2)
                for d in (1, 3):
                    self.hop(2, half, self.line(half), self.line(half),
                             d * (1 - half), d * half, 0)

        def fourth(self):
            for half in range(2):
                self.arrived(half, 2, 16)
                n = self.lanes(half)
                if half:
                    before = self.buf.at[0:2, xs[3], :, :, n]
                    after = self.buf.at[2:4, xs[1], :, :, n]
                else:
                    before = self.buf.at[ys[3], 0:2, :, :, n]
                    after = self.buf.at[ys[1], 2:4, :, :, n]
                self.hop(3, half, before, before, 1 - half, half, 0)
                self.hop(3, half, after, after, 3 * (1 - half), 3 * half, 0)

        def last(self):
            for half in range(2):
                self.arrived(half, 3, 8)

    mixes = Long(hrs, hrrecv, hr_s, hr_r, count_mix)
    heads = Short(hmsg, hgrecv, hg_s, hg_r, idrecv)
    grads_a = Short(rmsg_a, agrecv_a, aga_s, aga_r, idrecv)
    grads_b = Short(rmsg_b, agrecv_b, agb_s, agb_r, count_grad)

    heads.first()

    @pl.when(role != LEARNER)
    def _():
        mixes.first()

    @pl.when(role == LEARNER)
    def _():
        g_tiles = [None] * 16
        for half in range(2):
            settle(g_plane.at[half], gp_r.at[half])
            total = g_sum[half, y if half else x, zl]
            for k in range(7):
                total += g_plane[half, k].astype(F32)
            for i in range(4):
                cols = slice(i * 128, (i + 1) * 128)
                g_tiles[4 * half + i] = jnp.where(live8, total[0:8, cols], 0.0)
                g_tiles[8 + 4 * half + i] = jnp.where(live8, total[8:16, cols], 0.0)
        g_all = stack(g_tiles).astype(BF16)
        gw1 = stack([nt(g_tiles[h].astype(BF16), head(vals, h)) for h in range(16)])
        gw2 = nt(g_all, v_new)
        dots = jnp.sum(w1 * gw1, axis=1, keepdims=True) + jnp.sum(w2 * gw2, axis=1, keepdims=True)
        gs1 = w1 * (gw1 - dots) * scale
        gs2 = (w2 * (gw2 - dots) * scale).astype(BF16)
        gq2 = nn(gs2, k_new)
        gk = tn(gs2, q_all)
        gv = tn(r2, g_all)
        gp = [
            nn(gs1[8 * h:8 * h + 8].astype(BF16), head(keys, h)) + gq2[8 * h:8 * h + 8]
            for h in range(16)
        ]
        gp += [gk[8 * h:8 * h + 8] for h in range(16)]
        gp += [gv[8 * h:8 * h + 8] for h in range(16)]
        for q in range(4):
            for i in range(6):
                pair = stack([gp[12 * q + i], gp[12 * q + 6 + i]]).astype(BF16)
                if i < 2:
                    rsend_a[q, :, i * 128:(i + 1) * 128] = pair
                else:
                    rsend_b[q, :, (i - 2) * 128:(i - 1) * 128] = pair
        for q in range(3):
            put(rsend_a.at[q], rmsg_a, rela_s.at[q], rela_r, q, shard)
        for q in range(3):
            put(rsend_b.at[q], rmsg_b, relb_s.at[q], relb_r, q, shard)
        rmsg_a[...] = rsend_a[3]
        rmsg_b[...] = rsend_b[3]

    copies = []

    def copy_out(a, b):
        pltpu.make_async_copy(a, b, out_sem.at[len(copies)]).start()
        copies.append(a)

    def spread(src, dst, n):
        put(src, dst, e_s.at[1, n], e_r.at[1, n], across, shard)
        put(src, dst, e_s.at[0, n], e_r.at[0, n], sibling, shard)
        copy_out(src, dst)

    def q_cols(of, n):
        at, width = CHUNKS[n]
        return nq_out.at[:, pl.ds(pl.multiple_of(of * 1536 + at, 128), width)]

    def o_rows(of):
        return no_out.at[pl.ds(pl.multiple_of(of * 512, 128), 512), :]

    half = (lax.broadcasted_iota(jnp.int32, (512, 128), 0) // 8) % 2

    def update_out():
        copies.clear()
        fetches[8].wait()
        fetches[9].wait()
        cot_wide = jnp.broadcast_to(
            cot[...].astype(F32).reshape(32, 1, 8, 128), (32, 2, 8, 128)).reshape(512, 128)
        cot_both = jnp.concatenate(
            [jnp.where(half == j, cot_wide, 0.0).astype(BF16) for j in range(2)], axis=1)
        heads.last()
        grad_out = tn(hgrecv[...].reshape(512, 256), cot_both)
        for j in range(2):
            here = slice(j * 256, (j + 1) * 256)
            params = wout[pl.ds(pl.multiple_of(row0 + j * 256, 128), 256), :]
            new, one, two = adamw(
                params, grad_out[:, j * 128:(j + 1) * 128], m_o[here, :], v_o[here, :])
            no[here, :] = new.astype(BF16)
            m_o[here, :] = one
            v_o[here, :] = two
        spread(no, o_rows(role), N_CHUNK)
        copy_out(m_o, mo_out)
        copy_out(v_o, so_out)

    @pl.when(role != LEARNER)
    def _():
        settle(rmsg_a, rela_r)
    grads_a.first()

    @pl.when(role != LEARNER)
    def _():
        settle(rmsg_b, relb_r)
    grads_b.first()
    heads.second()
    grads_a.second()
    grads_b.second()

    @pl.when(role == LEARNER)
    def _():
        mixes.first()

    @pl.when(role != LEARNER)
    def _():
        settle(cot, cot_r)
    mixes.second()
    update_out()

    got_ids = idrecv[...].astype(F32)[:, 8:16, 64:65]
    got_ids = jnp.broadcast_to(
        jnp.concatenate([got_ids, got_ids], axis=1), (32, 16, 128)).reshape(512, 128)
    lane = lax.broadcasted_iota(jnp.int32, (512, 128), 1).astype(F32)
    low = jnp.where(got_ids == lane, 1.0, 0.0).astype(BF16)
    high = jnp.where(got_ids == lane + 128.0, 1.0, 0.0).astype(BF16)
    rows = nn(low, table[0:128, :]) + nn(high, table[128:256, :])
    halves = [jnp.where(half == j, rows, 0.0).T.astype(BF16) for j in range(2)]
    fetches[6].wait()
    fetches[7].wait()
    for n, (at, width) in enumerate(CHUNKS):
        cols = slice(at, at + width)
        if n == 0:
            grads_a.last()
        if n == 2:
            mixes.third()
            grads_b.last()
        buf = agrecv_b if n >= 2 else agrecv_a
        grad = nn(halves[n % 2], buf[...].reshape(512, width))
        new, one, two = adamw(wq[:, cols], grad, m_q[:, cols], v_q[:, cols])
        nq[:, cols] = new.astype(BF16)
        m_q[:, cols] = one
        v_q[:, cols] = two
        spread(nq.at[:, cols], q_cols(role, n), n)
    copy_out(m_q, mq_out)
    copy_out(v_q, sq_out)
    mixes.fourth()

    def part(of, n):
        return q_cols(of, n) if n < N_CHUNK else o_rows(of)

    for n in (N_CHUNK, *range(N_CHUNK)):
        settle(part(across, n), e_r.at[1, n])
        put(part(across, n), part(across, n), e_s.at[2, n], e_r.at[2, n], sibling, shard)

    mixes.last()
    mix = hrrecv[...].reshape(512, 1024)
    upper = nn(mix, wout[0:1024, :]).reshape(32, 2, 8, 128)
    lower = nn(mix, wout[1024:2048, :]).reshape(32, 2, 8, 128)
    dec[...] = (upper[:, 0] + lower[:, 1]).reshape(256, 128).astype(BF16)
    copy_out(dec, dec_out)

    for n in range(N_CHUNK + 1):
        settle(part(sibling, n), e_r.at[0, n])
        settle(part((1 - z_hi) * 2 + (1 - core), n), e_r.at[2, n])
        for way in range(3):
            settle(part(role, n), e_s.at[way, n])
    for i, a in enumerate(copies):
        settle(a, out_sem.at[i])
    for q in range(3):
        settle(idx4.at[0], id_s.at[q])
        settle(xsend.at[0], x_s.at[q])

    @pl.when(holder)
    def _():
        for half in range(2):
            settle(plane_in.at[half, 0:5], tp_s.at[half])
        settle(selsend.at[0:31], sel_s)

    @pl.when(jnp.logical_not(holder))
    def _():
        for half in range(2):
            settle(plane_in.at[half, 0:6], tp_s.at[half])

    @pl.when(role == LEARNER)
    def _():
        for q in range(3):
            settle(cot, cot_s.at[q])
            settle(rmsg_a, rela_s.at[q])
            settle(rmsg_b, relb_s.at[q])
            settle(hmsg, hrel_s.at[q])
        for half in range(2):
            settle(g_line.at[half], gs_s.at[half])
            settle(g_plane.at[half], gp_s.at[half])
    settle(idrecv.at[0:31], idg_s)
    for half in range(2):
        settle(line_in.at[half], ts_s.at[half])
    heads.sent()
    grads_a.sent()
    grads_b.sent()
    mixes.sent()


SHAPES = (
    ((256, 128), BF16), ((128, 6144), BF16), ((2048, 128), BF16),
    ((128, 1536), F32), ((128, 1536), F32), ((512, 128), F32), ((512, 128), F32),
)


def hand_over(*refs):
    ins, outs, stage, sems = refs[:7], refs[7:14], refs[14:21], refs[21]
    moves = []
    for a, v, b in zip(ins, stage, outs):
        pieces = 4 if a.shape == (128, 6144) else 2 if a.shape[0] * a.shape[1] > 131072 else 1
        rows = a.shape[0] // pieces
        for i in range(pieces):
            part, n = pl.ds(i * rows, rows), len(moves)
            moves.append((
                pltpu.make_async_copy(a.at[part, :], v.at[part, :], sems.at[0, n]),
                pltpu.make_async_copy(v.at[part, :], b.at[part, :], sems.at[1, n])))
    for m, _ in moves:
        m.start()
    for m, n in moves:
        m.wait()
        n.start()
    for _, n in moves:
        n.wait()


def shards(*args):
    any_ = pl.BlockSpec(memory_space=pl.ANY)
    smem = pl.BlockSpec(memory_space=pltpu.SMEM)
    dma, vm = pltpu.SemaphoreType.DMA, pltpu.VMEM
    done = pl.pallas_call(
        kernel,
        out_shape=tuple(jax.ShapeDtypeStruct(*a) for a in SHAPES),
        in_specs=[smem, smem] + [any_] * 10,
        out_specs=(any_,) * 7,
        scratch_shapes=[
            vm((256, 128), BF16),
            vm((128, 2048), BF16),
            vm((128, 2048), BF16),
            vm((128, 1536), BF16),
            vm((2048, 128), BF16),
            vm((128, 1536), F32),
            vm((128, 1536), F32),
            vm((512, 128), F32),
            vm((512, 128), F32),
            vm((256, 128), BF16),
            vm((2, 24, 64, 128), BF16),
            vm((2, 3, 6, 64, 128), BF16),
            vm((2, 6, 64, 128), F32),
            vm((2, 6, 64, 128), MIDDLE),
            vm((2, 7, 64, 128), MIDDLE),
            vm((2, 4, 4, 2, 16, 512), BF16),
            vm((2, 3, 4, 2, 16, 512), BF16),
            vm((2, 4, 2, 16, 512), F32),
            vm((2, 4, 2, 16, 512), BF16),
            vm((2, 7, 16, 512), BF16),
            vm((4, 8, 128), F32),
            vm((16, 128), BF16),
            vm((32, 16, 128), BF16),
            vm((32, 32, 128), BF16),
            vm((24, 32, 128), BF16),
            vm((4, 16, 768), BF16),
            vm((4, 16, 768), BF16),
            vm((16, 1024), BF16),
            vm((4, 4, 2, 16, 1024), BF16),
            vm((4, 16, 256), BF16),
            vm((16, 256), BF16),
            vm((4, 4, 2, 16, 256), BF16),
            vm((4, 16, 256), BF16),
            vm((4, 16, 512), BF16),
            vm((16, 256), BF16),
            vm((16, 512), BF16),
            vm((4, 4, 2, 16, 256), BF16),
            vm((4, 4, 2, 16, 512), BF16),
            vm((31, 16, 512), BF16),
            vm((31, 16, 256), BF16),
            vm((128, 1536), BF16),
            vm((512, 128), BF16),
            vm((256, 128), BF16),
            dma((10,)),
            dma((N_CHUNK + 6,)),
            dma((3,)), dma((3,)),
            dma, dma,
            dma((2,)), dma((2,)),
            dma((2,)), dma((2,)),
            dma((2,)), dma((2,)),
            dma((2,)), dma((2,)),
            dma((3,)), dma,
            dma, dma,
            dma((3,)), dma((3,)),
            dma((3,)), dma,
            dma((3,)), dma,
            dma((3,)), dma,
            dma((2,)), dma((2, 2)),
            dma((2,)), dma((2, 2)),
            dma((2,)), dma((2, 2)),
            dma((2,)), dma((2, 4)),
            dma((3, N_CHUNK + 1)), dma((3, N_CHUNK + 1)),
        ],
        compiler_params=pltpu.CompilerParams(
            collective_id=0, has_side_effects=True, vmem_limit_bytes=60 * 1024 * 1024),
        name="policy_update",
    )(*args)
    return tuple(pl.pallas_call(
        hand_over,
        out_shape=tuple(jax.ShapeDtypeStruct(*a) for a in SHAPES),
        in_specs=[any_] * 7,
        out_specs=(any_,) * 7,
        scratch_shapes=[vm(*a) for a in SHAPES] + [dma((2, 16))],
        compiler_params=pltpu.CompilerParams(vmem_limit_bytes=60 * 1024 * 1024),
        name="hand_over",
    )(*done))


def solution(mesh):
    both = ("role", "shard")
    return jax.shard_map(
        shards,
        mesh=mesh,
        in_specs=(
            P(both, None), P(both), P(None, "shard"), P(both, None, None), P(both, None, None),
            P("shard", None), P(None, "shard"), P("shard", "role"), P("shard", "role"),
            P("role", "shard"), P("role", "shard"), P("role", "shard"),
        ),
        out_specs=(
            P("role", "shard"), P("shard", None), P(None, "shard"), P("shard", "role"),
            P("shard", "role"), P("role", "shard"), P("role", "shard"),
        ),
        check_vma=False,
    )
```

```python
import jax
import jax.numpy as jnp
from jax import lax
from jax.experimental import pallas as pl
from jax.experimental.pallas import tpu as pltpu
from jax.sharding import PartitionSpec as P

HD = 128
MESH = pl.DeviceIdType.MESH
F32 = jnp.float32
BF16 = jnp.bfloat16
LEARNER = 3

learn_rate = 0.001
first_decay = 0.9
second_decay = 0.95
adam_eps = 1e-08
weight_decay = 0.1
first_fix = 1.0 - 0.9**10
second_fix = 1.0 - 0.95**10
scale = HD ** (-0.5)

N_CHUNK = 4
CHUNKS = ((0, 256), (768, 256), (256, 512), (1024, 512))
MIDDLE = BF16
ORDER = 13


def adamw(params, gradient, first_moment, second_moment):
    moment_one = first_decay * first_moment + (1.0 - first_decay) * gradient
    moment_two = second_decay * second_moment + (1.0 - second_decay) * gradient * gradient
    stepped = moment_one / first_fix / (jnp.sqrt(moment_two / second_fix) + adam_eps)
    wide_params = params.astype(F32)
    updated = wide_params - learn_rate * (stepped + weight_decay * wide_params)
    return (updated, moment_one, moment_two)


def settle(ref, sem):
    pltpu.make_async_copy(ref, ref, sem).wait()


def nt(a, b):
    return lax.dot_general(a, b, (((1,), (1,)), ((), ())), preferred_element_type=F32)


def tn(a, b):
    return lax.dot_general(a, b, (((0,), (0,)), ((), ())), preferred_element_type=F32)


def nn(a, b):
    return jnp.dot(a, b, preferred_element_type=F32)


def kernel(
    ids_ref, len_ref, table_hbm, keys_hbm, vals_hbm, wqkv_hbm, wout_hbm,
    m_q_hbm, v_q_hbm, m_o_hbm, v_o_hbm, cot_hbm,
    dec_out, nq_out, no_out, mq_out, sq_out, mo_out, so_out,
    table, keys, vals, wq, wout, m_q, v_q, m_o, v_o, cot,
    tsend, line_in, line_sum, line_out, plane_in,
    gsend, g_line, g_sum, g_out, g_plane, idx4, idsend, idrecv, selsend, selrecv,
    xsend, xrecv, hrs, hrrecv, hsend, hmsg, hgrecv, rsend_a, rsend_b, rmsg_a, rmsg_b,
    agrecv_a, agrecv_b,
    count_mix, count_grad, nq, no, dec,
    ready, loc, out_sem, id_s, id_r, idg_s, idg_r, ts_s, ts_r, tp_s, tp_r, gs_s, gs_r, gp_s, gp_r,
    cot_s, cot_r, sel_s, sel_r, x_s, x_r, hrel_s, hrel_r, rela_s, rela_r, relb_s, relb_r,
    hg_s, hg_r, aga_s, aga_r, agb_s, agb_r, hr_s, hr_r,
    e_s, e_r,
):
    role = lax.axis_index("role")
    shard = lax.axis_index("shard")
    y, x, zl = shard >> 3, (shard >> 1) & 3, shard & 1
    z_hi, core = role >> 1, role & 1
    sibling = z_hi * 2 + (1 - core)
    across = (1 - z_hi) * 2 + core
    others = [(role + q) & 3 for q in range(4)]

    ys = [(y + d) & 3 for d in range(4)]
    xs = [(x + d) & 3 for d in range(4)]
    zs = [zl, 1 - zl]
    spots = [(x + y + d) & 3 for d in range(4)]
    holds = [spot < 3 for spot in spots]
    rows_at = [v * 8 for v in ys]
    cols_at = [v * 2 for v in xs]
    unit_row = [v * 6 for v in ys]
    unit_col = [v * 2 for v in spots]

    def peer(k):
        dy, dx, dz = k >> 3, (k >> 1) & 3, k & 1
        turn = (dy + dx) & 3
        return (rows_at[dy] + cols_at[dx] + zs[dz], holds[turn],
                unit_row[dy] + unit_col[turn] + zs[dz])

    holder = holds[0]
    my_unit = jnp.where(holder, peer(0)[2], 0)

    def put(src, dst, send, recv, to_role, to_shard):
        pltpu.make_async_remote_copy(
            src_ref=src, dst_ref=dst, send_sem=send, recv_sem=recv,
            device_id=(to_role, to_shard), device_id_type=MESH,
        ).start()

    def each_peer(body, first=1, last=32):
        for j in range(first, last):
            k = j * ORDER % 32
            body(k, *peer(k))

    barrier = pltpu.get_barrier_semaphore()
    for k in (1, 2, 3, 4, 5, 6, 7, 8, 16, 24):
        pl.semaphore_signal(barrier, inc=1, device_id=(role, peer(k)[0]), device_id_type=MESH)
    for q in range(1, 4):
        pl.semaphore_signal(
            barrier, inc=1, device_id=(others[q], shard), device_id_type=MESH)

    col0 = pl.multiple_of(role * 1536, 128)
    row0 = pl.multiple_of(role * 512, 128)
    fetches = [
        pltpu.make_async_copy(a, b, loc.at[i])
        for i, (a, b) in enumerate((
            (table_hbm, table),
            (wqkv_hbm.at[:, pl.ds(col0, 1536)], wq),
            (wout_hbm, wout),
            (cot_hbm, cot),
            (keys_hbm.at[0], keys),
            (vals_hbm.at[0], vals),
            (m_q_hbm, m_q),
            (v_q_hbm, v_q),
            (m_o_hbm, m_o),
            (v_o_hbm, v_o),
        ))
    ]
    for i, f in enumerate(fetches):
        if i != 3:
            f.start()

    @pl.when(role == LEARNER)
    def _():
        fetches[3].start()

    row8 = lax.broadcasted_iota(jnp.int32, (8, 128), 0)
    lane8 = lax.broadcasted_iota(jnp.int32, (8, 128), 1)
    ids = jnp.zeros((8, 128), jnp.int32)
    for i in range(8):
        ids = jnp.where(row8 == i, ids_ref[0, i], ids)
    ids = ids.astype(F32)
    length = len_ref[0]
    live8 = row8 < length
    idx4[role] = ids

    fetches[0].wait()
    fetches[1].wait()
    for c in range(12):
        part = nn(table[...], wq[:, c * 128:(c + 1) * 128]).astype(BF16)
        for h in range(2):
            u = 2 * c + h
            row, spot, pz = u // 6, u % 6 // 2, u % 2
            tsend[0, u] = part[h * 128:h * 128 + 64]
            tsend[1, (spot - row) % 4 * 6 + spot * 2 + pz] = part[h * 128 + 64:h * 128 + 128]

    pl.semaphore_wait(barrier, 13)
    for k in (8, 16, 24):
        pl.semaphore_signal(ready, inc=1, device_id=(role, peer(k)[0]), device_id_type=MESH)

    for q in range(1, 4):
        put(idx4.at[role], idx4.at[role], id_s.at[q - 1], id_r.at[q - 1], others[q], shard)

    for d in (2, 1, 3):
        put(tsend.at[0, pl.ds(ys[d] * 6, 6)], line_in.at[0, d - 1], ts_s.at[0], ts_r.at[0],
            role, rows_at[d] + cols_at[0] + zs[0])
        put(tsend.at[1, pl.ds(xs[d] * 6, 6)], line_in.at[1, d - 1], ts_s.at[1], ts_r.at[1],
            role, rows_at[0] + cols_at[d] + zs[0])

    for q in range(1, 4):
        settle(idx4.at[0], id_r.at[q - 1])
    lane16 = lax.broadcasted_iota(jnp.int32, (16, 128), 1)
    all_ids = jnp.where(
        lane16 < 64,
        jnp.concatenate([idx4[0], idx4[1]], axis=0),
        jnp.concatenate([idx4[2], idx4[3]], axis=0)).astype(BF16)
    idsend[...] = all_ids
    idrecv[shard] = all_ids

    def send_ids(now):
        def body(k, p, h, u):
            @pl.when(h if now else jnp.logical_not(h))
            def _():
                put(idsend, idrecv.at[shard], idg_s, idg_r, role, p)
        each_peer(body)
    pl.semaphore_wait(ready, 3)
    send_ids(True)

    for half in range(2):
        settle(line_in.at[half], ts_r.at[half])
        total = tsend[half, pl.ds((xs[0] if half else ys[0]) * 6, 6)].astype(F32)
        for d in range(3):
            total += line_in[half, d].astype(F32)
        line_sum[half] = total
        line_out[half] = total.astype(line_out.dtype)
        for d, dz in ((2, 0), (2, 1), (1, 1), (3, 1), (1, 0), (3, 0), (0, 1)):
            @pl.when(holds[d])
            def _():
                put(line_out.at[half, spots[d] * 2 + zs[dz]], plane_in.at[half, d * 2 + dz - 1],
                    tp_s.at[half], tp_r.at[half], role,
                    (rows_at[d] + cols_at[0] if half else rows_at[0] + cols_at[d]) + zs[dz])

    @pl.when(role == LEARNER)
    def _():
        fetches[2].wait()
        fetches[3].wait()
        for i in range(8):
            upper, lower = (
                nt(cot[...], wout[j * 1024 + i * 128:j * 1024 + (i + 1) * 128, :])
                .reshape(32, 8, 128)
                for j in range(2)
            )
            gsend[i // 4, :, :, :, :, i % 4 * 128:(i % 4 + 1) * 128] = jnp.concatenate(
                [upper, lower], axis=1).astype(BF16).reshape(4, 4, 2, 16, 128)

    @pl.when(role != LEARNER)
    def _():
        fetches[2].wait()

    @pl.when(holder)
    def _():
        settle(idrecv.at[0:31], idg_r)
        got = idrecv[...].astype(F32)
        got = jnp.concatenate([
            jnp.broadcast_to(got[:, :, 0:1], (32, 16, 128)),
            jnp.broadcast_to(got[:, :, 64:65], (32, 16, 128))], axis=1).reshape(1024, 128)
        lane = lax.broadcasted_iota(jnp.int32, (1024, 128), 1) + 128 * (my_unit & 1)
        chosen = jnp.where(got == lane.astype(F32), 1.0, 0.0).astype(BF16)
        parts = []
        for half in range(2):
            settle(plane_in.at[half], tp_r.at[half])
            total = line_sum[half, spots[0] * 2 + zl]
            for k in range(7):
                total += plane_in[half, k].astype(F32)
            parts.append(total)
        whole = jnp.concatenate(parts, axis=0).astype(BF16)
        selsend[...] = nn(chosen, whole).astype(BF16).reshape(32, 32, 128)

        def send_rows(k, p, h, u):
            put(selsend.at[p], selrecv.at[my_unit], sel_s, sel_r, role, p)
        each_peer(send_rows)
        selrecv[my_unit] = selsend[shard]

    @pl.when(role == LEARNER)
    def _():
        for d in (2, 1, 3):
            put(gsend.at[0, ys[d]], g_line.at[0, d - 1], gs_s.at[0], gs_r.at[0],
                role, rows_at[d] + cols_at[0] + zs[0])
            put(gsend.at[1, :, xs[d]], g_line.at[1, d - 1], gs_s.at[1], gs_r.at[1],
                role, rows_at[0] + cols_at[d] + zs[0])
        for q in range(3):
            put(cot_hbm, cot, cot_s.at[q], cot_r, q, shard)
    send_ids(False)

    @pl.when(holder)
    def _():
        settle(selrecv.at[0:23], sel_r)

    @pl.when(jnp.logical_not(holder))
    def _():
        settle(idrecv.at[0:31], idg_r)
        settle(selrecv, sel_r)

    blocks = [selrecv[2 * c].astype(F32) + selrecv[2 * c + 1].astype(F32) for c in range(12)]
    for q in range(4):
        for i in range(6):
            pair = jnp.concatenate(
                [blocks[i][8 * q:8 * q + 8], blocks[6 + i][8 * q:8 * q + 8]], axis=0)
            xsend[q, :, i * 128:(i + 1) * 128] = pair.astype(BF16)
    for q in range(1, 4):
        to = others[q]
        put(xsend.at[to], xrecv.at[role], x_s.at[q - 1], x_r.at[q - 1], to, shard)
    xrecv[role] = xsend[role]

    @pl.when(role == LEARNER)
    def _():
        for half in range(2):
            settle(g_line.at[half], gs_r.at[half])
            total = (gsend[1, :, x] if half else gsend[0, y]).astype(F32)
            for d in range(3):
                total += g_line[half, d].astype(F32)
            g_sum[half] = total
            g_out[half] = total.astype(BF16)
            for d, dz in ((2, 0), (2, 1), (1, 1), (3, 1), (1, 0), (3, 0), (0, 1)):
                put(g_out.at[half, ys[d] if half else xs[d], zs[dz]],
                    g_plane.at[half, d * 2 + dz - 1], gp_s.at[half], gp_r.at[half], role,
                    (rows_at[d] + cols_at[0] if half else rows_at[0] + cols_at[d]) + zs[dz])

    fetches[4].wait()
    fetches[5].wait()
    for q in range(1, 4):
        settle(xrecv.at[0], x_r.at[q - 1])

    pieces = [xrecv[q].astype(F32) for q in range(4)]

    def tile(c):
        block, i = divmod(c, 12)
        return pieces[block][8 * (i // 6):8 * (i // 6) + 8, (i % 6) * 128:(i % 6 + 1) * 128]

    def stack(tiles):
        return jnp.concatenate(tiles, axis=0)

    q_tiles = [tile(h) for h in range(16)]
    q_all = stack(q_tiles).astype(BF16)
    k_new = stack([tile(16 + h) for h in range(16)]).astype(BF16)
    v_new = stack([tile(32 + h) for h in range(16)]).astype(BF16)

    def head(ref, h):
        return ref[:, h * 128:(h + 1) * 128]

    s1 = stack([nt(q_tiles[h].astype(BF16), head(keys, h)) for h in range(16)]) * scale
    s2 = nt(q_all, k_new) * scale
    ri = lax.broadcasted_iota(jnp.int32, (128, 128), 0)
    ci = lax.broadcasted_iota(jnp.int32, (128, 128), 1)
    allowed = (ri // 8 == ci // 8) & (ci % 8 <= ri % 8) & (ci % 8 < length)
    s2 = jnp.where(allowed, s2, -1e30)
    top = jnp.maximum(jnp.max(s1, axis=1, keepdims=True), jnp.max(s2, axis=1, keepdims=True))
    e1, e2 = jnp.exp(s1 - top), jnp.exp(s2 - top)
    den = jnp.sum(e1, axis=1, keepdims=True) + jnp.sum(e2, axis=1, keepdims=True)
    w1, w2 = e1 / den, e2 / den
    r2 = w2.astype(BF16)
    o2 = nn(r2, v_new)
    out_tiles = [
        nn(w1[8 * h:8 * h + 8].astype(BF16), head(vals, h)) + o2[8 * h:8 * h + 8]
        for h in range(16)
    ]
    for i in range(8):
        hrs[:, i * 128:(i + 1) * 128] = stack([out_tiles[i], out_tiles[8 + i]]).astype(BF16)

    @pl.when(role == LEARNER)
    def _():
        live_out = [jnp.where(live8, t, 0.0) for t in out_tiles]
        for q in range(4):
            for i in range(2):
                hsend[q, :, i * 128:(i + 1) * 128] = stack(
                    [live_out[4 * q + i], live_out[4 * q + 2 + i]]).astype(BF16)
        for q in range(3):
            put(hsend.at[q], hmsg, hrel_s.at[q], hrel_r, q, shard)
        hmsg[...] = hsend[3]

    @pl.when(role != LEARNER)
    def _():
        settle(hmsg, hrel_r)
    def shard_at(py, px, pz):
        return rows_at[py] + cols_at[px] + zs[pz]

    class Gather:
        def __init__(self, msg, buf, send, recv, count):
            self.msg, self.buf, self.send, self.recv, self.count = msg, buf, send, recv, count

        def lanes(self, half):
            width = self.msg.shape[1] // 2
            return pl.ds(half * width, width)

        def hop(self, step, half, src, dst, dy, dx, dz):
            put(src, dst, self.send.at[half], self.recv.at[half, step], role,
                shard_at(dy, dx, dz))

        def arrived(self, half, step, blocks):
            settle(self.count.at[0:blocks], self.recv.at[half, step])

        def start(self, far):
            self.buf[y, x, zl] = self.msg[...]
            for half in range(2):
                n = self.lanes(half)
                spots = [(0, 1), (1, 0), (3, 0), (1, 1), (3, 1)] + far
                for d, dz in spots:
                    self.hop(0, half, self.msg.at[:, n], self.buf.at[y, x, zl, :, n],
                             d * half, d * (1 - half), dz)

        def line(self, half):
            n = self.lanes(half)
            return self.buf.at[:, x, :, :, n] if half else self.buf.at[y, :, :, :, n]

        def sent(self):
            for half in range(2):
                settle(self.count.at[0:31], self.send.at[half])

    class Short(Gather):
        def first(self):
            self.start([(2, 0), (2, 1)])

        def second(self):
            for half in range(2):
                self.arrived(half, 0, 7)
                for d in (2, 1, 3):
                    self.hop(1, half, self.line(half), self.line(half),
                             d * (1 - half), d * half, 0)

        def last(self):
            for half in range(2):
                self.arrived(half, 1, 24)

    class Long(Gather):
        def first(self):
            self.start([])

        def second(self):
            for half in range(2):
                self.arrived(half, 0, 5)
                n = self.lanes(half)
                dy, dx = half, 1 - half
                before = self.buf.at[ys[3 * dy], xs[3 * dx], zl, :, n]
                after = self.buf.at[ys[dy], xs[dx], 1 - zl, :, n]
                self.hop(1, half, before, before, dy, dx, 0)
                self.hop(1, half, after, after, 3 * dy, 3 * dx, 0)

        def third(self):
            for half in range(2):
                self.arrived(half, 1, 2)
                for d in (1, 3):
                    self.hop(2, half, self.line(half), self.line(half),
                             d * (1 - half), d * half, 0)

        def fourth(self):
            for half in range(2):
                self.arrived(half, 2, 16)
                n = self.lanes(half)
                if half:
                    before = self.buf.at[0:2, xs[3], :, :, n]
                    after = self.buf.at[2:4, xs[1], :, :, n]
                else:
                    before = self.buf.at[ys[3], 0:2, :, :, n]
                    after = self.buf.at[ys[1], 2:4, :, :, n]
                self.hop(3, half, before, before, 1 - half, half, 0)
                self.hop(3, half, after, after, 3 * (1 - half), 3 * half, 0)

        def last(self):
            for half in range(2):
                self.arrived(half, 3, 8)

    mixes = Long(hrs, hrrecv, hr_s, hr_r, count_mix)
    heads = Short(hmsg, hgrecv, hg_s, hg_r, idrecv)
    grads_a = Short(rmsg_a, agrecv_a, aga_s, aga_r, idrecv)
    grads_b = Short(rmsg_b, agrecv_b, agb_s, agb_r, count_grad)

    heads.first()

    @pl.when(role != LEARNER)
    def _():
        mixes.first()

    @pl.when(role == LEARNER)
    def _():
        g_tiles = [None] * 16
        for half in range(2):
            settle(g_plane.at[half], gp_r.at[half])
            total = g_sum[half, y if half else x, zl]
            for k in range(7):
                total += g_plane[half, k].astype(F32)
            for i in range(4):
                cols = slice(i * 128, (i + 1) * 128)
                g_tiles[4 * half + i] = jnp.where(live8, total[0:8, cols], 0.0)
                g_tiles[8 + 4 * half + i] = jnp.where(live8, total[8:16, cols], 0.0)
        g_all = stack(g_tiles).astype(BF16)
        gw1 = stack([nt(g_tiles[h].astype(BF16), head(vals, h)) for h in range(16)])
        gw2 = nt(g_all, v_new)
        dots = jnp.sum(w1 * gw1, axis=1, keepdims=True) + jnp.sum(w2 * gw2, axis=1, keepdims=True)
        gs1 = w1 * (gw1 - dots) * scale
        gs2 = (w2 * (gw2 - dots) * scale).astype(BF16)
        gq2 = nn(gs2, k_new)
        gk = tn(gs2, q_all)
        gv = tn(r2, g_all)
        gp = [
            nn(gs1[8 * h:8 * h + 8].astype(BF16), head(keys, h)) + gq2[8 * h:8 * h + 8]
            for h in range(16)
        ]
        gp += [gk[8 * h:8 * h + 8] for h in range(16)]
        gp += [gv[8 * h:8 * h + 8] for h in range(16)]
        for q in range(4):
            for i in range(6):
                pair = stack([gp[12 * q + i], gp[12 * q + 6 + i]]).astype(BF16)
                if i < 2:
                    rsend_a[q, :, i * 128:(i + 1) * 128] = pair
                else:
                    rsend_b[q, :, (i - 2) * 128:(i - 1) * 128] = pair
        for q in range(3):
            put(rsend_a.at[q], rmsg_a, rela_s.at[q], rela_r, q, shard)
        for q in range(3):
            put(rsend_b.at[q], rmsg_b, relb_s.at[q], relb_r, q, shard)
        rmsg_a[...] = rsend_a[3]
        rmsg_b[...] = rsend_b[3]

    copies = []

    def copy_out(a, b):
        pltpu.make_async_copy(a, b, out_sem.at[len(copies)]).start()
        copies.append(a)

    def spread(src, dst, n):
        put(src, dst, e_s.at[1, n], e_r.at[1, n], across, shard)
        put(src, dst, e_s.at[0, n], e_r.at[0, n], sibling, shard)
        copy_out(src, dst)

    def q_cols(of, n):
        at, width = CHUNKS[n]
        return nq_out.at[:, pl.ds(pl.multiple_of(of * 1536 + at, 128), width)]

    def o_rows(of):
        return no_out.at[pl.ds(pl.multiple_of(of * 512, 128), 512), :]

    half = (lax.broadcasted_iota(jnp.int32, (512, 128), 0) // 8) % 2

    def update_out():
        copies.clear()
        fetches[8].wait()
        fetches[9].wait()
        cot_wide = jnp.broadcast_to(
            cot[...].astype(F32).reshape(32, 1, 8, 128), (32, 2, 8, 128)).reshape(512, 128)
        cot_both = jnp.concatenate(
            [jnp.where(half == j, cot_wide, 0.0).astype(BF16) for j in range(2)], axis=1)
        heads.last()
        grad_out = tn(hgrecv[...].reshape(512, 256), cot_both)
        for j in range(2):
            here = slice(j * 256, (j + 1) * 256)
            params = wout[pl.ds(pl.multiple_of(row0 + j * 256, 128), 256), :]
            new, one, two = adamw(
                params, grad_out[:, j * 128:(j + 1) * 128], m_o[here, :], v_o[here, :])
            no[here, :] = new.astype(BF16)
            m_o[here, :] = one
            v_o[here, :] = two
        spread(no, o_rows(role), N_CHUNK)
        copy_out(m_o, mo_out)
        copy_out(v_o, so_out)

    @pl.when(role != LEARNER)
    def _():
        settle(rmsg_a, rela_r)
    grads_a.first()

    @pl.when(role != LEARNER)
    def _():
        settle(rmsg_b, relb_r)
    grads_b.first()
    heads.second()
    grads_a.second()
    grads_b.second()

    @pl.when(role == LEARNER)
    def _():
        mixes.first()

    @pl.when(role != LEARNER)
    def _():
        settle(cot, cot_r)
    mixes.second()
    update_out()

    got_ids = idrecv[...].astype(F32)[:, 8:16, 64:65]
    got_ids = jnp.broadcast_to(
        jnp.concatenate([got_ids, got_ids], axis=1), (32, 16, 128)).reshape(512, 128)
    lane = lax.broadcasted_iota(jnp.int32, (512, 128), 1).astype(F32)
    low = jnp.where(got_ids == lane, 1.0, 0.0).astype(BF16)
    high = jnp.where(got_ids == lane + 128.0, 1.0, 0.0).astype(BF16)
    rows = nn(low, table[0:128, :]) + nn(high, table[128:256, :])
    halves = [jnp.where(half == j, rows, 0.0).T.astype(BF16) for j in range(2)]
    fetches[6].wait()
    fetches[7].wait()
    for n, (at, width) in enumerate(CHUNKS):
        cols = slice(at, at + width)
        if n == 0:
            grads_a.last()
        if n == 2:
            mixes.third()
            grads_b.last()
        buf = agrecv_b if n >= 2 else agrecv_a
        grad = nn(halves[n % 2], buf[...].reshape(512, width))
        new, one, two = adamw(wq[:, cols], grad, m_q[:, cols], v_q[:, cols])
        nq[:, cols] = new.astype(BF16)
        m_q[:, cols] = one
        v_q[:, cols] = two
        spread(nq.at[:, cols], q_cols(role, n), n)
    copy_out(m_q, mq_out)
    copy_out(v_q, sq_out)
    mixes.fourth()

    def part(of, n):
        return q_cols(of, n) if n < N_CHUNK else o_rows(of)

    for n in (N_CHUNK, *range(N_CHUNK)):
        settle(part(across, n), e_r.at[1, n])
        put(part(across, n), part(across, n), e_s.at[2, n], e_r.at[2, n], sibling, shard)

    mixes.last()
    mix = hrrecv[...].reshape(512, 1024)
    upper = nn(mix, wout[0:1024, :]).reshape(32, 2, 8, 128)
    lower = nn(mix, wout[1024:2048, :]).reshape(32, 2, 8, 128)
    dec[...] = (upper[:, 0] + lower[:, 1]).reshape(256, 128).astype(BF16)
    copy_out(dec, dec_out)

    for n in range(N_CHUNK + 1):
        settle(part(sibling, n), e_r.at[0, n])
        settle(part((1 - z_hi) * 2 + (1 - core), n), e_r.at[2, n])
        for way in range(3):
            settle(part(role, n), e_s.at[way, n])
    for i, a in enumerate(copies):
        settle(a, out_sem.at[i])
    for q in range(3):
        settle(idx4.at[0], id_s.at[q])
        settle(xsend.at[0], x_s.at[q])

    @pl.when(holder)
    def _():
        for half in range(2):
            settle(plane_in.at[half, 0:5], tp_s.at[half])
        settle(selsend.at[0:31], sel_s)

    @pl.when(jnp.logical_not(holder))
    def _():
        for half in range(2):
            settle(plane_in.at[half, 0:6], tp_s.at[half])

    @pl.when(role == LEARNER)
    def _():
        for q in range(3):
            settle(cot, cot_s.at[q])
            settle(rmsg_a, rela_s.at[q])
            settle(rmsg_b, relb_s.at[q])
            settle(hmsg, hrel_s.at[q])
        for half in range(2):
            settle(g_line.at[half], gs_s.at[half])
            settle(g_plane.at[half], gp_s.at[half])
    settle(idrecv.at[0:31], idg_s)
    for half in range(2):
        settle(line_in.at[half], ts_s.at[half])
    heads.sent()
    grads_a.sent()
    grads_b.sent()
    mixes.sent()


SHAPES = (
    ((256, 128), BF16), ((128, 6144), BF16), ((2048, 128), BF16),
    ((128, 1536), F32), ((128, 1536), F32), ((512, 128), F32), ((512, 128), F32),
)


def hand_over(*refs):
    ins, outs, stage, sems = refs[:7], refs[7:14], refs[14:21], refs[21]
    moves = []
    for a, v, b in zip(ins, stage, outs):
        pieces = 2 if a.shape == (128, 6144) else 1
        rows = a.shape[0] // pieces
        for i in range(pieces):
            part, n = pl.ds(i * rows, rows), len(moves)
            moves.append((
                pltpu.make_async_copy(a.at[part, :], v.at[part, :], sems.at[0, n]),
                pltpu.make_async_copy(v.at[part, :], b.at[part, :], sems.at[1, n])))
    for m, _ in moves:
        m.start()
    for m, n in moves:
        m.wait()
        n.start()
    for _, n in moves:
        n.wait()


def shards(*args):
    any_ = pl.BlockSpec(memory_space=pl.ANY)
    smem = pl.BlockSpec(memory_space=pltpu.SMEM)
    dma, vm = pltpu.SemaphoreType.DMA, pltpu.VMEM
    done = pl.pallas_call(
        kernel,
        out_shape=tuple(jax.ShapeDtypeStruct(*a) for a in SHAPES),
        in_specs=[smem, smem] + [any_] * 10,
        out_specs=(any_,) * 7,
        scratch_shapes=[
            vm((256, 128), BF16),
            vm((128, 2048), BF16),
            vm((128, 2048), BF16),
            vm((128, 1536), BF16),
            vm((2048, 128), BF16),
            vm((128, 1536), F32),
            vm((128, 1536), F32),
            vm((512, 128), F32),
            vm((512, 128), F32),
            vm((256, 128), BF16),
            vm((2, 24, 64, 128), BF16),
            vm((2, 3, 6, 64, 128), BF16),
            vm((2, 6, 64, 128), F32),
            vm((2, 6, 64, 128), MIDDLE),
            vm((2, 7, 64, 128), MIDDLE),
            vm((2, 4, 4, 2, 16, 512), BF16),
            vm((2, 3, 4, 2, 16, 512), BF16),
            vm((2, 4, 2, 16, 512), F32),
            vm((2, 4, 2, 16, 512), BF16),
            vm((2, 7, 16, 512), BF16),
            vm((4, 8, 128), F32),
            vm((16, 128), BF16),
            vm((32, 16, 128), BF16),
            vm((32, 32, 128), BF16),
            vm((24, 32, 128), BF16),
            vm((4, 16, 768), BF16),
            vm((4, 16, 768), BF16),
            vm((16, 1024), BF16),
            vm((4, 4, 2, 16, 1024), BF16),
            vm((4, 16, 256), BF16),
            vm((16, 256), BF16),
            vm((4, 4, 2, 16, 256), BF16),
            vm((4, 16, 256), BF16),
            vm((4, 16, 512), BF16),
            vm((16, 256), BF16),
            vm((16, 512), BF16),
            vm((4, 4, 2, 16, 256), BF16),
            vm((4, 4, 2, 16, 512), BF16),
            vm((31, 16, 512), BF16),
            vm((31, 16, 256), BF16),
            vm((128, 1536), BF16),
            vm((512, 128), BF16),
            vm((256, 128), BF16),
            pltpu.SemaphoreType.REGULAR,
            dma((10,)),
            dma((N_CHUNK + 6,)),
            dma((3,)), dma((3,)),
            dma, dma,
            dma((2,)), dma((2,)),
            dma((2,)), dma((2,)),
            dma((2,)), dma((2,)),
            dma((2,)), dma((2,)),
            dma((3,)), dma,
            dma, dma,
            dma((3,)), dma((3,)),
            dma((3,)), dma,
            dma((3,)), dma,
            dma((3,)), dma,
            dma((2,)), dma((2, 2)),
            dma((2,)), dma((2, 2)),
            dma((2,)), dma((2, 2)),
            dma((2,)), dma((2, 4)),
            dma((3, N_CHUNK + 1)), dma((3, N_CHUNK + 1)),
        ],
        compiler_params=pltpu.CompilerParams(
            collective_id=0, has_side_effects=True, vmem_limit_bytes=60 * 1024 * 1024),
        name="policy_update",
    )(*args)
    return tuple(pl.pallas_call(
        hand_over,
        out_shape=tuple(jax.ShapeDtypeStruct(*a) for a in SHAPES),
        in_specs=[any_] * 7,
        out_specs=(any_,) * 7,
        scratch_shapes=[vm(*a) for a in SHAPES] + [dma((2, 16))],
        compiler_params=pltpu.CompilerParams(vmem_limit_bytes=60 * 1024 * 1024),
        name="hand_over",
    )(*done))


def solution(mesh):
    both = ("role", "shard")
    return jax.shard_map(
        shards,
        mesh=mesh,
        in_specs=(
            P(both, None), P(both), P(None, "shard"), P(both, None, None), P(both, None, None),
            P("shard", None), P(None, "shard"), P("shard", "role"), P("shard", "role"),
            P("role", "shard"), P("role", "shard"), P("role", "shard"),
        ),
        out_specs=(
            P("role", "shard"), P("shard", None), P(None, "shard"), P("shard", "role"),
            P("shard", "role"), P("role", "shard"), P("role", "shard"),
        ),
        check_vma=False,
    )
```

```python
import jax
import jax.numpy as jnp
from jax import lax
from jax.experimental import pallas as pl
from jax.experimental.pallas import tpu as pltpu
from jax.sharding import PartitionSpec as P

HD = 128
MESH = pl.DeviceIdType.MESH
F32 = jnp.float32
BF16 = jnp.bfloat16
LEARNER = 3

learn_rate = 0.001
first_decay = 0.9
second_decay = 0.95
adam_eps = 1e-08
weight_decay = 0.1
first_fix = 1.0 - 0.9**10
second_fix = 1.0 - 0.95**10
scale = HD ** (-0.5)

N_CHUNK = 4
CHUNKS = ((0, 256), (768, 256), (256, 512), (1024, 512))
MIDDLE = BF16
ORDER = 13


def adamw(params, gradient, first_moment, second_moment):
    moment_one = first_decay * first_moment + (1.0 - first_decay) * gradient
    moment_two = second_decay * second_moment + (1.0 - second_decay) * gradient * gradient
    stepped = moment_one / first_fix / (jnp.sqrt(moment_two / second_fix) + adam_eps)
    wide_params = params.astype(F32)
    updated = wide_params - learn_rate * (stepped + weight_decay * wide_params)
    return (updated, moment_one, moment_two)


def settle(ref, sem):
    pltpu.make_async_copy(ref, ref, sem).wait()


def nt(a, b):
    return lax.dot_general(a, b, (((1,), (1,)), ((), ())), preferred_element_type=F32)


def tn(a, b):
    return lax.dot_general(a, b, (((0,), (0,)), ((), ())), preferred_element_type=F32)


def nn(a, b):
    return jnp.dot(a, b, preferred_element_type=F32)


def kernel(
    ids_ref, len_ref, table_hbm, keys_hbm, vals_hbm, wqkv_hbm, wout_hbm,
    m_q_hbm, v_q_hbm, m_o_hbm, v_o_hbm, cot_hbm,
    dec_out, nq_out, no_out, mq_out, sq_out, mo_out, so_out,
    table, keys, vals, wq, wout, m_q, v_q, m_o, v_o, cot,
    tsend, line_in, line_sum, line_out, plane_in,
    gsend, g_line, g_sum, g_out, g_plane, idx4, idsend, idrecv, selsend, selrecv,
    xsend, xrecv, hrs, hrrecv, hsend, hmsg, hgrecv, rsend_a, rsend_b, rmsg_a, rmsg_b,
    agrecv_a, agrecv_b,
    count_mix, count_grad, nq, no, dec,
    ready, loc, out_sem, id_s, id_r, idg_s, idg_r, ts_s, ts_r, tp_s, tp_r, gs_s, gs_r, gp_s, gp_r,
    cot_s, cot_r, sel_s, sel_r, x_s, x_r, hrel_s, hrel_r, rela_s, rela_r, relb_s, relb_r,
    hg_s, hg_r, aga_s, aga_r, agb_s, agb_r, hr_s, hr_r,
    e_s, e_r,
):
    role = lax.axis_index("role")
    shard = lax.axis_index("shard")
    y, x, zl = shard >> 3, (shard >> 1) & 3, shard & 1
    z_hi, core = role >> 1, role & 1
    sibling = z_hi * 2 + (1 - core)
    across = (1 - z_hi) * 2 + core
    others = [(role + q) & 3 for q in range(4)]

    ys = [(y + d) & 3 for d in range(4)]
    xs = [(x + d) & 3 for d in range(4)]
    zs = [zl, 1 - zl]
    spots = [(x + y + d) & 3 for d in range(4)]
    holds = [spot < 3 for spot in spots]
    rows_at = [v * 8 for v in ys]
    cols_at = [v * 2 for v in xs]
    unit_row = [v * 6 for v in ys]
    unit_col = [v * 2 for v in spots]

    def peer(k):
        dy, dx, dz = k >> 3, (k >> 1) & 3, k & 1
        turn = (dy + dx) & 3
        return (rows_at[dy] + cols_at[dx] + zs[dz], holds[turn],
                unit_row[dy] + unit_col[turn] + zs[dz])

    holder = holds[0]
    my_unit = jnp.where(holder, peer(0)[2], 0)

    def put(src, dst, send, recv, to_role, to_shard):
        pltpu.make_async_remote_copy(
            src_ref=src, dst_ref=dst, send_sem=send, recv_sem=recv,
            device_id=(to_role, to_shard), device_id_type=MESH,
        ).start()

    def each_peer(body, first=1, last=32):
        for j in range(first, last):
            k = j * ORDER % 32
            body(k, *peer(k))

    barrier = pltpu.get_barrier_semaphore()
    for k in (1, 2, 3, 4, 5, 6, 7, 8, 16, 24):
        pl.semaphore_signal(barrier, inc=1, device_id=(role, peer(k)[0]), device_id_type=MESH)
    for q in range(1, 4):
        pl.semaphore_signal(
            barrier, inc=1, device_id=(others[q], shard), device_id_type=MESH)

    col0 = pl.multiple_of(role * 1536, 128)
    row0 = pl.multiple_of(role * 512, 128)
    fetches = [
        pltpu.make_async_copy(a, b, loc.at[i])
        for i, (a, b) in enumerate((
            (table_hbm, table),
            (wqkv_hbm.at[:, pl.ds(col0, 1536)], wq),
            (wout_hbm, wout),
            (cot_hbm, cot),
            (keys_hbm.at[0], keys),
            (vals_hbm.at[0], vals),
            (m_q_hbm, m_q),
            (v_q_hbm, v_q),
            (m_o_hbm, m_o),
            (v_o_hbm, v_o),
        ))
    ]
    for i, f in enumerate(fetches):
        if i != 3:
            f.start()

    @pl.when(role == LEARNER)
    def _():
        fetches[3].start()

    row8 = lax.broadcasted_iota(jnp.int32, (8, 128), 0)
    lane8 = lax.broadcasted_iota(jnp.int32, (8, 128), 1)
    ids = jnp.zeros((8, 128), jnp.int32)
    for i in range(8):
        ids = jnp.where(row8 == i, ids_ref[0, i], ids)
    ids = ids.astype(F32)
    length = len_ref[0]
    live8 = row8 < length
    idx4[role] = ids

    fetches[0].wait()
    fetches[1].wait()
    for c in range(12):
        part = nn(table[...], wq[:, c * 128:(c + 1) * 128]).astype(BF16)
        for h in range(2):
            u = 2 * c + h
            row, spot, pz = u // 6, u % 6 // 2, u % 2
            tsend[0, u] = part[h * 128:h * 128 + 64]
            tsend[1, (spot - row) % 4 * 6 + spot * 2 + pz] = part[h * 128 + 64:h * 128 + 128]

    pl.semaphore_wait(barrier, 13)
    for k in (8, 16, 24):
        pl.semaphore_signal(ready, inc=1, device_id=(role, peer(k)[0]), device_id_type=MESH)

    for q in range(1, 4):
        put(idx4.at[role], idx4.at[role], id_s.at[q - 1], id_r.at[q - 1], others[q], shard)

    for d in (2, 1, 3):
        put(tsend.at[0, pl.ds(ys[d] * 6, 6)], line_in.at[0, d - 1], ts_s.at[0], ts_r.at[0],
            role, rows_at[d] + cols_at[0] + zs[0])
        put(tsend.at[1, pl.ds(xs[d] * 6, 6)], line_in.at[1, d - 1], ts_s.at[1], ts_r.at[1],
            role, rows_at[0] + cols_at[d] + zs[0])

    for q in range(1, 4):
        settle(idx4.at[0], id_r.at[q - 1])
    lane16 = lax.broadcasted_iota(jnp.int32, (16, 128), 1)
    all_ids = jnp.where(
        lane16 < 64,
        jnp.concatenate([idx4[0], idx4[1]], axis=0),
        jnp.concatenate([idx4[2], idx4[3]], axis=0)).astype(BF16)
    idsend[...] = all_ids
    idrecv[shard] = all_ids

    def send_ids(now):
        def body(k, p, h, u):
            @pl.when(h if now else jnp.logical_not(h))
            def _():
                put(idsend, idrecv.at[shard], idg_s, idg_r, role, p)
        each_peer(body)
    pl.semaphore_wait(ready, 3)
    send_ids(True)

    for half in range(2):
        settle(line_in.at[half], ts_r.at[half])
        total = tsend[half, pl.ds((xs[0] if half else ys[0]) * 6, 6)].astype(F32)
        for d in range(3):
            total += line_in[half, d].astype(F32)
        line_sum[half] = total
        line_out[half] = total.astype(line_out.dtype)
        for d, dz in ((2, 0), (2, 1), (1, 1), (3, 1), (1, 0), (3, 0), (0, 1)):
            @pl.when(holds[d])
            def _():
                put(line_out.at[half, spots[d] * 2 + zs[dz]], plane_in.at[half, d * 2 + dz - 1],
                    tp_s.at[half], tp_r.at[half], role,
                    (rows_at[d] + cols_at[0] if half else rows_at[0] + cols_at[d]) + zs[dz])

    @pl.when(role == LEARNER)
    def _():
        fetches[2].wait()
        fetches[3].wait()
        for i in range(8):
            upper, lower = (
                nt(cot[...], wout[j * 1024 + i * 128:j * 1024 + (i + 1) * 128, :])
                .reshape(32, 8, 128)
                for j in range(2)
            )
            gsend[i // 4, :, :, :, :, i % 4 * 128:(i % 4 + 1) * 128] = jnp.concatenate(
                [upper, lower], axis=1).astype(BF16).reshape(4, 4, 2, 16, 128)

    @pl.when(role != LEARNER)
    def _():
        fetches[2].wait()

    @pl.when(holder)
    def _():
        settle(idrecv.at[0:31], idg_r)
        got = idrecv[...].astype(F32)
        got = jnp.concatenate([
            jnp.broadcast_to(got[:, :, 0:1], (32, 16, 128)),
            jnp.broadcast_to(got[:, :, 64:65], (32, 16, 128))], axis=1).reshape(1024, 128)
        lane = lax.broadcasted_iota(jnp.int32, (1024, 128), 1) + 128 * (my_unit & 1)
        chosen = jnp.where(got == lane.astype(F32), 1.0, 0.0).astype(BF16)
        parts = []
        for half in range(2):
            settle(plane_in.at[half], tp_r.at[half])
            total = line_sum[half, spots[0] * 2 + zl]
            for k in range(7):
                total += plane_in[half, k].astype(F32)
            parts.append(total)
        whole = jnp.concatenate(parts, axis=0).astype(BF16)
        selsend[...] = nn(chosen, whole).astype(BF16).reshape(32, 32, 128)

        def send_rows(k, p, h, u):
            put(selsend.at[p], selrecv.at[my_unit], sel_s, sel_r, role, p)
        each_peer(send_rows)
        selrecv[my_unit] = selsend[shard]

    @pl.when(role == LEARNER)
    def _():
        for d in (2, 1, 3):
            put(gsend.at[0, ys[d]], g_line.at[0, d - 1], gs_s.at[0], gs_r.at[0],
                role, rows_at[d] + cols_at[0] + zs[0])
            put(gsend.at[1, :, xs[d]], g_line.at[1, d - 1], gs_s.at[1], gs_r.at[1],
                role, rows_at[0] + cols_at[d] + zs[0])
        for q in range(3):
            put(cot_hbm, cot, cot_s.at[q], cot_r, q, shard)
    send_ids(False)

    @pl.when(holder)
    def _():
        settle(selrecv.at[0:23], sel_r)

    @pl.when(jnp.logical_not(holder))
    def _():
        settle(idrecv.at[0:31], idg_r)
        settle(selrecv, sel_r)

    blocks = [selrecv[2 * c].astype(F32) + selrecv[2 * c + 1].astype(F32) for c in range(12)]
    for q in range(4):
        for i in range(6):
            pair = jnp.concatenate(
                [blocks[i][8 * q:8 * q + 8], blocks[6 + i][8 * q:8 * q + 8]], axis=0)
            xsend[q, :, i * 128:(i + 1) * 128] = pair.astype(BF16)
    for q in range(1, 4):
        to = others[q]
        put(xsend.at[to], xrecv.at[role], x_s.at[q - 1], x_r.at[q - 1], to, shard)
    xrecv[role] = xsend[role]

    @pl.when(role == LEARNER)
    def _():
        for half in range(2):
            settle(g_line.at[half], gs_r.at[half])
            total = (gsend[1, :, x] if half else gsend[0, y]).astype(F32)
            for d in range(3):
                total += g_line[half, d].astype(F32)
            g_sum[half] = total
            g_out[half] = total.astype(BF16)
            for d, dz in ((2, 0), (2, 1), (1, 1), (3, 1), (1, 0), (3, 0), (0, 1)):
                put(g_out.at[half, ys[d] if half else xs[d], zs[dz]],
                    g_plane.at[half, d * 2 + dz - 1], gp_s.at[half], gp_r.at[half], role,
                    (rows_at[d] + cols_at[0] if half else rows_at[0] + cols_at[d]) + zs[dz])

    fetches[4].wait()
    fetches[5].wait()
    for q in range(1, 4):
        settle(xrecv.at[0], x_r.at[q - 1])

    pieces = [xrecv[q].astype(F32) for q in range(4)]

    def tile(c):
        block, i = divmod(c, 12)
        return pieces[block][8 * (i // 6):8 * (i // 6) + 8, (i % 6) * 128:(i % 6 + 1) * 128]

    def stack(tiles):
        return jnp.concatenate(tiles, axis=0)

    q_tiles = [tile(h) for h in range(16)]
    q_all = stack(q_tiles).astype(BF16)
    k_new = stack([tile(16 + h) for h in range(16)]).astype(BF16)
    v_new = stack([tile(32 + h) for h in range(16)]).astype(BF16)

    def head(ref, h):
        return ref[:, h * 128:(h + 1) * 128]

    s1 = stack([nt(q_tiles[h].astype(BF16), head(keys, h)) for h in range(16)]) * scale
    s2 = nt(q_all, k_new) * scale
    ri = lax.broadcasted_iota(jnp.int32, (128, 128), 0)
    ci = lax.broadcasted_iota(jnp.int32, (128, 128), 1)
    allowed = (ri // 8 == ci // 8) & (ci % 8 <= ri % 8) & (ci % 8 < length)
    s2 = jnp.where(allowed, s2, -1e30)
    top = jnp.maximum(jnp.max(s1, axis=1, keepdims=True), jnp.max(s2, axis=1, keepdims=True))
    e1, e2 = jnp.exp(s1 - top), jnp.exp(s2 - top)
    den = jnp.sum(e1, axis=1, keepdims=True) + jnp.sum(e2, axis=1, keepdims=True)
    w1, w2 = e1 / den, e2 / den
    r2 = w2.astype(BF16)
    o2 = nn(r2, v_new)
    out_tiles = [
        nn(w1[8 * h:8 * h + 8].astype(BF16), head(vals, h)) + o2[8 * h:8 * h + 8]
        for h in range(16)
    ]
    for i in range(8):
        hrs[:, i * 128:(i + 1) * 128] = stack([out_tiles[i], out_tiles[8 + i]]).astype(BF16)

    @pl.when(role == LEARNER)
    def _():
        live_out = [jnp.where(live8, t, 0.0) for t in out_tiles]
        for q in range(4):
            for i in range(2):
                hsend[q, :, i * 128:(i + 1) * 128] = stack(
                    [live_out[4 * q + i], live_out[4 * q + 2 + i]]).astype(BF16)
        for q in range(3):
            put(hsend.at[q], hmsg, hrel_s.at[q], hrel_r, q, shard)
        hmsg[...] = hsend[3]

    @pl.when(role != LEARNER)
    def _():
        settle(hmsg, hrel_r)
    def shard_at(py, px, pz):
        return rows_at[py] + cols_at[px] + zs[pz]

    class Gather:
        def __init__(self, msg, buf, send, recv, count):
            self.msg, self.buf, self.send, self.recv, self.count = msg, buf, send, recv, count

        def lanes(self, half):
            width = self.msg.shape[1] // 2
            return pl.ds(half * width, width)

        def hop(self, step, half, src, dst, dy, dx, dz):
            put(src, dst, self.send.at[half], self.recv.at[half, step], role,
                shard_at(dy, dx, dz))

        def arrived(self, half, step, blocks):
            settle(self.count.at[0:blocks], self.recv.at[half, step])

        def start(self, far):
            self.buf[y, x, zl] = self.msg[...]
            for half in range(2):
                n = self.lanes(half)
                spots = [(0, 1), (1, 0), (3, 0), (1, 1), (3, 1)] + far
                for d, dz in spots:
                    self.hop(0, half, self.msg.at[:, n], self.buf.at[y, x, zl, :, n],
                             d * half, d * (1 - half), dz)

        def line(self, half):
            n = self.lanes(half)
            return self.buf.at[:, x, :, :, n] if half else self.buf.at[y, :, :, :, n]

        def sent(self):
            for half in range(2):
                settle(self.count.at[0:31], self.send.at[half])

    class Short(Gather):
        def first(self):
            self.start([(2, 0), (2, 1)])

        def second(self):
            for half in range(2):
                self.arrived(half, 0, 7)
                for d in (2, 1, 3):
                    self.hop(1, half, self.line(half), self.line(half),
                             d * (1 - half), d * half, 0)

        def last(self):
            for half in range(2):
                self.arrived(half, 1, 24)

    class Long(Gather):
        def first(self):
            self.start([])

        def second(self):
            for half in range(2):
                self.arrived(half, 0, 5)
                n = self.lanes(half)
                dy, dx = half, 1 - half
                before = self.buf.at[ys[3 * dy], xs[3 * dx], zl, :, n]
                after = self.buf.at[ys[dy], xs[dx], 1 - zl, :, n]
                self.hop(1, half, before, before, dy, dx, 0)
                self.hop(1, half, after, after, 3 * dy, 3 * dx, 0)

        def third(self):
            for half in range(2):
                self.arrived(half, 1, 2)
                for d in (1, 3):
                    self.hop(2, half, self.line(half), self.line(half),
                             d * (1 - half), d * half, 0)

        def fourth(self):
            for half in range(2):
                self.arrived(half, 2, 16)
                n = self.lanes(half)
                if half:
                    before = self.buf.at[0:2, xs[3], :, :, n]
                    after = self.buf.at[2:4, xs[1], :, :, n]
                else:
                    before = self.buf.at[ys[3], 0:2, :, :, n]
                    after = self.buf.at[ys[1], 2:4, :, :, n]
                self.hop(3, half, before, before, 1 - half, half, 0)
                self.hop(3, half, after, after, 3 * (1 - half), 3 * half, 0)

        def last(self):
            for half in range(2):
                self.arrived(half, 3, 8)

    mixes = Long(hrs, hrrecv, hr_s, hr_r, count_mix)
    heads = Short(hmsg, hgrecv, hg_s, hg_r, idrecv)
    grads_a = Short(rmsg_a, agrecv_a, aga_s, aga_r, idrecv)
    grads_b = Short(rmsg_b, agrecv_b, agb_s, agb_r, count_grad)

    heads.first()

    @pl.when(role != LEARNER)
    def _():
        mixes.first()

    @pl.when(role == LEARNER)
    def _():
        g_tiles = [None] * 16
        for half in range(2):
            settle(g_plane.at[half], gp_r.at[half])
            total = g_sum[half, y if half else x, zl]
            for k in range(7):
                total += g_plane[half, k].astype(F32)
            for i in range(4):
                cols = slice(i * 128, (i + 1) * 128)
                g_tiles[4 * half + i] = jnp.where(live8, total[0:8, cols], 0.0)
                g_tiles[8 + 4 * half + i] = jnp.where(live8, total[8:16, cols], 0.0)
        g_all = stack(g_tiles).astype(BF16)
        gw1 = stack([nt(g_tiles[h].astype(BF16), head(vals, h)) for h in range(16)])
        gw2 = nt(g_all, v_new)
        dots = jnp.sum(w1 * gw1, axis=1, keepdims=True) + jnp.sum(w2 * gw2, axis=1, keepdims=True)
        gs1 = w1 * (gw1 - dots) * scale
        gs2 = (w2 * (gw2 - dots) * scale).astype(BF16)
        gq2 = nn(gs2, k_new)
        gk = tn(gs2, q_all)
        gv = tn(r2, g_all)
        gp = [
            nn(gs1[8 * h:8 * h + 8].astype(BF16), head(keys, h)) + gq2[8 * h:8 * h + 8]
            for h in range(16)
        ]
        gp += [gk[8 * h:8 * h + 8] for h in range(16)]
        gp += [gv[8 * h:8 * h + 8] for h in range(16)]
        for q in range(4):
            for i in range(6):
                pair = stack([gp[12 * q + i], gp[12 * q + 6 + i]]).astype(BF16)
                if i < 2:
                    rsend_a[q, :, i * 128:(i + 1) * 128] = pair
                else:
                    rsend_b[q, :, (i - 2) * 128:(i - 1) * 128] = pair
        for q in range(3):
            put(rsend_a.at[q], rmsg_a, rela_s.at[q], rela_r, q, shard)
        for q in range(3):
            put(rsend_b.at[q], rmsg_b, relb_s.at[q], relb_r, q, shard)
        rmsg_a[...] = rsend_a[3]
        rmsg_b[...] = rsend_b[3]

    copies, near = [], []

    def copy_out(a, b):
        pltpu.make_async_copy(a, b, out_sem.at[len(copies)]).start()
        copies.append(a)

    def spread(src, dst, n):
        put(src, dst, e_s.at[1, n], e_r.at[1, n], across, shard)
        copy_out(src, dst)
        near.append((src, n))

    def q_cols(of, n):
        at, width = CHUNKS[n]
        return nq_out.at[:, pl.ds(pl.multiple_of(of * 1536 + at, 128), width)]

    def o_rows(of):
        return no_out.at[pl.ds(pl.multiple_of(of * 512, 128), 512), :]

    half = (lax.broadcasted_iota(jnp.int32, (512, 128), 0) // 8) % 2

    def update_out():
        copies.clear()
        near.clear()
        fetches[8].wait()
        fetches[9].wait()
        cot_wide = jnp.broadcast_to(
            cot[...].astype(F32).reshape(32, 1, 8, 128), (32, 2, 8, 128)).reshape(512, 128)
        cot_both = jnp.concatenate(
            [jnp.where(half == j, cot_wide, 0.0).astype(BF16) for j in range(2)], axis=1)
        heads.last()
        grad_out = tn(hgrecv[...].reshape(512, 256), cot_both)
        for j in range(2):
            here = slice(j * 256, (j + 1) * 256)
            params = wout[pl.ds(pl.multiple_of(row0 + j * 256, 128), 256), :]
            new, one, two = adamw(
                params, grad_out[:, j * 128:(j + 1) * 128], m_o[here, :], v_o[here, :])
            no[here, :] = new.astype(BF16)
            m_o[here, :] = one
            v_o[here, :] = two
        spread(no, o_rows(role), N_CHUNK)
        copy_out(m_o, mo_out)
        copy_out(v_o, so_out)

    @pl.when(role != LEARNER)
    def _():
        settle(rmsg_a, rela_r)
    grads_a.first()

    @pl.when(role != LEARNER)
    def _():
        settle(rmsg_b, relb_r)
    grads_b.first()
    heads.second()
    grads_a.second()
    grads_b.second()

    @pl.when(role == LEARNER)
    def _():
        mixes.first()

    @pl.when(role != LEARNER)
    def _():
        settle(cot, cot_r)
    mixes.second()
    update_out()

    got_ids = idrecv[...].astype(F32)[:, 8:16, 64:65]
    got_ids = jnp.broadcast_to(
        jnp.concatenate([got_ids, got_ids], axis=1), (32, 16, 128)).reshape(512, 128)
    lane = lax.broadcasted_iota(jnp.int32, (512, 128), 1).astype(F32)
    low = jnp.where(got_ids == lane, 1.0, 0.0).astype(BF16)
    high = jnp.where(got_ids == lane + 128.0, 1.0, 0.0).astype(BF16)
    rows = nn(low, table[0:128, :]) + nn(high, table[128:256, :])
    halves = [jnp.where(half == j, rows, 0.0).T.astype(BF16) for j in range(2)]
    fetches[6].wait()
    fetches[7].wait()
    for n, (at, width) in enumerate(CHUNKS):
        cols = slice(at, at + width)
        if n == 0:
            grads_a.last()
        if n == 2:
            mixes.third()
            grads_b.last()
        buf = agrecv_b if n >= 2 else agrecv_a
        grad = nn(halves[n % 2], buf[...].reshape(512, width))
        new, one, two = adamw(wq[:, cols], grad, m_q[:, cols], v_q[:, cols])
        nq[:, cols] = new.astype(BF16)
        m_q[:, cols] = one
        v_q[:, cols] = two
        spread(nq.at[:, cols], q_cols(role, n), n)
    copy_out(m_q, mq_out)
    copy_out(v_q, sq_out)
    mixes.fourth()

    def part(of, n):
        return q_cols(of, n) if n < N_CHUNK else o_rows(of)

    for src, n in near:
        put(src, part(role, n), e_s.at[0, n], e_r.at[0, n], sibling, shard)

    for n in (N_CHUNK, *range(N_CHUNK)):
        settle(part(across, n), e_r.at[1, n])
        put(part(across, n), part(across, n), e_s.at[2, n], e_r.at[2, n], sibling, shard)

    mixes.last()
    mix = hrrecv[...].reshape(512, 1024)
    upper = nn(mix, wout[0:1024, :]).reshape(32, 2, 8, 128)
    lower = nn(mix, wout[1024:2048, :]).reshape(32, 2, 8, 128)
    dec[...] = (upper[:, 0] + lower[:, 1]).reshape(256, 128).astype(BF16)
    copy_out(dec, dec_out)

    for n in range(N_CHUNK + 1):
        settle(part(sibling, n), e_r.at[0, n])
        settle(part((1 - z_hi) * 2 + (1 - core), n), e_r.at[2, n])
        for way in range(3):
            settle(part(role, n), e_s.at[way, n])
    for i, a in enumerate(copies):
        settle(a, out_sem.at[i])
    for q in range(3):
        settle(idx4.at[0], id_s.at[q])
        settle(xsend.at[0], x_s.at[q])

    @pl.when(holder)
    def _():
        for half in range(2):
            settle(plane_in.at[half, 0:5], tp_s.at[half])
        settle(selsend.at[0:31], sel_s)

    @pl.when(jnp.logical_not(holder))
    def _():
        for half in range(2):
            settle(plane_in.at[half, 0:6], tp_s.at[half])

    @pl.when(role == LEARNER)
    def _():
        for q in range(3):
            settle(cot, cot_s.at[q])
            settle(rmsg_a, rela_s.at[q])
            settle(rmsg_b, relb_s.at[q])
            settle(hmsg, hrel_s.at[q])
        for half in range(2):
            settle(g_line.at[half], gs_s.at[half])
            settle(g_plane.at[half], gp_s.at[half])
    settle(idrecv.at[0:31], idg_s)
    for half in range(2):
        settle(line_in.at[half], ts_s.at[half])
    heads.sent()
    grads_a.sent()
    grads_b.sent()
    mixes.sent()


SHAPES = (
    ((256, 128), BF16), ((128, 6144), BF16), ((2048, 128), BF16),
    ((128, 1536), F32), ((128, 1536), F32), ((512, 128), F32), ((512, 128), F32),
)


def hand_over(*refs):
    ins, outs, stage, sems = refs[:7], refs[7:14], refs[14:21], refs[21]
    moves = []
    for a, v, b in zip(ins, stage, outs):
        pieces = 2 if a.shape == (128, 6144) else 1
        rows = a.shape[0] // pieces
        for i in range(pieces):
            part, n = pl.ds(i * rows, rows), len(moves)
            moves.append((
                pltpu.make_async_copy(a.at[part, :], v.at[part, :], sems.at[0, n]),
                pltpu.make_async_copy(v.at[part, :], b.at[part, :], sems.at[1, n])))
    for m, _ in moves:
        m.start()
    for m, n in moves:
        m.wait()
        n.start()
    for _, n in moves:
        n.wait()


def shards(*args):
    any_ = pl.BlockSpec(memory_space=pl.ANY)
    smem = pl.BlockSpec(memory_space=pltpu.SMEM)
    dma, vm = pltpu.SemaphoreType.DMA, pltpu.VMEM
    done = pl.pallas_call(
        kernel,
        out_shape=tuple(jax.ShapeDtypeStruct(*a) for a in SHAPES),
        in_specs=[smem, smem] + [any_] * 10,
        out_specs=(any_,) * 7,
        scratch_shapes=[
            vm((256, 128), BF16),
            vm((128, 2048), BF16),
            vm((128, 2048), BF16),
            vm((128, 1536), BF16),
            vm((2048, 128), BF16),
            vm((128, 1536), F32),
            vm((128, 1536), F32),
            vm((512, 128), F32),
            vm((512, 128), F32),
            vm((256, 128), BF16),
            vm((2, 24, 64, 128), BF16),
            vm((2, 3, 6, 64, 128), BF16),
            vm((2, 6, 64, 128), F32),
            vm((2, 6, 64, 128), MIDDLE),
            vm((2, 7, 64, 128), MIDDLE),
            vm((2, 4, 4, 2, 16, 512), BF16),
            vm((2, 3, 4, 2, 16, 512), BF16),
            vm((2, 4, 2, 16, 512), F32),
            vm((2, 4, 2, 16, 512), BF16),
            vm((2, 7, 16, 512), BF16),
            vm((4, 8, 128), F32),
            vm((16, 128), BF16),
            vm((32, 16, 128), BF16),
            vm((32, 32, 128), BF16),
            vm((24, 32, 128), BF16),
            vm((4, 16, 768), BF16),
            vm((4, 16, 768), BF16),
            vm((16, 1024), BF16),
            vm((4, 4, 2, 16, 1024), BF16),
            vm((4, 16, 256), BF16),
            vm((16, 256), BF16),
            vm((4, 4, 2, 16, 256), BF16),
            vm((4, 16, 256), BF16),
            vm((4, 16, 512), BF16),
            vm((16, 256), BF16),
            vm((16, 512), BF16),
            vm((4, 4, 2, 16, 256), BF16),
            vm((4, 4, 2, 16, 512), BF16),
            vm((31, 16, 512), BF16),
            vm((31, 16, 256), BF16),
            vm((128, 1536), BF16),
            vm((512, 128), BF16),
            vm((256, 128), BF16),
            pltpu.SemaphoreType.REGULAR,
            dma((10,)),
            dma((N_CHUNK + 6,)),
            dma((3,)), dma((3,)),
            dma, dma,
            dma((2,)), dma((2,)),
            dma((2,)), dma((2,)),
            dma((2,)), dma((2,)),
            dma((2,)), dma((2,)),
            dma((3,)), dma,
            dma, dma,
            dma((3,)), dma((3,)),
            dma((3,)), dma,
            dma((3,)), dma,
            dma((3,)), dma,
            dma((2,)), dma((2, 2)),
            dma((2,)), dma((2, 2)),
            dma((2,)), dma((2, 2)),
            dma((2,)), dma((2, 4)),
            dma((3, N_CHUNK + 1)), dma((3, N_CHUNK + 1)),
        ],
        compiler_params=pltpu.CompilerParams(
            collective_id=0, has_side_effects=True, vmem_limit_bytes=60 * 1024 * 1024),
        name="policy_update",
    )(*args)
    return tuple(pl.pallas_call(
        hand_over,
        out_shape=tuple(jax.ShapeDtypeStruct(*a) for a in SHAPES),
        in_specs=[any_] * 7,
        out_specs=(any_,) * 7,
        scratch_shapes=[vm(*a) for a in SHAPES] + [dma((2, 16))],
        compiler_params=pltpu.CompilerParams(vmem_limit_bytes=60 * 1024 * 1024),
        name="hand_over",
    )(*done))


def solution(mesh):
    both = ("role", "shard")
    return jax.shard_map(
        shards,
        mesh=mesh,
        in_specs=(
            P(both, None), P(both), P(None, "shard"), P(both, None, None), P(both, None, None),
            P("shard", None), P(None, "shard"), P("shard", "role"), P("shard", "role"),
            P("role", "shard"), P("role", "shard"), P("role", "shard"),
        ),
        out_specs=(
            P("role", "shard"), P("shard", None), P(None, "shard"), P("shard", "role"),
            P("shard", "role"), P("role", "shard"), P("role", "shard"),
        ),
        check_vma=False,
    )
```
